32 devices in a mesh: rep: 2 (over core), req: 8 (over z, y), tp: 2 (over x).
Axes of the slice: x: 2, y: 2, z: 4, core: 2. Of those that a mesh axis runs over, the one named last changes fastest.
Arguments:
- hidden: bfloat16 [256, 1536], P(('rep', 'req'), 'tp'), may hold values from -6 to 6
- lengths: int32 [2, 128], P(None, 'req'), may hold values from 16 to 1024, as said below
- migrate: int32 [8], P('req'), may hold values from 0 to 15
- kv_cache: bfloat16 [256, 1024, 8, 128], P(('rep', 'req'), None, 'tp'), may hold values from -250 to 250
- attn_gain: float32 [1536], replicated, may hold values from 0.1 to 1.9
- moe_gain: float32 [1536], replicated, may hold values from 0.1 to 1.9
- w_query: bfloat16 [1536, 1536], P(None, 'tp'), may hold values from -0.15625 to 0.15625
- key_value_weight: bfloat16 [1536, 1024], P(None, 'tp'), may hold values from -0.15625 to 0.15625
- output_weight: bfloat16 [1536, 1536], P('tp'), may hold values from -0.25 to 0.25
- w_gateup: bfloat16 [16, 1536, 2, 512], P(('rep', 'req'), None, None, 'tp'), may hold values from -0.15625 to 0.15625
- w_down: bfloat16 [16, 512, 1536], P(('rep', 'req'), 'tp'), may hold values from -0.25 to 0.25
- expert_ids: int32 [256, 8], P(('rep', 'req')), may hold values from 0 to 15, all different within a row; in each aligned block of 16 rows (0 to 15, 16 to 31, ...) at most 16 rows name the same one
- expert_gates: float32 [256, 8], P(('rep', 'req')), may hold values from 0.1 to 0.4
Outputs:
- layer_out: bfloat16 [256, 1536], P(('rep', 'req'), 'tp')
The draws below stay inside these ranges and needn't reach their ends.
Inputs may be any that keep to these rules, and one draw needn't show every extreme that they name: A request attends to its first lengths positions and to its own new key. `expert_ids`: each row names 8 distinct experts; among the rows of one device (an aligned block of 16 rows) no expert is named more than 16 times, and in some blocks one expert is named exactly 16 times.
All inputs are finite; a program needn't handle non-finite values.
Results may differ from the reference program's by a relative error of at most 0.015.
Values may be sent and summed in bfloat16 or wider, within the bound.
No kernel may reach another device: no remote copies, remote signals or barrier semaphores. Data moves between devices by JAX's collectives and lax.ppermute only.
A program may use at most 128 MiB of HBM per device.

```python
import math
import jax
import jax.numpy as jnp
import numpy as np
from jax import lax

MODEL_DIM = 1536
QUERY_HEADS = 24
KEY_VALUE_HEADS = 8
HEAD_SIZE = 64
EXP_HID = 512
TOPK = 8
RQ_DEV = 16
CONTEXT_SLOTS = 1024
REQUEST_TOTAL = 256
EXPERTS = 16
CAP = 16
N_REP = 2
N_REQ = 8


def draw_lengths(key, part):
    top_bits = CONTEXT_SLOTS.bit_length() - 1
    first_key, second_key = jax.random.split(key)
    complete_shape = (N_REP, REQUEST_TOTAL // N_REP)
    exponent = jax.random.randint(first_key, complete_shape, 4, top_bits + 1)
    floor_len = jnp.left_shift(jnp.ones(complete_shape, jnp.int32), exponent)
    offset = jax.random.randint(second_key, complete_shape, 0, 1 << 30) % floor_len
    drawn = jnp.minimum(floor_len + offset, CONTEXT_SLOTS)
    return drawn.at[0, 0].set(CONTEXT_SLOTS)


def draw_kv_cache(key, part):
    complete_shape = (REQUEST_TOTAL, CONTEXT_SLOTS, KEY_VALUE_HEADS, 2 * HEAD_SIZE)
    is_key = (jnp.arange(2 * HEAD_SIZE) < HEAD_SIZE)[None, None, None, :]
    spread = jnp.where(is_key, 2.0, 1.0)
    return (jnp.clip(jax.random.normal(key, complete_shape, jnp.float32), -4.0, 4.0) * spread).astype(jnp.bfloat16)


def plant(array, key, low, largest):
    spot = [jax.random.randint(jax.random.fold_in(key, axis), (), 0, length) for axis, length in enumerate(array.shape)]
    longest = array.shape.index(max(array.shape))
    next_to = spot[:longest] + [(spot[longest] + 1) % array.shape[longest]] + spot[longest + 1:]
    return array.at[tuple(spot)].set(low).at[tuple(next_to)].set(largest)


def block_levels(rng, shape, cuts, low, largest):
    factor_of, own = 1.0, jax.random.fold_in(rng, 6)
    for dim, parts in cuts:
        steps = jnp.exp(jax.random.uniform(jax.random.fold_in(own, dim), (parts,), jnp.float32, low / len(cuts), largest / len(cuts)))
        factor_of = factor_of * jnp.repeat(steps, shape[dim] // parts).reshape([-1 if axis == dim else 1 for axis in range(len(shape))])
    return factor_of


def assign_block(rng, own, number, rows, count, top, reach, slope):
    order = jax.random.permutation(rng, count)
    heavy_load, ordinary = load_shares(count, rows * top, reach, slope, True), load_shares(count, rows * top, reach, slope, False)
    places = jnp.arange(count)

    def named(tallies, turn):
        used = int((tallies > 0).sum())
        fixed = max(1, used // 4)
        shifted = fixed + (places - fixed + turn * (used - fixed)) % max(1, count - fixed)
        return jnp.zeros((count,), jnp.int32).at[order[jnp.where(places < fixed, places, shifted)]].set(jnp.asarray(tallies, jnp.int32))

    tallies = jnp.where(number % 4 == 0, named(heavy_load, number // 4), named(ordinary, number - number // 4 - 1))
    mixed = jax.random.permutation(jax.random.fold_in(own, 3), count)
    source_of, taker = mixed[0:count // 2 * 2:2], mixed[1:count // 2 * 2:2]
    slack = jnp.minimum(tallies[source_of] - 1, reach - tallies[taker]) // 2
    slack = jnp.where((source_of == order[0]) | (taker == order[0]) | (tallies[taker] == 0), 0, jnp.maximum(slack, 0))
    shifted = jax.random.randint(jax.random.fold_in(own, 4), (count // 2,), 0, 1 << 20) % (slack + 1)
    tallies = tallies.at[source_of].add(-shifted).at[taker].add(shifted)
    items = jnp.searchsorted(jnp.cumsum(tallies), jnp.arange(rows * top), side="right").astype(jnp.int32)
    table = items.reshape(top, rows).T
    table = table[jax.random.permutation(jax.random.fold_in(own, 1), rows)]
    turn = jax.random.randint(jax.random.fold_in(own, 2), (rows, 1), 0, top)
    return jnp.take_along_axis(table, (jnp.arange(top)[None, :] + turn) % top, axis=1)


def load_shares(count, total, bound, skew, full):
    portions = [(1 << 20) // math.isqrt(grade ** skew) + 1 for grade in range(1, count + 1)]
    largest = bound if full else min(bound, max(-(-total // count), total * portions[0] // sum(portions)))
    least = 1 if total - largest >= count - 1 else 0
    holding, spare = [largest] + [least] * (count - 1), total - largest - least * (count - 1)
    while spare > 0:
        candidates = [i for i in range(1, count) if holding[i] < largest] or [i for i in range(1, count) if holding[i] < bound]
        mass, budget = sum([portions[i] for i in candidates]), spare
        for i in candidates:
            extra = min(bound - holding[i], max(1, budget * portions[i] // mass), spare)
            holding[i] = holding[i] + extra
            spare = spare - extra
    return np.array(holding)


def centred(key, dims, scale, reach, cuts=(), kind=jnp.bfloat16):
    level = block_levels(key, dims, cuts, -0.22, 0.18) if cuts else 1.0
    entries = jax.random.normal(key, dims, jnp.float32) * scale * level
    return jnp.minimum(jnp.maximum(entries, -reach), reach).astype(kind)


def setup_inputs(seed: int = 0) -> dict:
    streams_of = jax.random.split(jax.random.key(seed), 14)
    hidden = centred(streams_of[0], (REQUEST_TOTAL, MODEL_DIM), 1.0, 6.0, ((0, 16), (1, 2)))
    lengths = draw_lengths(jax.random.fold_in(streams_of[13], 71), 0)
    migrate = plant(jax.random.randint(streams_of[2], (N_REQ,), 0, RQ_DEV), jax.random.fold_in(streams_of[2], 1), 0, RQ_DEV - 1).astype(jnp.int32)
    kv_cache = draw_kv_cache(jax.random.fold_in(streams_of[13], 71), 0)
    attn_gain = jnp.clip(1.0 + 0.18 * jax.random.normal(streams_of[4], (MODEL_DIM,), jnp.float32), 0.1, 1.9)
    moe_gain = jnp.clip(1.0 + 0.18 * jax.random.normal(streams_of[5], (MODEL_DIM,), jnp.float32), 0.1, 1.9)
    w_query = centred(streams_of[6], (MODEL_DIM, QUERY_HEADS * HEAD_SIZE), MODEL_DIM ** -0.5, 0.15625, ((1, 2),))
    key_value_weight = centred(streams_of[7], (MODEL_DIM, KEY_VALUE_HEADS * 2 * HEAD_SIZE), MODEL_DIM ** -0.5, 0.15625, ((1, 2),))
    output_weight = centred(streams_of[8], (QUERY_HEADS * HEAD_SIZE, MODEL_DIM), (KEY_VALUE_HEADS * HEAD_SIZE) ** -0.5, 0.25, ((0, 2),))
    w_gateup = centred(streams_of[9], (EXPERTS, MODEL_DIM, 2, EXP_HID), MODEL_DIM ** -0.5, 0.15625, ((0, 16), (3, 2)))
    w_down = centred(streams_of[10], (EXPERTS, EXP_HID, MODEL_DIM), EXP_HID ** -0.5, 0.25, ((0, 16), (1, 2)))
    expert_ids_keys = jax.random.split(jax.random.fold_in(streams_of[11], 1), REQUEST_TOTAL // RQ_DEV)
    expert_ids_turns = jax.random.permutation(jax.random.fold_in(streams_of[11], 3), REQUEST_TOTAL // RQ_DEV)
    expert_ids = jax.vmap(lambda own, number: assign_block(jax.random.fold_in(streams_of[11], 2), own, number, RQ_DEV, EXPERTS, TOPK, CAP, 2))(expert_ids_keys, expert_ids_turns).reshape((REQUEST_TOTAL, TOPK))
    expert_gates = jnp.clip(0.1 + 0.3 * jax.random.uniform(streams_of[12], (REQUEST_TOTAL, TOPK), jnp.float32) ** block_levels(streams_of[12], (REQUEST_TOTAL, TOPK), ((0, 16),), -0.2, 0.2), 0.1, 0.4)
    return dict(hidden=hidden, lengths=lengths, migrate=migrate, kv_cache=kv_cache, attn_gain=attn_gain, moe_gain=moe_gain, w_query=w_query, key_value_weight=key_value_weight, output_weight=output_weight, w_gateup=w_gateup, w_down=w_down, expert_ids=expert_ids, expert_gates=expert_gates)


epsilon = 1e-06
rope_base = 10000.0
masked_score = -1e+30

def rms_norm(values, gain):
    mean_square = lax.optimization_barrier(jnp.mean(values * values, axis=-1, keepdims=True))
    return values * lax.rsqrt(mean_square + epsilon) * gain

def apply_rotation(values, position):
    half_width = values.shape[-1] // 2
    inv_freq = rope_base ** (-jnp.arange(half_width, dtype=jnp.float32) * 2.0 / values.shape[-1])
    angles = position.astype(jnp.float32)[:, None, None] * inv_freq
    cosine = jnp.cos(angles)
    sine_part = jnp.sin(angles)
    first_half = values[..., :half_width]
    second_half = values[..., half_width:]
    return jnp.concatenate([first_half * cosine - second_half * sine_part, second_half * cosine + first_half * sine_part], axis=-1)

def reference(hidden, lengths, migrate, kv_cache, attn_gain, moe_gain, w_query, key_value_weight, output_weight, w_gateup, w_down, expert_ids, expert_gates):
    per_replica = N_REQ * RQ_DEV
    row_index = jnp.arange(REQUEST_TOTAL, dtype=jnp.int32)
    replica = row_index // per_replica
    within = row_index % per_replica
    is_moved = within % RQ_DEV == migrate[within // RQ_DEV]
    source = jnp.where(is_moved, (1 - replica) * per_replica + within, row_index).astype(jnp.int32)
    tokens = hidden[source]
    request_extent = lengths.reshape(-1)[source]
    normalized_input = rms_norm(tokens.astype(jnp.float32), attn_gain).astype(jnp.bfloat16)
    query_vectors = jnp.dot(normalized_input, w_query, preferred_element_type=jnp.float32).reshape(REQUEST_TOTAL, QUERY_HEADS, HEAD_SIZE)
    key_value_rows = jnp.dot(normalized_input, key_value_weight, preferred_element_type=jnp.float32).reshape(REQUEST_TOTAL, KEY_VALUE_HEADS, 2 * HEAD_SIZE)
    query_vectors = apply_rotation(query_vectors, request_extent).astype(jnp.bfloat16).reshape(REQUEST_TOTAL, KEY_VALUE_HEADS, QUERY_HEADS // KEY_VALUE_HEADS, HEAD_SIZE)
    key_new = apply_rotation(key_value_rows[..., :HEAD_SIZE], request_extent).astype(jnp.bfloat16)
    value_new = key_value_rows[..., HEAD_SIZE:].astype(jnp.bfloat16)
    score_scale = HEAD_SIZE ** (-0.5)

    def attend(request):
        anchor, query_row, key_row, value_row, span_now = request
        kv_rows = lax.dynamic_index_in_dim(kv_cache, anchor, 0, keepdims=False).astype(jnp.float32)
        cache_keys = kv_rows[..., :HEAD_SIZE]
        cache_values = kv_rows[..., HEAD_SIZE:]
        query_float = query_row.astype(jnp.float32)
        scores = jnp.einsum('hgd,thd->hgt', query_float, cache_keys) * score_scale
        own_score = jnp.einsum('hgd,hd->hg', query_float, key_row.astype(jnp.float32)) * score_scale
        visible = jnp.arange(CONTEXT_SLOTS, dtype=jnp.int32) < span_now
        scores = jnp.where(visible[None, None, :], scores, masked_score)
        row_peak = jnp.maximum(lax.optimization_barrier(jnp.max(scores, axis=-1)), own_score)
        cache_prob = jnp.exp(scores - row_peak[..., None])
        own_prob = jnp.exp(own_score - row_peak)
        denominator = lax.optimization_barrier(jnp.sum(cache_prob, axis=-1)) + own_prob
        cache_weight = lax.optimization_barrier((cache_prob / denominator[..., None]).astype(jnp.bfloat16)).astype(jnp.float32)
        own_weight = lax.optimization_barrier((own_prob / denominator).astype(jnp.bfloat16)).astype(jnp.float32)
        mixture = jnp.einsum('hgt,thd->hgd', cache_weight, cache_values)
        mixture = mixture + own_weight[..., None] * value_row.astype(jnp.float32)[:, None, :]
        return mixture.reshape(QUERY_HEADS * HEAD_SIZE)
    context = lax.map(attend, (source, query_vectors, key_new, value_new, request_extent)).astype(jnp.bfloat16)
    residual = tokens.astype(jnp.float32) + jnp.dot(context, output_weight, preferred_element_type=jnp.float32)
    expert_in = rms_norm(residual, moe_gain).astype(jnp.bfloat16)
    gate_weights = jnp.zeros((REQUEST_TOTAL, EXPERTS), jnp.float32).at[row_index[:, None], expert_ids].add(expert_gates)
    member_count = min(REQUEST_TOTAL, EXPERTS * CAP)

    def expert_step(mixture, expert):
        gate_up, down_rows, gate_column, expert_number = expert
        member = jnp.any(expert_ids == expert_number, axis=1).astype(jnp.int32)
        chosen = jnp.argsort(1 - member, stable=True)[:member_count].astype(jnp.int32)
        projected = jnp.dot(expert_in[chosen], gate_up.reshape(MODEL_DIM, 2 * EXP_HID), preferred_element_type=jnp.float32)
        activation = (jax.nn.silu(projected[:, :EXP_HID]) * projected[:, EXP_HID:]).astype(jnp.bfloat16)
        expert_out = jnp.dot(activation, down_rows, preferred_element_type=jnp.float32)
        return (mixture.at[chosen].add(gate_column[chosen][:, None] * expert_out), None)
    mixture, unused = lax.scan(expert_step, jnp.zeros((REQUEST_TOTAL, MODEL_DIM), jnp.float32), (w_gateup, w_down, gate_weights.T, jnp.arange(EXPERTS, dtype=jnp.int32)))
    return (residual + mixture).astype(jnp.bfloat16)
```

```python
import jax
import jax.numpy as jnp
from jax import lax
from jax.experimental import pallas as pl
from jax.experimental.pallas import tpu as pltpu
from jax.sharding import PartitionSpec as P

HEAD = 64
EPS = 1e-06
ROPE_BASE = 10000.0
MASKED = -1e30
LANES = 128
QROWS = 16
SPAN = 128
UNROLL = 4
MIB = 1 << 20

bf16 = jnp.bfloat16
f32 = jnp.float32


def vmem():
    return pl.BlockSpec(memory_space=pltpu.VMEM)


def smem():
    return pl.BlockSpec(memory_space=pltpu.SMEM)


def hbm():
    return pl.BlockSpec(memory_space=pl.ANY)


def swapped(value, axis):
    return lax.ppermute(value, axis, [(i, i ^ 1) for i in range(lax.axis_size(axis))])


def normed_rows(rows, gain):
    mean_square = jnp.mean(rows * rows, axis=-1, keepdims=True)
    return (rows * lax.rsqrt(mean_square + EPS) * gain).astype(bf16)


def attention_kernel(n_parts, *refs):
    place, lens = refs[0], refs[1]
    parts = refs[2 : 2 + n_parts]
    (cos_ref, sin_ref, gain_ref, wq_hbm, wkv_hbm, wo_hbm, kv_hbm) = refs[2 + n_parts : 9 + n_parts]
    (tok_out, keep_out, send_out) = refs[9 + n_parts : 12 + n_parts]
    (wq, wkv, wo, kvbuf, qf, qb, kvn, scores, macc, lacc, oacc, ctx, items, wsem, ksem) = refs[12 + n_parts :]
    rows = tok_out.shape[0]
    n_query = wq.shape[1] // HEAD
    n_kv = wkv.shape[1] // (2 * HEAD)
    group = n_query // n_kv
    per = kv_hbm.shape[1] // (SPAN * n_kv)
    wide = SPAN * n_kv
    rep, tp = place[0], place[1]

    copies = [
        pltpu.make_async_copy(src, dst, wsem.at[i])
        for i, (src, dst) in enumerate(((wq_hbm, wq), (wkv_hbm, wkv), (wo_hbm, wo)))
    ]
    copies[0].start()
    copies[1].start()

    def kv_copy(item):
        r, c = item // per, item % per
        start = pl.multiple_of(c * wide, wide)
        return pltpu.make_async_copy(
            kv_hbm.at[r, pl.ds(start, wide)], kvbuf.at[r, pl.ds(start, wide)], ksem.at[item]
        )

    def plan_row(r, n):
        def plan_chunk(c, n):
            items[n] = r * per + c
            kv_copy(r * per + c).start()
            return n + 1

        return lax.fori_loop(0, (lens[rep, r] + SPAN - 1) // SPAN, plan_chunk, n)

    total = lax.fori_loop(0, rows, plan_row, 0)
    for u in range(UNROLL):
        items[total + u] = rows * per
    blocks = (total + UNROLL - 1) // UNROLL
    copies[2].start()

    if n_parts == 2:
        tokens = jnp.concatenate(
            [
                jnp.where(tp == 0, parts[0][...], parts[1][...]),
                jnp.where(tp == 0, parts[1][...], parts[0][...]),
            ],
            axis=1,
        )
    else:
        tokens = parts[0][...]
    tok_out[...] = tokens
    normed = normed_rows(tokens.astype(f32), gain_ref[...])

    lane = lax.broadcasted_iota(jnp.int32, (rows, LANES), 1)
    low_half = lane < HEAD
    first = lane % HEAD < HEAD // 2
    cosine, sine = cos_ref[...], sin_ref[...]

    def rotate(v):
        partner = jnp.where(first, pltpu.roll(v, LANES - HEAD // 2, 1), pltpu.roll(v, HEAD // 2, 1))
        return v * cosine + partner * sine

    qf[...] = jnp.zeros_like(qf)
    kvn[...] = jnp.zeros_like(kvn)
    macc[...] = jnp.full_like(macc, MASKED)
    lacc[...] = jnp.zeros_like(lacc)
    oacc[...] = jnp.zeros_like(oacc)
    copies[0].wait()
    queries = jnp.dot(normed, wq[...], preferred_element_type=f32)
    for k in range(n_query // 2):
        turned = rotate(queries[:, k * LANES : (k + 1) * LANES]).astype(bf16).astype(f32)
        turned = turned * HEAD**-0.5
        qf[pl.ds(2 * k, rows, stride=QROWS), :] = jnp.where(low_half, turned, 0.0)
        qf[pl.ds(2 * k + 1, rows, stride=QROWS), :] = jnp.where(low_half, pltpu.roll(turned, HEAD, 1), 0.0)
    copies[1].wait()
    keyval = jnp.dot(normed, wkv[...], preferred_element_type=f32)
    for h in range(n_kv):
        v = keyval[:, h * LANES : (h + 1) * LANES]
        new = jnp.where(low_half, rotate(v), v).astype(bf16).astype(f32)
        for g in range(group):
            kvn[pl.ds(h * group + g, rows, stride=QROWS), :] = new
    qb[...] = qf[...].astype(bf16).reshape(qb.shape)

    row_head = lax.broadcasted_iota(jnp.int32, (QROWS, wide), 0) // group
    column = lax.broadcasted_iota(jnp.int32, (QROWS, wide), 1)
    reach = jnp.where(column % n_kv == row_head, column // n_kv, 1 << 30)

    def folded(op, value):
        out = value[:, :LANES]
        for j in range(1, wide // LANES):
            out = op(out, value[:, j * LANES : (j + 1) * LANES])
        return out

    def chunk(i):
        item = items[i]
        r = item // per
        c = item % per
        kr = jnp.minimum(r, rows - 1)
        return r, c, kvbuf[kr, pl.ds(pl.multiple_of(c * wide, wide), wide), :]

    def score_block(b, carry):
        for u in range(UNROLL):

            @pl.when(b * UNROLL + u < total)
            def _():
                kv_copy(items[b * UNROLL + u]).wait()

        for u in range(UNROLL):
            i = b * UNROLL + u
            r, c, kv = chunk(i)
            s = lax.dot_general(qb[r], kv, (((1,), (1,)), ((), ())), preferred_element_type=f32)
            span = lens[rep, jnp.minimum(r, rows - 1)]
            limit = jnp.where(r < rows, span - c * SPAN, 0)
            s = jnp.where(reach < limit, s, MASKED)
            scores[i] = s
            macc[r] = jnp.maximum(macc[r], folded(jnp.maximum, s))
        return carry

    lax.fori_loop(0, blocks, score_block, 0)

    own = jnp.sum(qf[...] * kvn[...], axis=-1, keepdims=True)
    peak = jnp.maximum(jnp.max(macc[...].reshape(qf.shape), axis=-1, keepdims=True), own)
    own_p = jnp.exp(own - peak)
    macc[...] = jnp.broadcast_to(peak, qf.shape).reshape(macc.shape)

    def value_block(b, carry):
        for u in range(UNROLL):
            i = b * UNROLL + u
            r, c, kv = chunk(i)
            m = macc[r]
            p = jnp.exp(scores[i] - jnp.concatenate([m] * (wide // LANES), axis=1))
            lacc[r] += folded(jnp.add, p)
            oacc[r] += jnp.dot(p.astype(bf16), kv, preferred_element_type=f32)
        return carry

    lax.fori_loop(0, blocks, value_block, 0)

    total_p = jnp.sum(lacc[...].reshape(qf.shape), axis=-1, keepdims=True) + own_p
    qf[...] = (oacc[...].reshape(qf.shape) + own_p * kvn[...]) / total_p
    for k in range(n_query // 2):
        a = qf[pl.ds(2 * k, rows, stride=QROWS), :]
        b = qf[pl.ds(2 * k + 1, rows, stride=QROWS), :]
        ctx[:, k * LANES : (k + 1) * LANES] = jnp.where(low_half, pltpu.roll(a, HEAD, 1), b).astype(bf16)
    copies[2].wait()
    partial = jnp.dot(ctx[...], wo[...], preferred_element_type=f32)
    keep_out[...] = partial
    send_out[...] = partial.astype(bf16)


def attention(place, lens, parts, cosine, sine, gain, wq, wkv, wo, kv):
    rows = parts[0].shape[0]
    width = wq.shape[0]
    n_kv = wkv.shape[1] // (2 * HEAD)
    per = kv.shape[1] // (SPAN * n_kv)
    slots = rows * per + UNROLL
    many = rows + 1
    return pl.pallas_call(
        lambda *refs: attention_kernel(len(parts), *refs),
        out_shape=(
            jax.ShapeDtypeStruct((rows, width), bf16),
            jax.ShapeDtypeStruct((rows, width), f32),
            jax.ShapeDtypeStruct((rows, width), bf16),
        ),
        in_specs=[smem(), smem()] + [vmem()] * (len(parts) + 3) + [hbm()] * 4,
        out_specs=(vmem(), vmem(), vmem()),
        scratch_shapes=[
            pltpu.VMEM(wq.shape, bf16),
            pltpu.VMEM(wkv.shape, bf16),
            pltpu.VMEM(wo.shape, bf16),
            pltpu.VMEM(kv.shape, bf16),
            pltpu.VMEM((many * QROWS, LANES), f32),
            pltpu.VMEM((many, QROWS, LANES), bf16),
            pltpu.VMEM((many * QROWS, LANES), f32),
            pltpu.VMEM((slots, QROWS, SPAN * n_kv), f32),
            pltpu.VMEM((many, QROWS, LANES), f32),
            pltpu.VMEM((many, QROWS, LANES), f32),
            pltpu.VMEM((many, QROWS, LANES), f32),
            pltpu.VMEM((rows, wq.shape[1]), bf16),
            pltpu.SMEM((slots,), jnp.int32),
            pltpu.SemaphoreType.DMA((3,)),
            pltpu.SemaphoreType.DMA((rows * per,)),
        ],
        compiler_params=pltpu.CompilerParams(vmem_limit_bytes=44 * MIB),
        name="attention",
    )(place, lens, *parts, cosine, sine, gain, wq, wkv, wo, kv)


def expert_input_kernel(n_tp, place, moved_slot, tokens, keep, other, gain, ids, gates, payload, residual_out):
    rows, width = tokens.shape
    tp = place[1]
    residual = tokens[...].astype(f32) + keep[...] + other[...].astype(f32)
    part = width // n_tp
    mine = residual[:, :part]
    for t in range(1, n_tp):
        mine = jnp.where(tp == t, residual[:, t * part : (t + 1) * part], mine)
    residual_out[...] = mine
    expert_in = normed_rows(residual, gain[...])
    extra = payload.shape[2] - width
    n_experts = (place[3])
    lane = lax.broadcasted_iota(jnp.int32, (rows, extra), 1)
    table = jnp.zeros((rows, extra), f32)
    low = jnp.zeros((rows, extra), f32)
    for k in range(ids.shape[1]):
        chosen = ids[:, k : k + 1]
        weight = gates[:, k : k + 1]
        top = weight.astype(bf16).astype(f32)
        table = jnp.where(lane == chosen, top, table)
        table = jnp.where(lane == chosen + n_experts, weight - top, table)
    slot = lax.broadcasted_iota(jnp.int32, (rows, extra), 0)
    table = jnp.where((lane == 2 * n_experts) & (slot == moved_slot[0]), 1.0, table)
    table = table.astype(bf16)
    for q in range(payload.shape[0]):
        payload[q, :, :width] = expert_in
        payload[q, :, width:] = table


def expert_input(n_tp, n_req, extra, place, migrate, tokens, keep, other, gain, ids, gates):
    rows, width = tokens.shape
    return pl.pallas_call(
        lambda *refs: expert_input_kernel(n_tp, *refs),
        out_shape=(
            jax.ShapeDtypeStruct((n_req, rows, width + extra), bf16),
            jax.ShapeDtypeStruct((rows, width // n_tp), f32),
        ),
        in_specs=[smem(), smem()] + [vmem()] * 6,
        out_specs=(vmem(), vmem()),
        name="expert_input",
    )(place, migrate, tokens, keep, other, gain, ids, gates)


def expert_rows(rows, gate_up, down):
    projected = jnp.dot(rows, gate_up, preferred_element_type=f32)
    hidden = projected.shape[1] // 2
    gate, up = projected[:, :hidden], projected[:, hidden:]
    active = (gate / (1.0 + jnp.exp(-gate)) * up).astype(bf16)
    return jnp.dot(active, down, preferred_element_type=f32)


def own_expert_kernel(x, gate_up, down, y):
    width = down.shape[1]
    y[...] = expert_rows(x[:, :width], gate_up[...], down[...])


def own_expert(x, gate_up, down):
    return pl.pallas_call(
        own_expert_kernel,
        out_shape=jax.ShapeDtypeStruct((x.shape[0], down.shape[1]), f32),
        in_specs=[vmem()] * 3,
        out_specs=vmem(),
        compiler_params=pltpu.CompilerParams(vmem_limit_bytes=32 * MIB),
        name="own_expert",
    )(x, gate_up, down)


def other_expert_kernel(place, x_own, x_other, y_own, gate_up, down, keep, send):
    width = down.shape[1]
    expert, n_experts = place[2], place[3]
    y_other = expert_rows(x_other[:, :width], gate_up[...], down[...])
    own_table = x_own[:, width:].astype(f32)
    other_table = x_other[:, width:].astype(f32)
    lane = lax.broadcasted_iota(jnp.int32, own_table.shape, 1)

    def picked(table, mask):
        return jnp.sum(jnp.where(mask, table, 0.0), axis=-1, keepdims=True)

    mine = (lane == expert) | (lane == expert + n_experts)
    own_gate, other_gate = picked(own_table, mine), picked(other_table, mine)
    moved = picked(own_table, lane == 2 * n_experts) > 0.5
    from_own = y_own[...] * jnp.where(moved, other_gate, own_gate)
    from_other = y_other * jnp.where(moved, own_gate, other_gate)
    keep[...] = jnp.where(moved, from_other, from_own)
    send[...] = jnp.where(moved, from_own, from_other).astype(bf16)


def other_expert(place, x_own, x_other, y_own, gate_up, down):
    return pl.pallas_call(
        other_expert_kernel,
        out_shape=(
            jax.ShapeDtypeStruct(y_own.shape, f32),
            jax.ShapeDtypeStruct(y_own.shape, bf16),
        ),
        in_specs=[smem()] + [vmem()] * 5,
        out_specs=(vmem(), vmem()),
        compiler_params=pltpu.CompilerParams(vmem_limit_bytes=40 * MIB),
        name="other_expert",
    )(place, x_own, x_other, y_own, gate_up, down)


def pair_sum_kernel(n_tp, keep, recv, out):
    n_req, _, rows, part = out.shape
    total = (keep[...] + recv[...].astype(f32)).astype(bf16)
    for q in range(n_req):
        for t in range(n_tp):
            out[q, t] = total[q * rows : (q + 1) * rows, t * part : (t + 1) * part]


def pair_sum(n_tp, n_req, keep, recv):
    rows, part = keep.shape[0] // n_req, keep.shape[1] // n_tp
    return pl.pallas_call(
        lambda *refs: pair_sum_kernel(n_tp, *refs),
        out_shape=jax.ShapeDtypeStruct((n_req, n_tp, rows, part), bf16),
        in_specs=[vmem()] * 2,
        out_specs=vmem(),
        compiler_params=pltpu.CompilerParams(vmem_limit_bytes=32 * MIB),
        name="pair_sum",
    )(keep, recv)


def final_kernel(moved_slot, pieces, own_residual, other_residual, out):
    total = pieces[0].astype(f32)
    for i in range(1, pieces.shape[0]):
        total = total + pieces[i].astype(f32)
    slot = lax.broadcasted_iota(jnp.int32, total.shape, 0)
    residual = jnp.where(slot == moved_slot[0], other_residual[...], own_residual[...])
    out[...] = (residual + total).astype(bf16)


def final(migrate, pieces, own_residual, other_residual):
    return pl.pallas_call(
        final_kernel,
        out_shape=jax.ShapeDtypeStruct(own_residual.shape, bf16),
        in_specs=[smem()] + [vmem()] * 3,
        out_specs=vmem(),
        name="final",
    )(migrate, pieces, own_residual, other_residual)


def shards(
    hidden,
    lengths,
    migrate,
    kv_cache,
    attn_gain,
    moe_gain,
    w_query,
    key_value_weight,
    output_weight,
    w_gateup,
    w_down,
    expert_ids,
    expert_gates,
):
    rows = hidden.shape[0]
    rep, req, tp = lax.axis_index("rep"), lax.axis_index("req"), lax.axis_index("tp")
    n_rep, n_req, n_tp = lax.axis_size("rep"), lax.axis_size("req"), lax.axis_size("tp")
    n_experts = n_rep * n_req
    place = jnp.stack([rep, tp, rep * n_req + req, jnp.int32(n_experts)]).astype(jnp.int32)

    if n_tp == 2:
        parts = [hidden, swapped(hidden, "tp")]
    else:
        parts = [lax.all_gather(hidden, "tp", axis=1, tiled=True)]

    span = lax.dynamic_index_in_dim(lengths, rep, 0, keepdims=False)
    half = HEAD // 2
    inv_freq = ROPE_BASE ** (-jnp.arange(half, dtype=f32) * 2.0 / HEAD)
    angles = span.astype(f32)[:, None] * inv_freq
    cosine, sine = jnp.cos(angles), jnp.sin(angles)
    cosine = jnp.concatenate([cosine] * 4, axis=1)
    sine = jnp.concatenate([-sine, sine, -sine, sine], axis=1)

    kv_rows = kv_cache.reshape(rows, -1, LANES)
    tokens, keep, send = attention(
        place,
        lengths,
        parts,
        cosine,
        sine,
        attn_gain[None, :],
        w_query,
        key_value_weight,
        output_weight,
        kv_rows,
    )
    if n_tp == 2:
        other = swapped(send, "tp")
    else:
        other = lax.psum(keep.astype(bf16), "tp").astype(f32) - keep
    extra = -(-(2 * n_experts + 1) // LANES) * LANES
    payload, residual = expert_input(
        n_tp, n_req, extra, place, migrate, tokens, keep, other, moe_gain[None, :], expert_ids, expert_gates
    )
    other_residual = swapped(residual, "rep")
    x_own = lax.all_to_all(payload, "req", split_axis=0, concat_axis=0, tiled=True)
    x_own = x_own.reshape(n_req * rows, -1)
    x_other = swapped(x_own, "rep")
    gate_up = w_gateup[0].reshape(w_gateup.shape[1], -1)
    down = w_down[0]
    y_own = own_expert(x_own, gate_up, down)
    mix_keep, mix_send = other_expert(place, x_own, x_other, y_own, gate_up, down)
    mix_recv = swapped(mix_send, "rep")
    pieces = pair_sum(n_tp, n_req, mix_keep, mix_recv)
    pieces = pieces.reshape(n_req * n_tp, rows, -1)
    pieces = lax.all_to_all(pieces, ("req", "tp"), split_axis=0, concat_axis=0, tiled=True)
    return final(migrate, pieces, residual, other_residual)


def solution(mesh):
    placed = (
        P(("rep", "req"), "tp"),
        P(None, "req"),
        P("req"),
        P(("rep", "req"), None, "tp", None),
        P(),
        P(),
        P(None, "tp"),
        P(None, "tp"),
        P("tp", None),
        P(("rep", "req"), None, None, "tp"),
        P(("rep", "req"), "tp", None),
        P(("rep", "req"), None),
        P(("rep", "req"), None),
    )
    return jax.shard_map(
        shards, mesh=mesh, in_specs=placed, out_specs=P(("rep", "req"), "tp"), check_vma=False
    )
```

```python
import jax
import jax.numpy as jnp
from jax import lax
from jax.experimental import pallas as pl
from jax.experimental.pallas import tpu as pltpu
from jax.sharding import PartitionSpec as P

HEAD = 64
EPS = 1e-06
ROPE_BASE = 10000.0
MASKED = -1e30
LANES = 128
QROWS = 16
SPAN = 128
UNROLL = 16
PIECES = 4
MIB = 1 << 20

bf16 = jnp.bfloat16
f32 = jnp.float32


def vmem():
    return pl.BlockSpec(memory_space=pltpu.VMEM)


def smem():
    return pl.BlockSpec(memory_space=pltpu.SMEM)


def hbm():
    return pl.BlockSpec(memory_space=pl.ANY)


def swapped(value, axis):
    return lax.ppermute(value, axis, [(i, i ^ 1) for i in range(lax.axis_size(axis))])


def normed_rows(rows, gain):
    mean_square = jnp.mean(rows * rows, axis=-1, keepdims=True)
    return (rows * lax.rsqrt(mean_square + EPS) * gain).astype(bf16)


def fetch_kernel(wide, per, *refs):
    (lens_hbm, moved_slot, ids_hbm, gates_hbm, gain_hbm, own_hbm, wq_hbm, wkv_hbm) = refs[:8]
    (own, wq, wkv, gain, cos_out, sin_out, table_out, spans, items, count, moved_out) = refs[8:19]
    lens, ids_t, gates_t, sems = refs[19:]
    rows = own.shape[0]
    rep = lax.axis_index("rep")

    pairs = (
        (lens_hbm, lens),
        (ids_hbm, ids_t),
        (gates_hbm, gates_t),
        (own_hbm, own),
        (gain_hbm, gain),
    )
    for src, dst in ((wq_hbm, wq), (wkv_hbm, wkv)):
        part = src.shape[0] // PIECES
        pairs += tuple((src.at[pl.ds(i * part, part)], dst.at[pl.ds(i * part, part)]) for i in range(PIECES))
    copies = [pltpu.make_async_copy(src, dst, sems.at[i]) for i, (src, dst) in enumerate(pairs)]
    for copy in copies:
        copy.start()

    lane = lax.broadcasted_iota(jnp.int32, (rows, LANES), 1)
    slot = lax.broadcasted_iota(jnp.int32, (rows, LANES), 0)
    half = HEAD // 2
    freq = jnp.zeros((1, LANES), f32)
    for i in range(half):
        freq = jnp.where(lane[:1] % half == i, ROPE_BASE ** (-2.0 * i / HEAD), freq)

    for copy in copies[:3]:
        copy.wait()
    span = jnp.zeros((rows, LANES), jnp.int32)
    for r in range(rows):
        span = jnp.where(slot == r, lens[rep, r], span)
        spans[r] = lens[rep, r]
    angle = span.astype(f32) * freq
    sine = jnp.sin(angle)
    cos_out[...] = jnp.cos(angle)
    sin_out[...] = jnp.where(lane % HEAD < half, -sine, sine)

    n_experts = lax.axis_size("rep") * lax.axis_size("req")
    extra = table_out.shape[1]
    lane = lax.broadcasted_iota(jnp.int32, (rows, extra), 1)
    slot = lax.broadcasted_iota(jnp.int32, (rows, extra), 0)
    ids, gates = jnp.transpose(ids_t[...]), jnp.transpose(gates_t[...])
    table = jnp.where((lane == 2 * n_experts) & (slot == moved_slot[0]), 1.0, jnp.zeros((rows, extra), f32))
    for k in range(ids.shape[1]):
        chosen, weight = ids[:, k : k + 1], gates[:, k : k + 1]
        top = weight.astype(bf16).astype(f32)
        table = jnp.where(lane == chosen, top, table)
        table = jnp.where(lane == chosen + n_experts, weight - top, table)
    table_out[...] = table.astype(bf16)

    def plan_row(r, n):
        def plan_chunk(c, n):
            items[n] = r * per + c
            return n + 1

        return lax.fori_loop(0, (spans[r] + SPAN - 1) // SPAN, plan_chunk, n)

    total = lax.fori_loop(0, rows, plan_row, 0)
    for u in range(UNROLL):
        items[total + u] = rows * per
    count[0] = total
    moved_out[0] = moved_slot[0]

    for copy in copies[3:]:
        copy.wait()


def far(*arrays):
    return [pltpu.with_memory_space_constraint(x, pltpu.HBM) for x in arrays]


def close(*arrays):
    return [pltpu.with_memory_space_constraint(x, pltpu.SMEM) for x in arrays]


def near(*arrays):
    return [pltpu.with_memory_space_constraint(x, pltpu.VMEM) for x in arrays]


def fetch(extra, lens, migrate, ids, gates, gain, own, wq, wkv, kv):
    rows = own.shape[0]
    wide = SPAN * (wkv.shape[1] // (2 * HEAD))
    per = kv.shape[1] // wide
    outs = [(own.shape, bf16), (wq.shape, bf16), (wkv.shape, bf16), (gain.shape, f32)]
    outs += [((rows, LANES), f32), ((rows, LANES), f32), ((rows, extra), bf16)]
    scalars = [(rows,), (rows * per + UNROLL,), (1,), (1,)]
    return pl.pallas_call(
        lambda *refs: fetch_kernel(wide, per, *refs),
        out_shape=tuple(pltpu.VMEM(shape, dtype) for shape, dtype in outs)
        + tuple(pltpu.SMEM(shape, jnp.int32) for shape in scalars),
        in_specs=[hbm(), smem()] + [hbm()] * 6,
        out_specs=(vmem(),) * len(outs) + (smem(),) * len(scalars),
        scratch_shapes=[
            pltpu.SMEM(lens.shape, jnp.int32),
            pltpu.VMEM(ids.shape[::-1], jnp.int32),
            pltpu.VMEM(gates.shape[::-1], f32),
            pltpu.SemaphoreType.DMA((5 + 2 * PIECES,)),
        ],
        compiler_params=pltpu.CompilerParams(vmem_limit_bytes=8 * MIB),
        name="fetch",
    )(*far(lens), migrate, *far(ids.T, gates.T, gain, own, wq, wkv))


def attention_kernel(n_parts, *refs):
    spans, items, count = refs[:3]
    refs = refs[3:]
    parts = refs[:n_parts]
    (cos_ref, sin_ref, gain_ref, wq, wkv, wo_hbm, kv_hbm) = refs[n_parts : 7 + n_parts]
    (tok_out, keep_out, send_out) = refs[7 + n_parts : 10 + n_parts]
    (wo, kvbuf, qf, qb, kvn, mixes, sums, peaks, macc, lacc, oacc, ctx, wsem, ksem) = refs[10 + n_parts :]
    rows = tok_out.shape[0]
    n_query = wq.shape[1] // HEAD
    n_kv = wkv.shape[1] // (2 * HEAD)
    group = n_query // n_kv
    wide = SPAN * n_kv
    per = kv_hbm.shape[1] // wide
    tp = lax.axis_index("tp")

    def kv_copy(r):
        size = pl.multiple_of((spans[r] + SPAN - 1) // SPAN * wide, wide)
        return pltpu.make_async_copy(
            kv_hbm.at[r, pl.ds(0, size)], kvbuf.at[r, pl.ds(0, size)], ksem.at[r]
        )

    total = count[0]
    blocks = (total + UNROLL - 1) // UNROLL
    for r in range(rows // 2):
        kv_copy(r).start()
    part = wo.shape[0] // PIECES
    wo_copies = [
        pltpu.make_async_copy(wo_hbm.at[pl.ds(i * part, part)], wo.at[pl.ds(i * part, part)], wsem.at[i])
        for i in range(PIECES)
    ]
    for copy in wo_copies:
        copy.start()

    if n_parts == 2:
        tokens = jnp.concatenate(
            [
                jnp.where(tp == 0, parts[0][...], parts[1][...]),
                jnp.where(tp == 0, parts[1][...], parts[0][...]),
            ],
            axis=1,
        )
    else:
        tokens = parts[0][...]
    tok_out[...] = tokens
    normed = normed_rows(tokens.astype(f32), gain_ref[...].reshape(1, -1))

    lane = lax.broadcasted_iota(jnp.int32, (rows, LANES), 1)
    low_half = lane < HEAD
    first = lane % HEAD < HEAD // 2
    cosine, sine = cos_ref[...], sin_ref[...]

    def rotate(v):
        partner = jnp.where(first, pltpu.roll(v, LANES - HEAD // 2, 1), pltpu.roll(v, HEAD // 2, 1))
        return v * cosine + partner * sine

    qf[...] = jnp.zeros_like(qf)
    kvn[...] = jnp.zeros_like(kvn)
    macc[...] = jnp.full_like(macc, MASKED)
    lacc[...] = jnp.zeros_like(lacc)
    oacc[...] = jnp.zeros_like(oacc)
    queries = jnp.dot(normed, wq[...], preferred_element_type=f32)
    for k in range(n_query // 2):
        turned = rotate(queries[:, k * LANES : (k + 1) * LANES]).astype(bf16).astype(f32)
        turned = turned * HEAD**-0.5
        qf[pl.ds(2 * k, rows, stride=QROWS), :] = jnp.where(low_half, turned, 0.0)
        qf[pl.ds(2 * k + 1, rows, stride=QROWS), :] = jnp.where(low_half, pltpu.roll(turned, HEAD, 1), 0.0)
    for r in range(rows // 2, rows):
        kv_copy(r).start()
    keyval = jnp.dot(normed, wkv[...], preferred_element_type=f32)
    for h in range(n_kv):
        v = keyval[:, h * LANES : (h + 1) * LANES]
        new = jnp.where(low_half, rotate(v), v).astype(bf16).astype(f32)
        for g in range(group):
            kvn[pl.ds(h * group + g, rows, stride=QROWS), :] = new
    qb[...] = qf[...].astype(bf16).reshape(qb.shape)

    query_row = lax.broadcasted_iota(jnp.int32, (QROWS, wide), 0)
    row_head = sum((query_row >= h * group).astype(jnp.int32) for h in range(1, n_kv + 1))
    column = lax.broadcasted_iota(jnp.int32, (QROWS, wide), 1)
    reach = jnp.where(column % n_kv == row_head, column // n_kv, 1 << 30)

    def folded(op, value):
        out = value[:, :LANES]
        for j in range(1, wide // LANES):
            out = op(out, value[:, j * LANES : (j + 1) * LANES])
        return out

    def chunk(i):
        item = items[i]
        r = item // per
        c = item % per
        kr = jnp.minimum(r, rows - 1)
        return r, c, kvbuf[kr, pl.ds(pl.multiple_of(c * wide, wide), wide), :]

    def arrive(r, carry):
        kv_copy(r).wait()
        return carry

    def block(b, ready):
        last = jnp.minimum(items[b * UNROLL + UNROLL - 1] // per, rows - 1) + 1
        lax.fori_loop(ready, last, arrive, 0)
        got = [chunk(b * UNROLL + u) for u in range(UNROLL)]
        dots = [
            lax.dot_general(qb[r], kv, (((1,), (1,)), ((), ())), preferred_element_type=f32) for r, c, kv in got
        ]
        tops, probs = [], []
        for (r, c, kv), s in zip(got, dots):
            span = spans[jnp.minimum(r, rows - 1)]
            limit = jnp.where(r < rows, span - c * SPAN, 0)
            s = jnp.where(reach < limit, s, MASKED)
            top = jnp.max(folded(jnp.maximum, s), axis=-1, keepdims=True)
            tops.append(jnp.broadcast_to(top, (QROWS, LANES)))
            probs.append(jnp.exp(s - top))
        for u, ((r, c, kv), p) in enumerate(zip(got, probs)):
            i = b * UNROLL + u
            mixes[i] = jnp.dot(p.astype(bf16), kv, preferred_element_type=f32)
            sums[i] = folded(jnp.add, p)
            peaks[i] = tops[u]
        for (r, c, kv), top in zip(got, tops):
            macc[r] = jnp.maximum(macc[r], top)
        return last

    lax.fori_loop(0, blocks, block, 0)

    own = jnp.sum(qf[...] * kvn[...], axis=-1, keepdims=True)
    peak = jnp.maximum(macc[...].reshape(qf.shape), own)
    own_p = jnp.exp(own - peak)
    macc[...] = peak.reshape(macc.shape)

    def merge(b, carry):
        for u in range(UNROLL):
            i = b * UNROLL + u
            r = items[i] // per
            weight = jnp.exp(peaks[i] - macc[r])
            lacc[r] += weight * sums[i]
            oacc[r] += weight * mixes[i]
        return carry

    lax.fori_loop(0, blocks, merge, 0)

    total_p = jnp.sum(lacc[...].reshape(qf.shape), axis=-1, keepdims=True) + own_p
    qf[...] = (oacc[...].reshape(qf.shape) + own_p * kvn[...]) / total_p
    for k in range(n_query // 2):
        a = qf[pl.ds(2 * k, rows, stride=QROWS), :]
        b = qf[pl.ds(2 * k + 1, rows, stride=QROWS), :]
        ctx[:, k * LANES : (k + 1) * LANES] = jnp.where(low_half, pltpu.roll(a, HEAD, 1), b).astype(bf16)
    for copy in wo_copies:
        copy.wait()
    partial = jnp.dot(ctx[...], wo[...], preferred_element_type=f32)
    keep_out[...] = partial
    send_out[...] = partial.astype(bf16)


def attention(plan, parts, cosine, sine, gain, wq, wkv, wo, kv):
    rows = parts[0].shape[0]
    width = wq.shape[0]
    n_kv = wkv.shape[1] // (2 * HEAD)
    per = kv.shape[1] // (SPAN * n_kv)
    slots = rows * per + UNROLL
    many = rows + 1
    return pl.pallas_call(
        lambda *refs: attention_kernel(len(parts), *refs),
        out_shape=(
            pltpu.VMEM((rows, width), bf16),
            pltpu.VMEM((rows, width), f32),
            pltpu.VMEM((rows, width), bf16),
        ),
        in_specs=[smem()] * 3 + [vmem()] * (len(parts) + 5) + [hbm()] * 2,
        out_specs=(vmem(), vmem(), vmem()),
        scratch_shapes=[
            pltpu.VMEM(wo.shape, bf16),
            pltpu.VMEM(kv.shape, bf16),
            pltpu.VMEM((many * QROWS, LANES), f32),
            pltpu.VMEM((many, QROWS, LANES), bf16),
            pltpu.VMEM((many * QROWS, LANES), f32),
            pltpu.VMEM((slots, QROWS, LANES), f32),
            pltpu.VMEM((slots, QROWS, LANES), f32),
            pltpu.VMEM((slots, QROWS, LANES), f32),
            pltpu.VMEM((many, QROWS, LANES), f32),
            pltpu.VMEM((many, QROWS, LANES), f32),
            pltpu.VMEM((many, QROWS, LANES), f32),
            pltpu.VMEM((rows, wq.shape[1]), bf16),
            pltpu.SemaphoreType.DMA((PIECES,)),
            pltpu.SemaphoreType.DMA((rows,)),
        ],
        compiler_params=pltpu.CompilerParams(vmem_limit_bytes=36 * MIB),
        name="attention",
    )(*close(*plan), *near(*parts, cosine, sine, gain, wq, wkv), *far(wo, kv))


def expert_input_kernel(n_tp, tokens, keep, other, gain, table, payload, residual_out):
    width = tokens.shape[1]
    tp = lax.axis_index("tp")
    residual = tokens[...].astype(f32) + keep[...] + other[...].astype(f32)
    part = width // n_tp
    mine = residual[:, :part]
    for t in range(1, n_tp):
        mine = jnp.where(tp == t, residual[:, t * part : (t + 1) * part], mine)
    residual_out[...] = mine
    expert_in = normed_rows(residual, gain[...].reshape(1, -1))
    for q in range(payload.shape[0]):
        payload[q, :, :width] = expert_in
        payload[q, :, width:] = table[...]


def expert_input(n_tp, n_req, tokens, keep, other, gain, table):
    rows, width = tokens.shape
    return pl.pallas_call(
        lambda *refs: expert_input_kernel(n_tp, *refs),
        out_shape=(
            pltpu.VMEM((n_req, rows, width + table.shape[1]), bf16),
            pltpu.VMEM((rows, width // n_tp), f32),
        ),
        in_specs=[vmem()] * 5,
        out_specs=(vmem(), vmem()),
        compiler_params=pltpu.CompilerParams(vmem_limit_bytes=8 * MIB),
        name="expert_input",
    )(*near(tokens, keep, other), gain, *near(table))


def expert_rows(rows, gate_up, down):
    projected = jnp.dot(rows, gate_up, preferred_element_type=f32)
    hidden = projected.shape[1] // 2
    gate, up = projected[:, :hidden], projected[:, hidden:]
    active = (gate / (1.0 + jnp.exp(-gate)) * up).astype(bf16)
    return jnp.dot(active, down, preferred_element_type=f32)


def own_expert_kernel(x, gate_up, down, y):
    width = down.shape[1]
    y[...] = expert_rows(x[:, :width], gate_up[...], down[...])


def own_expert(x, gate_up, down):
    return pl.pallas_call(
        own_expert_kernel,
        out_shape=jax.ShapeDtypeStruct((x.shape[0], down.shape[1]), f32),
        in_specs=[vmem()] * 3,
        out_specs=vmem(),
        compiler_params=pltpu.CompilerParams(vmem_limit_bytes=32 * MIB),
        name="own_expert",
    )(x, gate_up, down)


def other_expert_kernel(x_own, x_other, y_own, gate_up, down, keep, send):
    width = down.shape[1]
    n_req = lax.axis_size("req")
    n_experts = lax.axis_size("rep") * n_req
    expert = lax.axis_index("rep") * n_req + lax.axis_index("req")
    y_other = expert_rows(x_other[:, :width], gate_up[...], down[...])
    own_table = x_own[:, width:].astype(f32)
    other_table = x_other[:, width:].astype(f32)
    lane = lax.broadcasted_iota(jnp.int32, own_table.shape, 1)

    def picked(table, mask):
        return jnp.sum(jnp.where(mask, table, 0.0), axis=-1, keepdims=True)

    mine = (lane == expert) | (lane == expert + n_experts)
    own_gate, other_gate = picked(own_table, mine), picked(other_table, mine)
    moved = picked(own_table, lane == 2 * n_experts) > 0.5
    from_own = y_own[...] * jnp.where(moved, other_gate, own_gate)
    from_other = y_other * jnp.where(moved, own_gate, other_gate)
    keep[...] = jnp.where(moved, from_other, from_own)
    send[...] = jnp.where(moved, from_own, from_other).astype(bf16)


def other_expert(x_own, x_other, y_own, gate_up, down):
    return pl.pallas_call(
        other_expert_kernel,
        out_shape=(
            jax.ShapeDtypeStruct(y_own.shape, f32),
            jax.ShapeDtypeStruct(y_own.shape, bf16),
        ),
        in_specs=[vmem()] * 5,
        out_specs=(vmem(), vmem()),
        compiler_params=pltpu.CompilerParams(vmem_limit_bytes=40 * MIB),
        name="other_expert",
    )(x_own, x_other, y_own, gate_up, down)


def pair_sum_kernel(n_tp, keep, recv, out):
    n_req, _, rows, part = out.shape
    total = (keep[...] + recv[...].astype(f32)).astype(bf16)
    for q in range(n_req):
        for t in range(n_tp):
            out[q, t] = total[q * rows : (q + 1) * rows, t * part : (t + 1) * part]


def pair_sum(n_tp, n_req, keep, recv):
    rows, part = keep.shape[0] // n_req, keep.shape[1] // n_tp
    return pl.pallas_call(
        lambda *refs: pair_sum_kernel(n_tp, *refs),
        out_shape=jax.ShapeDtypeStruct((n_req, n_tp, rows, part), bf16),
        in_specs=[vmem()] * 2,
        out_specs=vmem(),
        compiler_params=pltpu.CompilerParams(vmem_limit_bytes=32 * MIB),
        name="pair_sum",
    )(keep, recv)


def final_kernel(moved_slot, pieces, own_residual, other_residual, out):
    total = pieces[0].astype(f32)
    for i in range(1, pieces.shape[0]):
        total = total + pieces[i].astype(f32)
    slot = lax.broadcasted_iota(jnp.int32, total.shape, 0)
    residual = jnp.where(slot == moved_slot[0], other_residual[...], own_residual[...])
    out[...] = (residual + total).astype(bf16)


def final(moved, pieces, own_residual, other_residual):
    return pl.pallas_call(
        final_kernel,
        out_shape=jax.ShapeDtypeStruct(own_residual.shape, bf16),
        in_specs=[smem()] + [vmem()] * 3,
        out_specs=vmem(),
        compiler_params=pltpu.CompilerParams(vmem_limit_bytes=8 * MIB),
        name="final",
    )(*close(moved), pieces, own_residual, other_residual)


def shards(
    hidden,
    lengths,
    migrate,
    kv_cache,
    attn_gain,
    moe_gain,
    w_query,
    key_value_weight,
    output_weight,
    w_gateup,
    w_down,
    expert_ids,
    expert_gates,
):
    rows = hidden.shape[0]
    n_rep, n_req, n_tp = lax.axis_size("rep"), lax.axis_size("req"), lax.axis_size("tp")
    extra = -(-(2 * n_rep * n_req + 1) // LANES) * LANES

    if n_tp == 2:
        other_part = swapped(hidden, "tp")
    else:
        all_parts = lax.all_gather(hidden, "tp", axis=1, tiled=True)
    kv = kv_cache.reshape(rows, -1, LANES)
    own, wq, wkv, gain, cosine, sine, table, *plan, moved = fetch(
        extra,
        lengths,
        migrate,
        expert_ids,
        expert_gates,
        attn_gain,
        hidden,
        w_query,
        key_value_weight,
        kv,
    )
    parts = [own, other_part] if n_tp == 2 else [all_parts]
    tokens, keep, send = attention(plan, parts, cosine, sine, gain, wq, wkv, output_weight, kv)
    if n_tp == 2:
        other = swapped(send, "tp")
    else:
        other = lax.psum(keep.astype(bf16), "tp").astype(f32) - keep
    payload, residual = expert_input(n_tp, n_req, tokens, keep, other, moe_gain, table)
    other_residual = swapped(residual, "rep")
    x_own = lax.all_to_all(payload, "req", split_axis=0, concat_axis=0, tiled=True)
    x_own = x_own.reshape(n_req * rows, -1)
    x_other = swapped(x_own, "rep")
    gate_up = w_gateup[0].reshape(w_gateup.shape[1], -1)
    down = w_down[0]
    y_own = own_expert(x_own, gate_up, down)
    mix_keep, mix_send = other_expert(x_own, x_other, y_own, gate_up, down)
    mix_recv = swapped(mix_send, "rep")
    pieces = pair_sum(n_tp, n_req, mix_keep, mix_recv)
    pieces = pieces.reshape(n_req * n_tp, rows, -1)
    pieces = lax.all_to_all(pieces, ("req", "tp"), split_axis=0, concat_axis=0, tiled=True)
    return final(moved, pieces, residual, other_residual)


def solution(mesh):
    placed = (
        P(("rep", "req"), "tp"),
        P(None, "req"),
        P("req"),
        P(("rep", "req"), None, "tp", None),
        P(),
        P(),
        P(None, "tp"),
        P(None, "tp"),
        P("tp", None),
        P(("rep", "req"), None, None, "tp"),
        P(("rep", "req"), "tp", None),
        P(("rep", "req"), None),
        P(("rep", "req"), None),
    )
    return jax.shard_map(
        shards, mesh=mesh, in_specs=placed, out_specs=P(("rep", "req"), "tp"), check_vma=False
    )
```

```python
import jax
import jax.numpy as jnp
from jax import lax
from jax.experimental import pallas as pl
from jax.experimental.pallas import tpu as pltpu
from jax.sharding import PartitionSpec as P

HEAD = 64
EPS = 1e-06
ROPE_BASE = 10000.0
MASKED = -1e30
LANES = 128
QROWS = 16
SPAN = 128
UNROLL = 16
PIECES = 4
MIB = 1 << 20

bf16 = jnp.bfloat16
f32 = jnp.float32


def vmem():
    return pl.BlockSpec(memory_space=pltpu.VMEM)


def smem():
    return pl.BlockSpec(memory_space=pltpu.SMEM)


def hbm():
    return pl.BlockSpec(memory_space=pl.ANY)


def swapped(value, axis):
    return lax.ppermute(value, axis, [(i, i ^ 1) for i in range(lax.axis_size(axis))])


def normed_rows(rows, gain):
    mean_square = jnp.mean(rows * rows, axis=-1, keepdims=True)
    return (rows * lax.rsqrt(mean_square + EPS) * gain).astype(bf16)


def rest_copy(kv_hbm, kvbuf, sem, spans, wide, r):
    count = (spans[r] + SPAN - 1) // SPAN - 1
    rest = pl.ds(wide, pl.multiple_of(count * wide, wide))
    return count > 0, pltpu.make_async_copy(kv_hbm.at[r, rest], kvbuf.at[r, rest], sem.at[r])


def fetch_kernel(wide, per, *refs):
    (lens_hbm, ids_hbm, gates_hbm, gain_hbm, own_hbm, kv_hbm) = refs[:6]
    (own, gain, cos_out, sin_out, table_out, kvbuf, spans, items, count) = refs[6:15]
    lens, ids_t, gates_t, sems, ksem = refs[15:]
    rows = own.shape[0]
    rep = lax.axis_index("rep")

    pairs = (
        (lens_hbm, lens),
        (ids_hbm, ids_t),
        (gates_hbm, gates_t),
        (own_hbm, own),
        (gain_hbm, gain),
    )
    first = pl.ds(0, wide)
    copies = [pltpu.make_async_copy(src, dst, sems.at[i]) for i, (src, dst) in enumerate(pairs)]
    for copy in copies:
        copy.start()
    head_copies = [pltpu.make_async_copy(kv_hbm.at[r, first], kvbuf.at[r, first], ksem.at[r]) for r in range(rows)]
    for copy in head_copies:
        copy.start()

    lane = lax.broadcasted_iota(jnp.int32, (rows, LANES), 1)
    slot = lax.broadcasted_iota(jnp.int32, (rows, LANES), 0)
    half = HEAD // 2
    freq = jnp.zeros((1, LANES), f32)
    for i in range(half):
        freq = jnp.where(lane[:1] % half == i, ROPE_BASE ** (-2.0 * i / HEAD), freq)

    copies[0].wait()
    for r in range(rows):
        spans[r] = lens[rep, r]

        items[r] = r * per

    def plan_row(r, n):
        def plan_chunk(c, n):
            items[n] = r * per + c
            return n + 1

        return lax.fori_loop(1, (spans[r] + SPAN - 1) // SPAN, plan_chunk, n)

    total = lax.fori_loop(0, rows, plan_row, rows)
    for u in range(UNROLL):
        items[total + u] = rows * per
    count[0] = total

    copies[1].wait()
    copies[2].wait()
    span = jnp.zeros((rows, LANES), jnp.int32)
    for r in range(rows):
        span = jnp.where(slot == r, lens[rep, r], span)
    angle = span.astype(f32) * freq
    sine = jnp.sin(angle)
    cos_out[...] = jnp.cos(angle)
    sin_out[...] = jnp.where(lane % HEAD < half, -sine, sine)

    n_experts = lax.axis_size("rep") * lax.axis_size("req")
    extra = table_out.shape[1]
    lane = lax.broadcasted_iota(jnp.int32, (rows, extra), 1)
    ids, gates = jnp.transpose(ids_t[...]), jnp.transpose(gates_t[...])
    table = jnp.zeros((rows, extra), f32)
    for k in range(ids.shape[1]):
        chosen, weight = ids[:, k : k + 1], gates[:, k : k + 1]
        top = weight.astype(bf16).astype(f32)
        table = jnp.where(lane == chosen, top, table)
        table = jnp.where(lane == chosen + n_experts, weight - top, table)
    table_out[...] = table.astype(bf16)

    for copy in head_copies:
        copy.wait()
    for copy in copies[3:]:
        copy.wait()


def far(*arrays):
    return [pltpu.with_memory_space_constraint(x, pltpu.HBM) for x in arrays]


def close(*arrays):
    return [pltpu.with_memory_space_constraint(x, pltpu.SMEM) for x in arrays]


def near(*arrays):
    return [pltpu.with_memory_space_constraint(x, pltpu.VMEM) for x in arrays]


def fetch(extra, lens, ids, gates, gain, own, wq, wkv, kv):
    rows = own.shape[0]
    wide = SPAN * (wkv.shape[1] // (2 * HEAD))
    per = kv.shape[1] // wide
    outs = [(own.shape, bf16), (gain.shape, f32)]
    outs += [((rows, LANES), f32), ((rows, LANES), f32), ((rows, extra), bf16), (kv.shape, bf16)]
    scalars = [(rows,), (rows * per + UNROLL,), (1,)]
    return pl.pallas_call(
        lambda *refs: fetch_kernel(wide, per, *refs),
        out_shape=tuple(pltpu.VMEM(shape, dtype) for shape, dtype in outs)
        + tuple(pltpu.SMEM(shape, jnp.int32) for shape in scalars),
        in_specs=[hbm()] * 6,
        out_specs=(vmem(),) * len(outs) + (smem(),) * len(scalars),
        scratch_shapes=[
            pltpu.SMEM(lens.shape, jnp.int32),
            pltpu.VMEM(ids.shape[::-1], jnp.int32),
            pltpu.VMEM(gates.shape[::-1], f32),
            pltpu.SemaphoreType.DMA((5,)),
            pltpu.SemaphoreType.DMA((rows,)),
        ],
        compiler_params=pltpu.CompilerParams(vmem_limit_bytes=8 * MIB),
        name="fetch",
    )(*far(lens, ids.T, gates.T, gain, own, kv))


def attention_kernel(n_parts, *refs):
    spans, items, count = refs[:3]
    refs = refs[3:]
    parts = refs[:n_parts]
    (cos_ref, sin_ref, gain_ref, wq, wkv, _, wo_hbm, kv_hbm) = refs[n_parts : 8 + n_parts]
    (tok_out, keep_out, send_out, kvbuf) = refs[8 + n_parts : 12 + n_parts]
    (wo, qf, qb, kvn, mixes, sums, peaks, macc, lacc, oacc, ctx, wsem, ksem) = refs[12 + n_parts :]
    rows = tok_out.shape[0]
    n_query = wq.shape[1] // HEAD
    n_kv = wkv.shape[1] // (2 * HEAD)
    group = n_query // n_kv
    wide = SPAN * n_kv
    per = kv_hbm.shape[1] // wide
    tp = lax.axis_index("tp")

    total = count[0]
    blocks = (total + UNROLL - 1) // UNROLL

    for r in range(rows):
        some, copy = rest_copy(kv_hbm, kvbuf, ksem, spans, wide, r)
        pl.when(some)(copy.start)
    part = wo.shape[0] // PIECES
    wo_copies = [
        pltpu.make_async_copy(wo_hbm.at[pl.ds(i * part, part)], wo.at[pl.ds(i * part, part)], wsem.at[i])
        for i in range(PIECES)
    ]
    for copy in wo_copies:
        copy.start()

    if n_parts == 2:
        tokens = jnp.concatenate(
            [
                jnp.where(tp == 0, parts[0][...], parts[1][...]),
                jnp.where(tp == 0, parts[1][...], parts[0][...]),
            ],
            axis=1,
        )
    else:
        tokens = parts[0][...]
    tok_out[...] = tokens
    normed = normed_rows(tokens.astype(f32), gain_ref[...].reshape(1, -1))

    lane = lax.broadcasted_iota(jnp.int32, (rows, LANES), 1)
    low_half = lane < HEAD
    first = lane % HEAD < HEAD // 2
    cosine, sine = cos_ref[...], sin_ref[...]

    def rotate(v):
        partner = jnp.where(first, pltpu.roll(v, LANES - HEAD // 2, 1), pltpu.roll(v, HEAD // 2, 1))
        return v * cosine + partner * sine

    qf[...] = jnp.zeros_like(qf)
    kvn[...] = jnp.zeros_like(kvn)
    macc[...] = jnp.full_like(macc, MASKED)
    lacc[...] = jnp.zeros_like(lacc)
    oacc[...] = jnp.zeros_like(oacc)
    queries = jnp.dot(normed, wq[...], preferred_element_type=f32)
    for k in range(n_query // 2):
        turned = rotate(queries[:, k * LANES : (k + 1) * LANES]).astype(bf16).astype(f32)
        turned = turned * HEAD**-0.5
        qf[pl.ds(2 * k, rows, stride=QROWS), :] = jnp.where(low_half, turned, 0.0)
        qf[pl.ds(2 * k + 1, rows, stride=QROWS), :] = jnp.where(low_half, pltpu.roll(turned, HEAD, 1), 0.0)
    keyval = jnp.dot(normed, wkv[...], preferred_element_type=f32)
    for h in range(n_kv):
        v = keyval[:, h * LANES : (h + 1) * LANES]
        new = jnp.where(low_half, rotate(v), v).astype(bf16).astype(f32)
        for g in range(group):
            kvn[pl.ds(h * group + g, rows, stride=QROWS), :] = new
    qb[...] = qf[...].astype(bf16).reshape(qb.shape)

    query_row = lax.broadcasted_iota(jnp.int32, (QROWS, wide), 0)
    row_head = sum((query_row >= h * group).astype(jnp.int32) for h in range(1, n_kv + 1))
    column = lax.broadcasted_iota(jnp.int32, (QROWS, wide), 1)
    reach = jnp.where(column % n_kv == row_head, column // n_kv, 1 << 30)

    def folded(op, value):
        out = value[:, :LANES]
        for j in range(1, wide // LANES):
            out = op(out, value[:, j * LANES : (j + 1) * LANES])
        return out

    def chunk(i):
        item = items[i]
        r = item // per
        c = item % per
        kr = jnp.minimum(r, rows - 1)
        return r, c, kvbuf[kr, pl.ds(pl.multiple_of(c * wide, wide), wide), :]

    def arrive(r, carry):
        some, copy = rest_copy(kv_hbm, kvbuf, ksem, spans, wide, r)
        pl.when(some)(copy.wait)
        return carry

    def block(b, ready):
        last = jnp.minimum(items[b * UNROLL + UNROLL - 1] // per, rows - 1) + 1
        last = jnp.where(b * UNROLL + UNROLL <= rows, 0, last)
        lax.fori_loop(ready, last, arrive, 0)
        got = [chunk(b * UNROLL + u) for u in range(UNROLL)]
        dots = [
            lax.dot_general(qb[r], kv, (((1,), (1,)), ((), ())), preferred_element_type=f32) for r, c, kv in got
        ]
        tops, probs = [], []
        for (r, c, kv), s in zip(got, dots):
            span = spans[jnp.minimum(r, rows - 1)]
            limit = jnp.where(r < rows, span - c * SPAN, 0)
            s = jnp.where(reach < limit, s, MASKED)
            top = jnp.max(folded(jnp.maximum, s), axis=-1, keepdims=True)
            tops.append(jnp.broadcast_to(top, (QROWS, LANES)))
            probs.append(jnp.exp(s - top))
        for u, ((r, c, kv), p) in enumerate(zip(got, probs)):
            i = b * UNROLL + u
            mixes[i] = jnp.dot(p.astype(bf16), kv, preferred_element_type=f32)
            sums[i] = folded(jnp.add, p)
            peaks[i] = tops[u]
        for (r, c, kv), top in zip(got, tops):
            macc[r] = jnp.maximum(macc[r], top)
        return jnp.maximum(ready, last)

    ready = lax.fori_loop(0, blocks, block, 0)
    lax.fori_loop(ready, rows, arrive, 0)

    own = jnp.sum(qf[...] * kvn[...], axis=-1, keepdims=True)
    peak = jnp.maximum(macc[...].reshape(qf.shape), own)
    own_p = jnp.exp(own - peak)
    macc[...] = peak.reshape(macc.shape)

    def merge(b, carry):
        for u in range(UNROLL):
            i = b * UNROLL + u
            r = items[i] // per
            weight = jnp.exp(peaks[i] - macc[r])
            lacc[r] += weight * sums[i]
            oacc[r] += weight * mixes[i]
        return carry

    lax.fori_loop(0, blocks, merge, 0)

    total_p = jnp.sum(lacc[...].reshape(qf.shape), axis=-1, keepdims=True) + own_p
    qf[...] = (oacc[...].reshape(qf.shape) + own_p * kvn[...]) / total_p
    for k in range(n_query // 2):
        a = qf[pl.ds(2 * k, rows, stride=QROWS), :]
        b = qf[pl.ds(2 * k + 1, rows, stride=QROWS), :]
        ctx[:, k * LANES : (k + 1) * LANES] = jnp.where(low_half, pltpu.roll(a, HEAD, 1), b).astype(bf16)
    for copy in wo_copies:
        copy.wait()
    partial = jnp.dot(ctx[...], wo[...], preferred_element_type=f32)
    keep_out[...] = partial
    send_out[...] = partial.astype(bf16)


def attention(plan, parts, cosine, sine, gain, wq, wkv, kv_near, wo, kv):
    rows = parts[0].shape[0]
    width = wq.shape[0]
    n_kv = wkv.shape[1] // (2 * HEAD)
    per = kv.shape[1] // (SPAN * n_kv)
    slots = rows * per + UNROLL
    many = rows + 1
    return pl.pallas_call(
        lambda *refs: attention_kernel(len(parts), *refs),
        out_shape=(
            pltpu.VMEM((rows, width), bf16),
            pltpu.VMEM((rows, width), f32),
            pltpu.VMEM((rows, width), bf16),
            pltpu.VMEM(kv.shape, bf16),
        ),
        in_specs=[smem()] * 3 + [vmem()] * (len(parts) + 6) + [hbm()] * 2,
        out_specs=(vmem(), vmem(), vmem(), vmem()),
        input_output_aliases={8 + len(parts): 3},
        scratch_shapes=[
            pltpu.VMEM(wo.shape, bf16),
            pltpu.VMEM((many * QROWS, LANES), f32),
            pltpu.VMEM((many, QROWS, LANES), bf16),
            pltpu.VMEM((many * QROWS, LANES), f32),
            pltpu.VMEM((slots, QROWS, LANES), f32),
            pltpu.VMEM((slots, QROWS, LANES), f32),
            pltpu.VMEM((slots, QROWS, LANES), f32),
            pltpu.VMEM((many, QROWS, LANES), f32),
            pltpu.VMEM((many, QROWS, LANES), f32),
            pltpu.VMEM((many, QROWS, LANES), f32),
            pltpu.VMEM((rows, wq.shape[1]), bf16),
            pltpu.SemaphoreType.DMA((PIECES,)),
            pltpu.SemaphoreType.DMA((rows,)),
        ],
        compiler_params=pltpu.CompilerParams(vmem_limit_bytes=16 * MIB),
        name="attention",
    )(*close(*plan), *near(*parts, cosine, sine, gain, wq, wkv, kv_near), *far(wo, kv))


def expert_input_kernel(n_tp, moved_slot, tokens, keep, other, gain, table, payload, residual_out):
    width = tokens.shape[1]
    tp = lax.axis_index("tp")
    residual = tokens[...].astype(f32) + keep[...] + other[...].astype(f32)
    part = width // n_tp
    mine = residual[:, :part]
    for t in range(1, n_tp):
        mine = jnp.where(tp == t, residual[:, t * part : (t + 1) * part], mine)
    residual_out[...] = mine
    expert_in = normed_rows(residual, gain[...].reshape(1, -1))
    lane = lax.broadcasted_iota(jnp.int32, table.shape, 1)
    slot = lax.broadcasted_iota(jnp.int32, table.shape, 0)
    n_experts = lax.axis_size("rep") * lax.axis_size("req")
    moved = (lane == 2 * n_experts) & (slot == moved_slot[0])
    marked = jnp.where(moved, 1.0, table[...].astype(f32)).astype(bf16)
    for q in range(payload.shape[0]):
        payload[q, :, :width] = expert_in
        payload[q, :, width:] = marked


def stacked_kernel(*refs):
    blocks, whole, tail = refs[:-2], refs[-2], refs[-1]
    rows = blocks[0].shape[0]
    for k, block in enumerate(blocks):
        whole[k * rows : (k + 1) * rows] = block[...]
        if k:
            tail[(k - 1) * rows : k * rows] = block[...]


def stacked(blocks):
    rows, width = blocks[0].shape
    return pl.pallas_call(
        stacked_kernel,
        out_shape=(
            pltpu.VMEM((len(blocks) * rows, width), bf16),
            pltpu.VMEM(((len(blocks) - 1) * rows, width), bf16),
        ),
        in_specs=[vmem()] * len(blocks),
        out_specs=(vmem(), vmem()),
        compiler_params=pltpu.CompilerParams(vmem_limit_bytes=8 * MIB),
        name="stacked",
    )(*near(*blocks))


def joined_kernel(first, second, out):
    rows = first.shape[0]
    out[:rows] = first[...]
    out[rows:] = second[...]


def joined(first, second):
    return pl.pallas_call(
        joined_kernel,
        out_shape=pltpu.VMEM((first.shape[0] + second.shape[0], first.shape[1]), bf16),
        in_specs=[vmem()] * 2,
        out_specs=vmem(),
        compiler_params=pltpu.CompilerParams(vmem_limit_bytes=8 * MIB),
        name="joined",
    )(*near(first, second))


def expert_input(n_tp, n_req, moved, tokens, keep, other, gain, table):
    rows, width = tokens.shape
    return pl.pallas_call(
        lambda *refs: expert_input_kernel(n_tp, *refs),
        out_shape=(
            pltpu.VMEM((n_req, rows, width + table.shape[1]), bf16),
            pltpu.VMEM((rows, width // n_tp), f32),
        ),
        in_specs=[smem()] + [vmem()] * 5,
        out_specs=(vmem(), vmem()),
        compiler_params=pltpu.CompilerParams(vmem_limit_bytes=8 * MIB),
        name="expert_input",
    )(moved, *near(tokens, keep, other), gain, *near(table))


def expert_rows(rows, gate_up, down):
    projected = jnp.dot(rows, gate_up, preferred_element_type=f32)
    hidden = projected.shape[1] // 2
    gate, up = projected[:, :hidden], projected[:, hidden:]
    active = (gate / (1.0 + jnp.exp(-gate)) * up).astype(bf16)
    return jnp.dot(active, down, preferred_element_type=f32)


def own_expert_kernel(x, gate_up, down, y):
    width = down.shape[1]
    y[...] = expert_rows(x[:, :width], gate_up[...], down[...])


def own_expert(x, gate_up, down):
    return pl.pallas_call(
        own_expert_kernel,
        out_shape=pltpu.VMEM((x.shape[0], down.shape[1]), f32),
        in_specs=[vmem()] * 3,
        out_specs=vmem(),
        compiler_params=pltpu.CompilerParams(vmem_limit_bytes=32 * MIB),
        cost_estimate=expert_cost(x.shape[0], gate_up, down),
        name="own_expert",
    )(*near(x), gate_up, down)


def expert_cost(count, gate_up, down):
    return pl.CostEstimate(
        flops=2 * count * (gate_up.size + down.size),
        bytes_accessed=2 * (gate_up.size + down.size) + 10 * count * down.shape[1],
        transcendentals=count * down.shape[0],
    )


def traded(width, x_own, x_other, from_own, from_other, keep, send):
    n_req = lax.axis_size("req")
    n_experts = lax.axis_size("rep") * n_req
    expert = lax.axis_index("rep") * n_req + lax.axis_index("req")
    own_table = x_own[:, width:].astype(f32)
    other_table = x_other[:, width:].astype(f32)
    lane = lax.broadcasted_iota(jnp.int32, own_table.shape, 1)

    def picked(table, mask):
        return jnp.sum(jnp.where(mask, table, 0.0), axis=-1, keepdims=True)

    gated = (lane == expert) | (lane == expert + n_experts)
    own_gate, other_gate = picked(own_table, gated), picked(other_table, gated)
    moved = picked(own_table, lane == 2 * n_experts) > 0.5
    from_own = from_own(jnp.where(moved, other_gate, own_gate))
    from_other = from_other() * jnp.where(moved, own_gate, other_gate)
    keep[...] = jnp.where(moved, from_other, from_own)
    send[...] = jnp.where(moved, from_own, from_other).astype(bf16)


def home_expert_kernel(n_tp, place, x_own, x_other, residual, gate_up, down, keep, send, mine):
    width = down.shape[1]
    count = x_own.shape[0]
    both = jnp.concatenate([x_own[:, :width], x_other[:, :width]], axis=0)
    y = expert_rows(both, gate_up[...], down[...])
    rows, part = residual.shape
    tp = lax.axis_index("tp")
    here = pl.ds(place() * rows, rows)

    def from_own(gate):
        mine[...] = y[:count] * gate
        for t in range(n_tp):

            @pl.when(tp == t)
            def _():
                mine[here, t * part : (t + 1) * part] += residual[...]

        return mine[...]

    traded(width, x_own, x_other, from_own, lambda: y[count:], keep, send)


def home_expert(n_tp, place, x_own, x_other, residual, gate_up, down):
    shape = (x_own.shape[0], down.shape[1])
    return pl.pallas_call(
        lambda *refs: home_expert_kernel(n_tp, place, *refs),
        out_shape=(pltpu.VMEM(shape, f32), pltpu.VMEM(shape, bf16)),
        in_specs=[vmem()] * 5,
        out_specs=(vmem(), vmem()),
        scratch_shapes=[pltpu.VMEM(shape, f32)],
        compiler_params=pltpu.CompilerParams(vmem_limit_bytes=40 * MIB if shape[0] > 256 else 16 * MIB),
        cost_estimate=expert_cost(2 * shape[0], gate_up, down),
        name="home_expert",
    )(*near(x_own, x_other, residual), gate_up, down)


def other_expert_kernel(x_own, x_other, y_own, gate_up, down, keep, send):
    width = down.shape[1]

    def from_other():
        return expert_rows(x_other[:, :width], gate_up[...], down[...])

    traded(width, x_own, x_other, lambda gate: y_own[...] * gate, from_other, keep, send)


def other_expert(x_own, x_other, y_own, gate_up, down):
    return pl.pallas_call(
        other_expert_kernel,
        out_shape=(pltpu.VMEM(y_own.shape, f32), pltpu.VMEM(y_own.shape, bf16)),
        in_specs=[vmem()] * 5,
        out_specs=(vmem(), vmem()),
        compiler_params=pltpu.CompilerParams(vmem_limit_bytes=16 * MIB),
        cost_estimate=expert_cost(y_own.shape[0], gate_up, down),
        name="other_expert",
    )(*near(x_own, x_other, y_own), gate_up, down)


def pair_sum_kernel(n_tp, spots, *refs):
    out = refs[-1]
    _, _, rows, part = out.shape
    for i, spot in enumerate(spots):
        keep, recv = refs[2 * i], refs[2 * i + 1]
        total = (keep[...] + recv[...].astype(f32)).astype(bf16)
        for q in range(total.shape[0] // rows):
            for t in range(n_tp):
                out[spot(q), t] = total[q * rows : (q + 1) * rows, t * part : (t + 1) * part]


def pair_sum(n_tp, n_req, rows, spots, *sums):
    part = sums[0].shape[1] // n_tp
    return pl.pallas_call(
        lambda *refs: pair_sum_kernel(n_tp, spots, *refs),
        out_shape=pltpu.VMEM((n_req, n_tp, rows, part), bf16),
        in_specs=[vmem()] * len(sums),
        out_specs=vmem(),
        compiler_params=pltpu.CompilerParams(vmem_limit_bytes=16 * MIB),
        name="pair_sum",
    )(*near(*sums))


def halves_kernel(keep, recv, mine, cross):
    total = keep[...] + recv[...].astype(f32)
    part = mine.shape[1]
    low, high = total[:, :part], total[:, part:]
    first = lax.axis_index("tp") == 0
    mine[...] = jnp.where(first, low, high).astype(mine.dtype)
    cross[...] = jnp.where(first, high, low).astype(bf16)


def halves(keep, recv, kind):
    shape = (keep.shape[0], keep.shape[1] // 2)
    return pl.pallas_call(
        halves_kernel,
        out_shape=(pltpu.VMEM(shape, kind), pltpu.VMEM(shape, bf16)),
        in_specs=[vmem()] * 2,
        out_specs=(vmem(), vmem()),
        compiler_params=pltpu.CompilerParams(vmem_limit_bytes=8 * MIB),
        name="halves",
    )(*near(keep, recv))


def square_sum_kernel(mine, *refs):
    arrived, outs = refs[:3], refs[3:]
    total = mine[...]
    for piece in arrived:
        total = total + piece[...].astype(f32)
    rows = outs[0].shape[0]
    for k, out in enumerate(outs):
        out[...] = total[k * rows : (k + 1) * rows].astype(out.dtype)


def square_sum(rows, mine, *arrived):
    shape = (rows, mine.shape[1])
    count = mine.shape[0] // rows
    return pl.pallas_call(
        square_sum_kernel,
        out_shape=(pltpu.VMEM(shape, f32),) + (pltpu.VMEM(shape, bf16),) * (count - 1),
        in_specs=[vmem()] * 4,
        out_specs=(vmem(),) * count,
        compiler_params=pltpu.CompilerParams(vmem_limit_bytes=8 * MIB),
        name="square_sum",
    )(*near(mine, *arrived))


def line_sum_kernel(*refs):
    total = refs[0][...]
    for piece in refs[1:-1]:
        total = total + piece[...].astype(f32)
    refs[-1][...] = total.astype(bf16)


def line_sum(mine, *arrived):
    return pl.pallas_call(
        line_sum_kernel,
        out_shape=jax.ShapeDtypeStruct(mine.shape, bf16),
        in_specs=[vmem()] * (1 + len(arrived)),
        out_specs=vmem(),
        compiler_params=pltpu.CompilerParams(vmem_limit_bytes=8 * MIB),
        name="line_sum",
    )(*near(mine, *arrived))


def final_kernel(pieces, out):
    total = pieces[0].astype(f32)
    for i in range(1, pieces.shape[0]):
        total = total + pieces[i].astype(f32)
    out[...] = total.astype(bf16)


def final(pieces):
    return pl.pallas_call(
        final_kernel,
        out_shape=jax.ShapeDtypeStruct(pieces.shape[1:], bf16),
        in_specs=[vmem()],
        out_specs=vmem(),
        compiler_params=pltpu.CompilerParams(vmem_limit_bytes=8 * MIB),
        name="final",
    )(*near(pieces))


def shards(
    hidden,
    lengths,
    migrate,
    kv_cache,
    attn_gain,
    moe_gain,
    w_query,
    key_value_weight,
    output_weight,
    w_gateup,
    w_down,
    expert_ids,
    expert_gates,
):
    rows = hidden.shape[0]
    n_rep, n_req, n_tp = lax.axis_size("rep"), lax.axis_size("req"), lax.axis_size("tp")
    extra = -(-(2 * n_rep * n_req + 1) // LANES) * LANES

    if n_tp == 2:
        other_part = swapped(hidden, "tp")
    else:
        all_parts = lax.all_gather(hidden, "tp", axis=1, tiled=True)
    kv = kv_cache.reshape(rows, -1, LANES)
    own, gain, cosine, sine, table, kv_near, *plan = fetch(
        extra,
        lengths,
        expert_ids,
        expert_gates,
        attn_gain,
        hidden,
        w_query,
        key_value_weight,
        kv,
    )
    parts = [own, other_part] if n_tp == 2 else [all_parts]
    tokens, keep, send, _ = attention(
        plan, parts, cosine, sine, gain, w_query, key_value_weight, kv_near, output_weight, kv
    )
    gate_up = w_gateup[0].reshape(w_gateup.shape[1], -1)
    down = w_down[0]
    if n_tp == 2:
        other = swapped(send, "tp")
        gate_up, other = lax.optimization_barrier((gate_up, other))
    else:
        other = lax.psum(keep.astype(bf16), "tp").astype(f32) - keep
    by_permute = n_req == 8 and n_tp == 2
    payload, residual = expert_input(n_tp, 1 if by_permute else n_req, migrate, tokens, keep, other, moe_gain, table)
    if by_permute:
        payload = payload[0]
        steps = [[(q, q ^ 2 * k) for q in range(n_req)] for k in (1, 2, 3)]
        beside = [lax.ppermute(payload, "req", step) for step in steps]
        across = swapped(payload, "req")
        home, tail = stacked([payload] + beside)
        away = joined(across, swapped(tail, "req"))
        home_other = swapped(home, "rep")
        home_keep, home_send = home_expert(
            n_tp, lambda: 0, home, home_other, residual, gate_up, down
        )
        home_recv = swapped(home_send, "rep")
        away_other = swapped(away, "rep")
        away_own = own_expert(away, gate_up, down)
        away_keep, away_send = other_expert(away, away_other, away_own, gate_up, down)
        away_recv = swapped(away_send, "rep")
        home_mine, home_cross = halves(home_keep, home_recv, f32)
        from_x = swapped(home_cross, "tp")
        away_mine, away_cross = halves(away_keep, away_recv, bf16)
        from_y = swapped(away_mine, "req")
        corner = [(i, i ^ 3) for i in range(n_req * n_tp)]
        from_corner = lax.ppermute(away_cross, ("req", "tp"), corner)
        mine, *others = square_sum(rows, home_mine, from_x, from_y, from_corner)
        line = [lax.ppermute(other, "req", step) for other, step in zip(others, steps)]
        return line_sum(mine, *line)
    x_own = lax.all_to_all(payload, "req", split_axis=0, concat_axis=0, tiled=True)
    x_own = x_own.reshape(n_req * rows, -1)
    x_other = swapped(x_own, "rep")
    mix_keep, mix_send = home_expert(
        n_tp, lambda: lax.axis_index("req"), x_own, x_other, residual, gate_up, down
    )
    mix_recv = swapped(mix_send, "rep")
    pieces = pair_sum(n_tp, n_req, rows, (lambda q: q,), mix_keep, mix_recv)
    pieces = pieces.reshape(n_req * n_tp, rows, -1)
    pieces = lax.all_to_all(pieces, ("req", "tp"), split_axis=0, concat_axis=0, tiled=True)
    return final(pieces)


def solution(mesh):
    placed = (
        P(("rep", "req"), "tp"),
        P(None, "req"),
        P("req"),
        P(("rep", "req"), None, "tp", None),
        P(),
        P(),
        P(None, "tp"),
        P(None, "tp"),
        P("tp", None),
        P(("rep", "req"), None, None, "tp"),
        P(("rep", "req"), "tp", None),
        P(("rep", "req"), None),
        P(("rep", "req"), None),
    )
    return jax.shard_map(
        shards, mesh=mesh, in_specs=placed, out_specs=P(("rep", "req"), "tp"), check_vma=False
    )
```

```python
import jax
import jax.numpy as jnp
from jax import lax
from jax.experimental import pallas as pl
from jax.experimental.pallas import tpu as pltpu
from jax.sharding import PartitionSpec as P

HEAD = 64
EPS = 1e-06
ROPE_BASE = 10000.0
MASKED = -1e30
LANES = 128
QROWS = 16
SPAN = 128
UNROLL = 16
EARLY = 17
PIECES = 4
MIB = 1 << 20

bf16 = jnp.bfloat16
f32 = jnp.float32


def vmem():
    return pl.BlockSpec(memory_space=pltpu.VMEM)


def smem():
    return pl.BlockSpec(memory_space=pltpu.SMEM)


def hbm():
    return pl.BlockSpec(memory_space=pl.ANY)


def swapped(value, axis):
    return lax.ppermute(value, axis, [(i, i ^ 1) for i in range(lax.axis_size(axis))])


def normed_rows(rows, gain):
    mean_square = jnp.mean(rows * rows, axis=-1, keepdims=True)
    return (rows * lax.rsqrt(mean_square + EPS) * gain).astype(bf16)


def rest_copy(kv_hbm, kvbuf, sem, spans, wide, r):
    count = (spans[r] + SPAN - 1) // SPAN - 1
    rest = pl.ds(wide, pl.multiple_of(count * wide, wide))
    return count > 0, pltpu.make_async_copy(kv_hbm.at[r, rest], kvbuf.at[r, rest], sem.at[r])


def fetch_kernel(wide, per, *refs):
    (lens_hbm, ids_hbm, gates_hbm, gain_hbm, own_hbm, kv_hbm) = refs[:6]
    (own, gain, cos_out, sin_out, table_out, kvbuf, spans, items, count) = refs[6:15]
    lens, ids_t, gates_t, sems, ksem, rsem = refs[15:]
    rows = own.shape[0]
    rep = lax.axis_index("rep")

    pairs = (
        (lens_hbm, lens),
        (ids_hbm, ids_t),
        (gates_hbm, gates_t),
        (own_hbm, own),
        (gain_hbm, gain),
    )
    first = pl.ds(0, wide)
    copies = [pltpu.make_async_copy(src, dst, sems.at[i]) for i, (src, dst) in enumerate(pairs)]
    for copy in copies:
        copy.start()
    head_copies = [pltpu.make_async_copy(kv_hbm.at[r, first], kvbuf.at[r, first], ksem.at[r]) for r in range(rows)]
    for copy in head_copies:
        copy.start()

    lane = lax.broadcasted_iota(jnp.int32, (rows, LANES), 1)
    slot = lax.broadcasted_iota(jnp.int32, (rows, LANES), 0)
    half = HEAD // 2
    freq = jnp.zeros((1, LANES), f32)
    for i in range(half):
        freq = jnp.where(lane[:1] % half == i, ROPE_BASE ** (-2.0 * i / HEAD), freq)

    copies[0].wait()
    for r in range(rows):
        spans[r] = lens[rep, r]

        items[r] = r * per

    def plan_row(r, carry):
        n, early = carry
        some, copy = rest_copy(kv_hbm, kvbuf, rsem, spans, wide, r)
        soon = n < EARLY
        pl.when(some & soon)(copy.start)

        def plan_chunk(c, n):
            items[n] = r * per + c
            return n + 1

        later = lax.fori_loop(1, (spans[r] + SPAN - 1) // SPAN, plan_chunk, n)
        return later, jnp.where(soon, r + 1, early)

    total, early = lax.fori_loop(0, rows, plan_row, (rows, 0))
    for u in range(UNROLL):
        items[total + u] = rows * per
    count[0] = total
    count[1] = early

    copies[1].wait()
    copies[2].wait()
    span = jnp.zeros((rows, LANES), jnp.int32)
    for r in range(rows):
        span = jnp.where(slot == r, lens[rep, r], span)
    angle = span.astype(f32) * freq
    sine = jnp.sin(angle)
    cos_out[...] = jnp.cos(angle)
    sin_out[...] = jnp.where(lane % HEAD < half, -sine, sine)

    n_experts = lax.axis_size("rep") * lax.axis_size("req")
    extra = table_out.shape[1]
    lane = lax.broadcasted_iota(jnp.int32, (rows, extra), 1)
    ids, gates = jnp.transpose(ids_t[...]), jnp.transpose(gates_t[...])
    table = jnp.zeros((rows, extra), f32)
    for k in range(ids.shape[1]):
        chosen, weight = ids[:, k : k + 1], gates[:, k : k + 1]
        top = weight.astype(bf16).astype(f32)
        table = jnp.where(lane == chosen, top, table)
        table = jnp.where(lane == chosen + n_experts, weight - top, table)
    table_out[...] = table.astype(bf16)

    for copy in head_copies:
        copy.wait()

    def arrive(r, carry):
        some, copy = rest_copy(kv_hbm, kvbuf, rsem, spans, wide, r)
        pl.when(some)(copy.wait)
        return carry

    lax.fori_loop(0, early, arrive, 0)
    for copy in copies[3:]:
        copy.wait()


def far(*arrays):
    return [pltpu.with_memory_space_constraint(x, pltpu.HBM) for x in arrays]


def close(*arrays):
    return [pltpu.with_memory_space_constraint(x, pltpu.SMEM) for x in arrays]


def near(*arrays):
    return [pltpu.with_memory_space_constraint(x, pltpu.VMEM) for x in arrays]


def fetch(extra, lens, ids, gates, gain, own, wq, wkv, kv):
    rows = own.shape[0]
    wide = SPAN * (wkv.shape[1] // (2 * HEAD))
    per = kv.shape[1] // wide
    outs = [(own.shape, bf16), (gain.shape, f32)]
    outs += [((rows, LANES), f32), ((rows, LANES), f32), ((rows, extra), bf16), (kv.shape, bf16)]
    scalars = [(rows,), (rows * per + UNROLL,), (2,)]
    return pl.pallas_call(
        lambda *refs: fetch_kernel(wide, per, *refs),
        out_shape=tuple(pltpu.VMEM(shape, dtype) for shape, dtype in outs)
        + tuple(pltpu.SMEM(shape, jnp.int32) for shape in scalars),
        in_specs=[hbm()] * 6,
        out_specs=(vmem(),) * len(outs) + (smem(),) * len(scalars),
        scratch_shapes=[
            pltpu.SMEM(lens.shape, jnp.int32),
            pltpu.VMEM(ids.shape[::-1], jnp.int32),
            pltpu.VMEM(gates.shape[::-1], f32),
            pltpu.SemaphoreType.DMA((5,)),
            pltpu.SemaphoreType.DMA((rows,)),
            pltpu.SemaphoreType.DMA((rows,)),
        ],
        compiler_params=pltpu.CompilerParams(vmem_limit_bytes=8 * MIB),
        name="fetch",
    )(*far(lens, ids.T, gates.T, gain, own, kv))


def attention_kernel(n_parts, *refs):
    spans, items, count = refs[:3]
    refs = refs[3:]
    parts = refs[:n_parts]
    (cos_ref, sin_ref, gain_ref, wq, wkv, _, wo_hbm, kv_hbm) = refs[n_parts : 8 + n_parts]
    (tok_out, keep_out, send_out, kvbuf) = refs[8 + n_parts : 12 + n_parts]
    (wo, qf, qb, kvn, mixes, sums, peaks, macc, lacc, oacc, ctx, wsem, ksem) = refs[12 + n_parts :]
    rows = tok_out.shape[0]
    n_query = wq.shape[1] // HEAD
    n_kv = wkv.shape[1] // (2 * HEAD)
    group = n_query // n_kv
    wide = SPAN * n_kv
    per = kv_hbm.shape[1] // wide
    tp = lax.axis_index("tp")

    total, early = count[0], count[1]
    blocks = (total + UNROLL - 1) // UNROLL

    def begin(r, carry):
        some, copy = rest_copy(kv_hbm, kvbuf, ksem, spans, wide, r)
        pl.when(some)(copy.start)
        return carry

    lax.fori_loop(early, rows, begin, 0)
    part = wo.shape[0] // PIECES
    wo_copies = [
        pltpu.make_async_copy(wo_hbm.at[pl.ds(i * part, part)], wo.at[pl.ds(i * part, part)], wsem.at[i])
        for i in range(PIECES)
    ]
    for copy in wo_copies:
        copy.start()

    if n_parts == 2:
        tokens = jnp.concatenate(
            [
                jnp.where(tp == 0, parts[0][...], parts[1][...]),
                jnp.where(tp == 0, parts[1][...], parts[0][...]),
            ],
            axis=1,
        )
    else:
        tokens = parts[0][...]
    tok_out[...] = tokens
    normed = normed_rows(tokens.astype(f32), gain_ref[...].reshape(1, -1))

    lane = lax.broadcasted_iota(jnp.int32, (rows, LANES), 1)
    low_half = lane < HEAD
    first = lane % HEAD < HEAD // 2
    cosine, sine = cos_ref[...], sin_ref[...]

    def rotate(v):
        partner = jnp.where(first, pltpu.roll(v, LANES - HEAD // 2, 1), pltpu.roll(v, HEAD // 2, 1))
        return v * cosine + partner * sine

    qf[...] = jnp.zeros_like(qf)
    kvn[...] = jnp.zeros_like(kvn)
    macc[...] = jnp.full_like(macc, MASKED)
    lacc[...] = jnp.zeros_like(lacc)
    oacc[...] = jnp.zeros_like(oacc)
    queries = jnp.dot(normed, wq[...], preferred_element_type=f32)
    for k in range(n_query // 2):
        turned = rotate(queries[:, k * LANES : (k + 1) * LANES]).astype(bf16).astype(f32)
        turned = turned * HEAD**-0.5
        qf[pl.ds(2 * k, rows, stride=QROWS), :] = jnp.where(low_half, turned, 0.0)
        qf[pl.ds(2 * k + 1, rows, stride=QROWS), :] = jnp.where(low_half, pltpu.roll(turned, HEAD, 1), 0.0)
    keyval = jnp.dot(normed, wkv[...], preferred_element_type=f32)
    for h in range(n_kv):
        v = keyval[:, h * LANES : (h + 1) * LANES]
        new = jnp.where(low_half, rotate(v), v).astype(bf16).astype(f32)
        for g in range(group):
            kvn[pl.ds(h * group + g, rows, stride=QROWS), :] = new
    qb[...] = qf[...].astype(bf16).reshape(qb.shape)

    query_row = lax.broadcasted_iota(jnp.int32, (QROWS, wide), 0)
    row_head = sum((query_row >= h * group).astype(jnp.int32) for h in range(1, n_kv + 1))
    column = lax.broadcasted_iota(jnp.int32, (QROWS, wide), 1)
    reach = jnp.where(column % n_kv == row_head, column // n_kv, 1 << 30)

    def folded(op, value):
        out = value[:, :LANES]
        for j in range(1, wide // LANES):
            out = op(out, value[:, j * LANES : (j + 1) * LANES])
        return out

    def chunk(i):
        item = items[i]
        r = item // per
        c = item % per
        kr = jnp.minimum(r, rows - 1)
        return r, c, kvbuf[kr, pl.ds(pl.multiple_of(c * wide, wide), wide), :]

    def arrive(r, carry):
        some, copy = rest_copy(kv_hbm, kvbuf, ksem, spans, wide, r)
        pl.when(some)(copy.wait)
        return carry

    def merge(base, row_of):
        for u in range(UNROLL):
            r = row_of(u)
            before = macc[r]
            after = jnp.maximum(before, peaks[base + u])
            macc[r] = after
            fade, weight = jnp.exp(before - after), jnp.exp(peaks[base + u] - after)
            lacc[r] = fade * lacc[r] + weight * sums[base + u]
            oacc[r] = fade * oacc[r] + weight * mixes[base + u]

    def block(b, ready):
        last = jnp.minimum(items[b * UNROLL + UNROLL - 1] // per, rows - 1) + 1
        last = jnp.where(b * UNROLL + UNROLL <= rows, 0, last)
        lax.fori_loop(ready, last, arrive, 0)
        earlier = jnp.maximum(b - 1, 0) * UNROLL
        merge(b * UNROLL, lambda u: jnp.where(b == 0, rows, items[earlier + u] // per))
        got = [chunk(b * UNROLL + u) for u in range(UNROLL)]
        dots = [
            lax.dot_general(qb[r], kv, (((1,), (1,)), ((), ())), preferred_element_type=f32) for r, c, kv in got
        ]
        tops, probs = [], []
        for (r, c, kv), s in zip(got, dots):
            span = spans[jnp.minimum(r, rows - 1)]
            limit = jnp.where(r < rows, span - c * SPAN, 0)
            s = jnp.where(reach < limit, s, MASKED)
            top = jnp.max(folded(jnp.maximum, s), axis=-1, keepdims=True)
            tops.append(jnp.broadcast_to(top, (QROWS, LANES)))
            probs.append(jnp.exp(s - top))
        for u, p in enumerate(probs):
            i = (b + 1) * UNROLL + u
            mixes[i] = jnp.dot(p.astype(bf16), got[u][2], preferred_element_type=f32)
            sums[i] = folded(jnp.add, p)
            peaks[i] = tops[u]
        return jnp.maximum(ready, last)

    mixes[:UNROLL] = jnp.zeros((UNROLL, QROWS, LANES), f32)
    sums[:UNROLL] = jnp.zeros((UNROLL, QROWS, LANES), f32)
    peaks[:UNROLL] = jnp.full((UNROLL, QROWS, LANES), MASKED, f32)
    ready = lax.fori_loop(0, blocks, block, early)
    lax.fori_loop(ready, rows, arrive, 0)
    merge(blocks * UNROLL, lambda u: items[(blocks - 1) * UNROLL + u] // per)

    own = jnp.sum(qf[...] * kvn[...], axis=-1, keepdims=True)
    before = macc[...].reshape(qf.shape)
    peak = jnp.maximum(before, own)
    own_p, fade = jnp.exp(own - peak), jnp.exp(before - peak)

    total_p = jnp.sum(fade * lacc[...].reshape(qf.shape), axis=-1, keepdims=True) + own_p
    qf[...] = (fade * oacc[...].reshape(qf.shape) + own_p * kvn[...]) / total_p
    for k in range(n_query // 2):
        a = qf[pl.ds(2 * k, rows, stride=QROWS), :]
        b = qf[pl.ds(2 * k + 1, rows, stride=QROWS), :]
        ctx[:, k * LANES : (k + 1) * LANES] = jnp.where(low_half, pltpu.roll(a, HEAD, 1), b).astype(bf16)
    for copy in wo_copies:
        copy.wait()
    partial = jnp.dot(ctx[...], wo[...], preferred_element_type=f32)
    keep_out[...] = partial
    send_out[...] = partial.astype(bf16)


def attention(plan, parts, cosine, sine, gain, wq, wkv, kv_near, wo, kv):
    rows = parts[0].shape[0]
    width = wq.shape[0]
    n_kv = wkv.shape[1] // (2 * HEAD)
    per = kv.shape[1] // (SPAN * n_kv)
    slots = rows * per + 2 * UNROLL
    many = rows + 1
    return pl.pallas_call(
        lambda *refs: attention_kernel(len(parts), *refs),
        out_shape=(
            pltpu.VMEM((rows, width), bf16),
            pltpu.VMEM((rows, width), f32),
            pltpu.VMEM((rows, width), bf16),
            pltpu.VMEM(kv.shape, bf16),
        ),
        in_specs=[smem()] * 3 + [vmem()] * (len(parts) + 6) + [hbm()] * 2,
        out_specs=(vmem(), vmem(), vmem(), vmem()),
        input_output_aliases={8 + len(parts): 3},
        scratch_shapes=[
            pltpu.VMEM(wo.shape, bf16),
            pltpu.VMEM((many * QROWS, LANES), f32),
            pltpu.VMEM((many, QROWS, LANES), bf16),
            pltpu.VMEM((many * QROWS, LANES), f32),
            pltpu.VMEM((slots, QROWS, LANES), f32),
            pltpu.VMEM((slots, QROWS, LANES), f32),
            pltpu.VMEM((slots, QROWS, LANES), f32),
            pltpu.VMEM((many, QROWS, LANES), f32),
            pltpu.VMEM((many, QROWS, LANES), f32),
            pltpu.VMEM((many, QROWS, LANES), f32),
            pltpu.VMEM((rows, wq.shape[1]), bf16),
            pltpu.SemaphoreType.DMA((PIECES,)),
            pltpu.SemaphoreType.DMA((rows,)),
        ],
        compiler_params=pltpu.CompilerParams(vmem_limit_bytes=16 * MIB),
        name="attention",
    )(*close(*plan), *near(*parts, cosine, sine, gain, wq, wkv, kv_near), *far(wo, kv))


def expert_input_kernel(n_tp, moved_slot, tokens, keep, other, gain, table, payload, residual_out):
    width = tokens.shape[1]
    tp = lax.axis_index("tp")
    residual = tokens[...].astype(f32) + keep[...] + other[...].astype(f32)
    part = width // n_tp
    mine = residual[:, :part]
    for t in range(1, n_tp):
        mine = jnp.where(tp == t, residual[:, t * part : (t + 1) * part], mine)
    residual_out[...] = mine
    expert_in = normed_rows(residual, gain[...].reshape(1, -1))
    lane = lax.broadcasted_iota(jnp.int32, table.shape, 1)
    slot = lax.broadcasted_iota(jnp.int32, table.shape, 0)
    n_experts = lax.axis_size("rep") * lax.axis_size("req")
    moved = (lane == 2 * n_experts) & (slot == moved_slot[0])
    marked = jnp.where(moved, 1.0, table[...].astype(f32)).astype(bf16)
    for q in range(payload.shape[0]):
        payload[q, :, :width] = expert_in
        payload[q, :, width:] = marked


def stacked_kernel(*refs):
    blocks, whole, tail = refs[:-2], refs[-2], refs[-1]
    rows = blocks[0].shape[0]
    for k, block in enumerate(blocks):
        whole[k * rows : (k + 1) * rows] = block[...]
        if k:
            tail[(k - 1) * rows : k * rows] = block[...]


def stacked(blocks):
    rows, width = blocks[0].shape
    return pl.pallas_call(
        stacked_kernel,
        out_shape=(
            pltpu.VMEM((len(blocks) * rows, width), bf16),
            pltpu.VMEM(((len(blocks) - 1) * rows, width), bf16),
        ),
        in_specs=[vmem()] * len(blocks),
        out_specs=(vmem(), vmem()),
        compiler_params=pltpu.CompilerParams(vmem_limit_bytes=8 * MIB),
        name="stacked",
    )(*near(*blocks))


def joined_kernel(first, second, out):
    rows = first.shape[0]
    out[:rows] = first[...]
    out[rows:] = second[...]


def joined(first, second):
    return pl.pallas_call(
        joined_kernel,
        out_shape=pltpu.VMEM((first.shape[0] + second.shape[0], first.shape[1]), bf16),
        in_specs=[vmem()] * 2,
        out_specs=vmem(),
        compiler_params=pltpu.CompilerParams(vmem_limit_bytes=8 * MIB),
        name="joined",
    )(*near(first, second))


def expert_input(n_tp, n_req, moved, tokens, keep, other, gain, table):
    rows, width = tokens.shape
    return pl.pallas_call(
        lambda *refs: expert_input_kernel(n_tp, *refs),
        out_shape=(
            pltpu.VMEM((n_req, rows, width + table.shape[1]), bf16),
            pltpu.VMEM((rows, width // n_tp), f32),
        ),
        in_specs=[smem()] + [vmem()] * 5,
        out_specs=(vmem(), vmem()),
        compiler_params=pltpu.CompilerParams(vmem_limit_bytes=8 * MIB),
        name="expert_input",
    )(moved, *near(tokens, keep, other), gain, *near(table))


def expert_rows(rows, gate_up, down):
    projected = jnp.dot(rows, gate_up, preferred_element_type=f32)
    hidden = projected.shape[1] // 2
    gate, up = projected[:, :hidden], projected[:, hidden:]
    active = (gate / (1.0 + jnp.exp(-gate)) * up).astype(bf16)
    return jnp.dot(active, down, preferred_element_type=f32)


def own_expert_kernel(x, gate_up, down, y):
    width = down.shape[1]
    y[...] = expert_rows(x[:, :width], gate_up[...], down[...])


def own_expert(x, gate_up, down):
    return pl.pallas_call(
        own_expert_kernel,
        out_shape=pltpu.VMEM((x.shape[0], down.shape[1]), f32),
        in_specs=[vmem()] * 3,
        out_specs=vmem(),
        compiler_params=pltpu.CompilerParams(vmem_limit_bytes=32 * MIB),
        cost_estimate=expert_cost(x.shape[0], gate_up, down),
        name="own_expert",
    )(*near(x), gate_up, down)


def expert_cost(count, gate_up, down):
    return pl.CostEstimate(
        flops=2 * count * (gate_up.size + down.size),
        bytes_accessed=2 * (gate_up.size + down.size) + 10 * count * down.shape[1],
        transcendentals=count * down.shape[0],
    )


def traded(width, x_own, x_other, from_own, from_other, keep, send):
    n_req = lax.axis_size("req")
    n_experts = lax.axis_size("rep") * n_req
    expert = lax.axis_index("rep") * n_req + lax.axis_index("req")
    own_table = x_own[:, width:].astype(f32)
    other_table = x_other[:, width:].astype(f32)
    lane = lax.broadcasted_iota(jnp.int32, own_table.shape, 1)

    def picked(table, mask):
        return jnp.sum(jnp.where(mask, table, 0.0), axis=-1, keepdims=True)

    gated = (lane == expert) | (lane == expert + n_experts)
    own_gate, other_gate = picked(own_table, gated), picked(other_table, gated)
    moved = picked(own_table, lane == 2 * n_experts) > 0.5
    from_own = from_own(jnp.where(moved, other_gate, own_gate))
    from_other = from_other() * jnp.where(moved, own_gate, other_gate)
    keep[...] = jnp.where(moved, from_other, from_own)
    send[...] = jnp.where(moved, from_own, from_other).astype(bf16)


def home_expert_kernel(n_tp, place, x_own, x_other, residual, gate_up, down, keep, send, mine):
    width = down.shape[1]
    count = x_own.shape[0]
    both = jnp.concatenate([x_own[:, :width], x_other[:, :width]], axis=0)
    y = expert_rows(both, gate_up[...], down[...])
    rows, part = residual.shape
    tp = lax.axis_index("tp")
    here = pl.ds(place() * rows, rows)

    def from_own(gate):
        mine[...] = y[:count] * gate
        for t in range(n_tp):

            @pl.when(tp == t)
            def _():
                mine[here, t * part : (t + 1) * part] += residual[...]

        return mine[...]

    traded(width, x_own, x_other, from_own, lambda: y[count:], keep, send)


def home_expert(n_tp, place, x_own, x_other, residual, gate_up, down):
    shape = (x_own.shape[0], down.shape[1])
    return pl.pallas_call(
        lambda *refs: home_expert_kernel(n_tp, place, *refs),
        out_shape=(pltpu.VMEM(shape, f32), pltpu.VMEM(shape, bf16)),
        in_specs=[vmem()] * 5,
        out_specs=(vmem(), vmem()),
        scratch_shapes=[pltpu.VMEM(shape, f32)],
        compiler_params=pltpu.CompilerParams(vmem_limit_bytes=40 * MIB if shape[0] > 256 else 16 * MIB),
        cost_estimate=expert_cost(2 * shape[0], gate_up, down),
        name="home_expert",
    )(*near(x_own, x_other, residual), gate_up, down)


def other_expert_kernel(x_own, x_other, y_own, gate_up, down, keep, send):
    width = down.shape[1]

    def from_other():
        return expert_rows(x_other[:, :width], gate_up[...], down[...])

    traded(width, x_own, x_other, lambda gate: y_own[...] * gate, from_other, keep, send)


def other_expert(x_own, x_other, y_own, gate_up, down):
    return pl.pallas_call(
        other_expert_kernel,
        out_shape=(pltpu.VMEM(y_own.shape, f32), pltpu.VMEM(y_own.shape, bf16)),
        in_specs=[vmem()] * 5,
        out_specs=(vmem(), vmem()),
        compiler_params=pltpu.CompilerParams(vmem_limit_bytes=16 * MIB),
        cost_estimate=expert_cost(y_own.shape[0], gate_up, down),
        name="other_expert",
    )(*near(x_own, x_other, y_own), gate_up, down)


def pair_sum_kernel(n_tp, spots, *refs):
    out = refs[-1]
    _, _, rows, part = out.shape
    for i, spot in enumerate(spots):
        keep, recv = refs[2 * i], refs[2 * i + 1]
        total = (keep[...] + recv[...].astype(f32)).astype(bf16)
        for q in range(total.shape[0] // rows):
            for t in range(n_tp):
                out[spot(q), t] = total[q * rows : (q + 1) * rows, t * part : (t + 1) * part]


def pair_sum(n_tp, n_req, rows, spots, *sums):
    part = sums[0].shape[1] // n_tp
    return pl.pallas_call(
        lambda *refs: pair_sum_kernel(n_tp, spots, *refs),
        out_shape=pltpu.VMEM((n_req, n_tp, rows, part), bf16),
        in_specs=[vmem()] * len(sums),
        out_specs=vmem(),
        compiler_params=pltpu.CompilerParams(vmem_limit_bytes=16 * MIB),
        name="pair_sum",
    )(*near(*sums))


def halves_kernel(keep, recv, mine, cross):
    total = keep[...] + recv[...].astype(f32)
    part = mine.shape[1]
    low, high = total[:, :part], total[:, part:]
    first = lax.axis_index("tp") == 0
    mine[...] = jnp.where(first, low, high).astype(mine.dtype)
    cross[...] = jnp.where(first, high, low).astype(bf16)


def halves(keep, recv, kind):
    shape = (keep.shape[0], keep.shape[1] // 2)
    return pl.pallas_call(
        halves_kernel,
        out_shape=(pltpu.VMEM(shape, kind), pltpu.VMEM(shape, bf16)),
        in_specs=[vmem()] * 2,
        out_specs=(vmem(), vmem()),
        compiler_params=pltpu.CompilerParams(vmem_limit_bytes=8 * MIB),
        name="halves",
    )(*near(keep, recv))


def square_sum_kernel(mine, *refs):
    arrived, outs = refs[:3], refs[3:]
    total = mine[...]
    for piece in arrived:
        total = total + piece[...].astype(f32)
    rows = outs[0].shape[0]
    for k, out in enumerate(outs):
        out[...] = total[k * rows : (k + 1) * rows].astype(out.dtype)


def square_sum(rows, mine, *arrived):
    shape = (rows, mine.shape[1])
    count = mine.shape[0] // rows
    return pl.pallas_call(
        square_sum_kernel,
        out_shape=(pltpu.VMEM(shape, f32),) + (pltpu.VMEM(shape, bf16),) * (count - 1),
        in_specs=[vmem()] * 4,
        out_specs=(vmem(),) * count,
        compiler_params=pltpu.CompilerParams(vmem_limit_bytes=8 * MIB),
        name="square_sum",
    )(*near(mine, *arrived))


def line_sum_kernel(*refs):
    total = refs[0][...]
    for piece in refs[1:-1]:
        total = total + piece[...].astype(f32)
    refs[-1][...] = total.astype(bf16)


def line_sum(mine, *arrived):
    return pl.pallas_call(
        line_sum_kernel,
        out_shape=jax.ShapeDtypeStruct(mine.shape, bf16),
        in_specs=[vmem()] * (1 + len(arrived)),
        out_specs=vmem(),
        compiler_params=pltpu.CompilerParams(vmem_limit_bytes=8 * MIB),
        name="line_sum",
    )(*near(mine, *arrived))


def final_kernel(pieces, out):
    total = pieces[0].astype(f32)
    for i in range(1, pieces.shape[0]):
        total = total + pieces[i].astype(f32)
    out[...] = total.astype(bf16)


def final(pieces):
    return pl.pallas_call(
        final_kernel,
        out_shape=jax.ShapeDtypeStruct(pieces.shape[1:], bf16),
        in_specs=[vmem()],
        out_specs=vmem(),
        compiler_params=pltpu.CompilerParams(vmem_limit_bytes=8 * MIB),
        name="final",
    )(*near(pieces))


def shards(
    hidden,
    lengths,
    migrate,
    kv_cache,
    attn_gain,
    moe_gain,
    w_query,
    key_value_weight,
    output_weight,
    w_gateup,
    w_down,
    expert_ids,
    expert_gates,
):
    rows = hidden.shape[0]
    n_rep, n_req, n_tp = lax.axis_size("rep"), lax.axis_size("req"), lax.axis_size("tp")
    extra = -(-(2 * n_rep * n_req + 1) // LANES) * LANES

    if n_tp == 2:
        other_part = swapped(hidden, "tp")
    else:
        all_parts = lax.all_gather(hidden, "tp", axis=1, tiled=True)
    kv = kv_cache.reshape(rows, -1, LANES)
    own, gain, cosine, sine, table, kv_near, *plan = fetch(
        extra,
        lengths,
        expert_ids,
        expert_gates,
        attn_gain,
        hidden,
        w_query,
        key_value_weight,
        kv,
    )
    parts = [own, other_part] if n_tp == 2 else [all_parts]
    tokens, keep, send, _ = attention(
        plan, parts, cosine, sine, gain, w_query, key_value_weight, kv_near, output_weight, kv
    )
    gate_up = w_gateup[0].reshape(w_gateup.shape[1], -1)
    down = w_down[0]
    if n_tp == 2:
        other = swapped(send, "tp")
        gate_up, other = lax.optimization_barrier((gate_up, other))
    else:
        other = lax.psum(keep.astype(bf16), "tp").astype(f32) - keep
    by_permute = n_req == 8 and n_tp == 2
    payload, residual = expert_input(n_tp, 1 if by_permute else n_req, migrate, tokens, keep, other, moe_gain, table)
    if by_permute:
        payload = payload[0]
        steps = [[(q, q ^ 2 * k) for q in range(n_req)] for k in (1, 2, 3)]
        beside = [lax.ppermute(payload, "req", step) for step in steps]
        across = swapped(payload, "req")
        home, tail = stacked([payload] + beside)
        away = joined(across, swapped(tail, "req"))
        home_other = swapped(home, "rep")
        home_keep, home_send = home_expert(
            n_tp, lambda: 0, home, home_other, residual, gate_up, down
        )
        home_recv = swapped(home_send, "rep")
        away_other = swapped(away, "rep")
        away_own = own_expert(away, gate_up, down)
        away_keep, away_send = other_expert(away, away_other, away_own, gate_up, down)
        away_recv = swapped(away_send, "rep")
        home_mine, home_cross = halves(home_keep, home_recv, f32)
        from_x = swapped(home_cross, "tp")
        away_mine, away_cross = halves(away_keep, away_recv, bf16)
        from_y = swapped(away_mine, "req")
        corner = [(i, i ^ 3) for i in range(n_req * n_tp)]
        from_corner = lax.ppermute(away_cross, ("req", "tp"), corner)
        mine, *others = square_sum(rows, home_mine, from_x, from_y, from_corner)
        line = [lax.ppermute(other, "req", step) for other, step in zip(others, steps)]
        return line_sum(mine, *line)
    x_own = lax.all_to_all(payload, "req", split_axis=0, concat_axis=0, tiled=True)
    x_own = x_own.reshape(n_req * rows, -1)
    x_other = swapped(x_own, "rep")
    mix_keep, mix_send = home_expert(
        n_tp, lambda: lax.axis_index("req"), x_own, x_other, residual, gate_up, down
    )
    mix_recv = swapped(mix_send, "rep")
    pieces = pair_sum(n_tp, n_req, rows, (lambda q: q,), mix_keep, mix_recv)
    pieces = pieces.reshape(n_req * n_tp, rows, -1)
    pieces = lax.all_to_all(pieces, ("req", "tp"), split_axis=0, concat_axis=0, tiled=True)
    return final(pieces)


def solution(mesh):
    placed = (
        P(("rep", "req"), "tp"),
        P(None, "req"),
        P("req"),
        P(("rep", "req"), None, "tp", None),
        P(),
        P(),
        P(None, "tp"),
        P(None, "tp"),
        P("tp", None),
        P(("rep", "req"), None, None, "tp"),
        P(("rep", "req"), "tp", None),
        P(("rep", "req"), None),
        P(("rep", "req"), None),
    )
    return jax.shard_map(
        shards, mesh=mesh, in_specs=placed, out_specs=P(("rep", "req"), "tp"), check_vma=False
    )
```

```python
import jax
import jax.numpy as jnp
from jax import lax
from jax.experimental import pallas as pl
from jax.experimental.pallas import tpu as pltpu
from jax.sharding import PartitionSpec as P

HEAD = 64
EPS = 1e-06
ROPE_BASE = 10000.0
MASKED = -1e30
LANES = 128
QROWS = 16
SPAN = 128
UNROLL = 16
EARLY = 17
PIECES = 4
MIB = 1 << 20

bf16 = jnp.bfloat16
f32 = jnp.float32


def vmem():
    return pl.BlockSpec(memory_space=pltpu.VMEM)


def smem():
    return pl.BlockSpec(memory_space=pltpu.SMEM)


def hbm():
    return pl.BlockSpec(memory_space=pl.ANY)


def swapped(value, axis):
    return lax.ppermute(value, axis, [(i, i ^ 1) for i in range(lax.axis_size(axis))])


def normed_rows(rows, gain):
    mean_square = jnp.mean(rows * rows, axis=-1, keepdims=True)
    return (rows * lax.rsqrt(mean_square + EPS) * gain).astype(bf16)


def rest_copy(kv_hbm, kvbuf, sem, spans, wide, r):
    count = (spans[r] + SPAN - 1) // SPAN - 1
    rest = pl.ds(wide, pl.multiple_of(count * wide, wide))
    return count > 0, pltpu.make_async_copy(kv_hbm.at[r, rest], kvbuf.at[r, rest], sem.at[r])


def fetch_kernel(wide, per, *refs):
    (lens_hbm, ids_hbm, gates_hbm, gain_hbm, own_hbm, kv_hbm) = refs[:6]
    (own, gain, cos_out, sin_out, table_out, kvbuf, spans, items, count) = refs[6:15]
    lens, ids_t, gates_t, sems, ksem, rsem = refs[15:]
    rows = own.shape[0]
    rep = lax.axis_index("rep")

    pairs = (
        (lens_hbm, lens),
        (ids_hbm, ids_t),
        (gates_hbm, gates_t),
        (own_hbm, own),
        (gain_hbm, gain),
    )
    first = pl.ds(0, wide)
    copies = [pltpu.make_async_copy(src, dst, sems.at[i]) for i, (src, dst) in enumerate(pairs)]
    for copy in copies:
        copy.start()
    head_copies = [pltpu.make_async_copy(kv_hbm.at[r, first], kvbuf.at[r, first], ksem.at[r]) for r in range(rows)]
    for copy in head_copies:
        copy.start()

    lane = lax.broadcasted_iota(jnp.int32, (rows, LANES), 1)
    slot = lax.broadcasted_iota(jnp.int32, (rows, LANES), 0)
    half = HEAD // 2
    freq = jnp.zeros((1, LANES), f32)
    for i in range(half):
        freq = jnp.where(lane[:1] % half == i, ROPE_BASE ** (-2.0 * i / HEAD), freq)

    copies[0].wait()
    for r in range(rows):
        spans[r] = lens[rep, r]

        items[r] = r * per

    def plan_row(r, carry):
        n, early = carry
        some, copy = rest_copy(kv_hbm, kvbuf, rsem, spans, wide, r)
        soon = n < EARLY
        pl.when(some & soon)(copy.start)

        def plan_chunk(c, n):
            items[n] = r * per + c
            return n + 1

        later = lax.fori_loop(1, (spans[r] + SPAN - 1) // SPAN, plan_chunk, n)
        return later, jnp.where(soon, r + 1, early)

    total, early = lax.fori_loop(0, rows, plan_row, (rows, 0))
    for u in range(UNROLL):
        items[total + u] = rows * per
    count[0] = total
    count[1] = early

    copies[1].wait()
    copies[2].wait()
    span = jnp.zeros((rows, LANES), jnp.int32)
    for r in range(rows):
        span = jnp.where(slot == r, lens[rep, r], span)
    angle = span.astype(f32) * freq
    sine = jnp.sin(angle)
    cos_out[...] = jnp.cos(angle)
    sin_out[...] = jnp.where(lane % HEAD < half, -sine, sine)

    n_experts = lax.axis_size("rep") * lax.axis_size("req")
    extra = table_out.shape[1]
    lane = lax.broadcasted_iota(jnp.int32, (rows, extra), 1)
    ids, gates = jnp.transpose(ids_t[...]), jnp.transpose(gates_t[...])
    table = jnp.zeros((rows, extra), f32)
    for k in range(ids.shape[1]):
        chosen, weight = ids[:, k : k + 1], gates[:, k : k + 1]
        top = weight.astype(bf16).astype(f32)
        table = jnp.where(lane == chosen, top, table)
        table = jnp.where(lane == chosen + n_experts, weight - top, table)
    table_out[...] = table.astype(bf16)

    for copy in head_copies:
        copy.wait()

    def arrive(r, carry):
        some, copy = rest_copy(kv_hbm, kvbuf, rsem, spans, wide, r)
        pl.when(some)(copy.wait)
        return carry

    lax.fori_loop(0, early, arrive, 0)
    for copy in copies[3:]:
        copy.wait()


def far(*arrays):
    return [pltpu.with_memory_space_constraint(x, pltpu.HBM) for x in arrays]


def close(*arrays):
    return [pltpu.with_memory_space_constraint(x, pltpu.SMEM) for x in arrays]


def near(*arrays):
    return [pltpu.with_memory_space_constraint(x, pltpu.VMEM) for x in arrays]


def fetch(extra, lens, ids, gates, gain, own, wq, wkv, kv):
    rows = own.shape[0]
    wide = SPAN * (wkv.shape[1] // (2 * HEAD))
    per = kv.shape[1] // wide
    outs = [(own.shape, bf16), (gain.shape, f32)]
    outs += [((rows, LANES), f32), ((rows, LANES), f32), ((rows, extra), bf16), (kv.shape, bf16)]
    scalars = [(rows,), (rows * per + UNROLL,), (2,)]
    return pl.pallas_call(
        lambda *refs: fetch_kernel(wide, per, *refs),
        out_shape=tuple(pltpu.VMEM(shape, dtype) for shape, dtype in outs)
        + tuple(pltpu.SMEM(shape, jnp.int32) for shape in scalars),
        in_specs=[hbm()] * 6,
        out_specs=(vmem(),) * len(outs) + (smem(),) * len(scalars),
        scratch_shapes=[
            pltpu.SMEM(lens.shape, jnp.int32),
            pltpu.VMEM(ids.shape[::-1], jnp.int32),
            pltpu.VMEM(gates.shape[::-1], f32),
            pltpu.SemaphoreType.DMA((5,)),
            pltpu.SemaphoreType.DMA((rows,)),
            pltpu.SemaphoreType.DMA((rows,)),
        ],
        compiler_params=pltpu.CompilerParams(vmem_limit_bytes=8 * MIB),
        name="fetch",
    )(*far(lens, ids.T, gates.T, gain, own, kv))


def attention_kernel(n_parts, *refs):
    spans, items, count = refs[:3]
    refs = refs[3:]
    parts = refs[:n_parts]
    (cos_ref, sin_ref, gain_ref, wq, wkv, _, wo_hbm, kv_hbm) = refs[n_parts : 8 + n_parts]
    (tok_out, keep_out, send_out, kvbuf) = refs[8 + n_parts : 12 + n_parts]
    (wo, qf, qb, kvn, mixes, sums, peaks, macc, lacc, oacc, ctx, wsem, ksem) = refs[12 + n_parts :]
    rows = tok_out.shape[0]
    n_query = wq.shape[1] // HEAD
    n_kv = wkv.shape[1] // (2 * HEAD)
    group = n_query // n_kv
    wide = SPAN * n_kv
    per = kv_hbm.shape[1] // wide
    tp = lax.axis_index("tp")

    total, early = count[0], count[1]
    blocks = (total + UNROLL - 1) // UNROLL

    def begin(r, carry):
        some, copy = rest_copy(kv_hbm, kvbuf, ksem, spans, wide, r)
        pl.when(some)(copy.start)
        return carry

    lax.fori_loop(early, rows, begin, 0)
    part = wo.shape[0] // PIECES
    wo_copies = [
        pltpu.make_async_copy(wo_hbm.at[pl.ds(i * part, part)], wo.at[pl.ds(i * part, part)], wsem.at[i])
        for i in range(PIECES)
    ]
    for copy in wo_copies:
        copy.start()

    if n_parts == 2:
        tokens = jnp.concatenate(
            [
                jnp.where(tp == 0, parts[0][...], parts[1][...]),
                jnp.where(tp == 0, parts[1][...], parts[0][...]),
            ],
            axis=1,
        )
    else:
        tokens = parts[0][...]
    tok_out[...] = tokens
    normed = normed_rows(tokens.astype(f32), gain_ref[...].reshape(1, -1))

    lane = lax.broadcasted_iota(jnp.int32, (rows, LANES), 1)
    low_half = lane < HEAD
    first = lane % HEAD < HEAD // 2
    cosine, sine = cos_ref[...], sin_ref[...]

    def rotate(v):
        partner = jnp.where(first, pltpu.roll(v, LANES - HEAD // 2, 1), pltpu.roll(v, HEAD // 2, 1))
        return v * cosine + partner * sine

    qf[...] = jnp.zeros_like(qf)
    kvn[...] = jnp.zeros_like(kvn)
    macc[...] = jnp.full_like(macc, MASKED)
    lacc[...] = jnp.zeros_like(lacc)
    oacc[...] = jnp.zeros_like(oacc)
    queries = jnp.dot(normed, wq[...], preferred_element_type=f32)
    for k in range(n_query // 2):
        turned = rotate(queries[:, k * LANES : (k + 1) * LANES]).astype(bf16).astype(f32)
        turned = turned * HEAD**-0.5
        qf[pl.ds(2 * k, rows, stride=QROWS), :] = jnp.where(low_half, turned, 0.0)
        qf[pl.ds(2 * k + 1, rows, stride=QROWS), :] = jnp.where(low_half, pltpu.roll(turned, HEAD, 1), 0.0)
    keyval = jnp.dot(normed, wkv[...], preferred_element_type=f32)
    for h in range(n_kv):
        v = keyval[:, h * LANES : (h + 1) * LANES]
        new = jnp.where(low_half, rotate(v), v).astype(bf16).astype(f32)
        for g in range(group):
            kvn[pl.ds(h * group + g, rows, stride=QROWS), :] = new
    qb[...] = qf[...].astype(bf16).reshape(qb.shape)

    query_row = lax.broadcasted_iota(jnp.int32, (QROWS, wide), 0)
    row_head = sum((query_row >= h * group).astype(jnp.int32) for h in range(1, n_kv + 1))
    column = lax.broadcasted_iota(jnp.int32, (QROWS, wide), 1)
    reach = jnp.where(column % n_kv == row_head, column // n_kv, 1 << 30)

    def folded(op, value):
        out = value[:, :LANES]
        for j in range(1, wide // LANES):
            out = op(out, value[:, j * LANES : (j + 1) * LANES])
        return out

    def chunk(i):
        item = items[i]
        r = item // per
        c = item % per
        kr = jnp.minimum(r, rows - 1)
        return r, c, kvbuf[kr, pl.ds(pl.multiple_of(c * wide, wide), wide), :]

    def arrive(r, carry):
        some, copy = rest_copy(kv_hbm, kvbuf, ksem, spans, wide, r)
        pl.when(some)(copy.wait)
        return carry

    def merge(base, row_of):
        for u in range(UNROLL):
            r = row_of(u)
            before = macc[r]
            after = jnp.maximum(before, peaks[base + u])
            macc[r] = after
            fade, weight = jnp.exp(before - after), jnp.exp(peaks[base + u] - after)
            lacc[r] = fade * lacc[r] + weight * sums[base + u]
            oacc[r] = fade * oacc[r] + weight * mixes[base + u]

    def block(b, ready):
        last = jnp.minimum(items[b * UNROLL + UNROLL - 1] // per, rows - 1) + 1
        last = jnp.where(b * UNROLL + UNROLL <= rows, 0, last)
        lax.fori_loop(ready, last, arrive, 0)
        earlier = jnp.maximum(b - 1, 0) * UNROLL
        merge(b * UNROLL, lambda u: jnp.where(b == 0, rows, items[earlier + u] // per))
        got = [chunk(b * UNROLL + u) for u in range(UNROLL)]
        dots = [
            lax.dot_general(qb[r], kv, (((1,), (1,)), ((), ())), preferred_element_type=f32) for r, c, kv in got
        ]
        tops, probs = [], []
        for (r, c, kv), s in zip(got, dots):
            span = spans[jnp.minimum(r, rows - 1)]
            limit = jnp.where(r < rows, span - c * SPAN, 0)
            s = jnp.where(reach < limit, s, MASKED)
            top = jnp.max(folded(jnp.maximum, s), axis=-1, keepdims=True)
            tops.append(jnp.broadcast_to(top, (QROWS, LANES)))
            probs.append(jnp.exp(s - top))
        for u, p in enumerate(probs):
            i = (b + 1) * UNROLL + u
            mixes[i] = jnp.dot(p.astype(bf16), got[u][2], preferred_element_type=f32)
            sums[i] = folded(jnp.add, p)
            peaks[i] = tops[u]
        return jnp.maximum(ready, last)

    mixes[:UNROLL] = jnp.zeros((UNROLL, QROWS, LANES), f32)
    sums[:UNROLL] = jnp.zeros((UNROLL, QROWS, LANES), f32)
    peaks[:UNROLL] = jnp.full((UNROLL, QROWS, LANES), MASKED, f32)
    ready = lax.fori_loop(0, blocks, block, early)
    lax.fori_loop(ready, rows, arrive, 0)
    merge(blocks * UNROLL, lambda u: items[(blocks - 1) * UNROLL + u] // per)

    own = jnp.sum(qf[...] * kvn[...], axis=-1, keepdims=True)
    before = macc[...].reshape(qf.shape)
    peak = jnp.maximum(before, own)
    own_p, fade = jnp.exp(own - peak), jnp.exp(before - peak)

    total_p = jnp.sum(fade * lacc[...].reshape(qf.shape), axis=-1, keepdims=True) + own_p
    qf[...] = (fade * oacc[...].reshape(qf.shape) + own_p * kvn[...]) / total_p
    for k in range(n_query // 2):
        a = qf[pl.ds(2 * k, rows, stride=QROWS), :]
        b = qf[pl.ds(2 * k + 1, rows, stride=QROWS), :]
        ctx[:, k * LANES : (k + 1) * LANES] = jnp.where(low_half, pltpu.roll(a, HEAD, 1), b).astype(bf16)
    for copy in wo_copies:
        copy.wait()
    partial = jnp.dot(ctx[...], wo[...], preferred_element_type=f32)
    keep_out[...] = partial
    send_out[...] = partial.astype(bf16)


def attention(plan, parts, cosine, sine, gain, wq, wkv, kv_near, wo, kv):
    rows = parts[0].shape[0]
    width = wq.shape[0]
    n_kv = wkv.shape[1] // (2 * HEAD)
    per = kv.shape[1] // (SPAN * n_kv)
    slots = rows * per + 2 * UNROLL
    many = rows + 1
    return pl.pallas_call(
        lambda *refs: attention_kernel(len(parts), *refs),
        out_shape=(
            pltpu.VMEM((rows, width), bf16),
            pltpu.VMEM((rows, width), f32),
            pltpu.VMEM((rows, width), bf16),
            pltpu.VMEM(kv.shape, bf16),
        ),
        in_specs=[smem()] * 3 + [vmem()] * (len(parts) + 6) + [hbm()] * 2,
        out_specs=(vmem(), vmem(), vmem(), vmem()),
        input_output_aliases={8 + len(parts): 3},
        scratch_shapes=[
            pltpu.VMEM(wo.shape, bf16),
            pltpu.VMEM((many * QROWS, LANES), f32),
            pltpu.VMEM((many, QROWS, LANES), bf16),
            pltpu.VMEM((many * QROWS, LANES), f32),
            pltpu.VMEM((slots, QROWS, LANES), f32),
            pltpu.VMEM((slots, QROWS, LANES), f32),
            pltpu.VMEM((slots, QROWS, LANES), f32),
            pltpu.VMEM((many, QROWS, LANES), f32),
            pltpu.VMEM((many, QROWS, LANES), f32),
            pltpu.VMEM((many, QROWS, LANES), f32),
            pltpu.VMEM((rows, wq.shape[1]), bf16),
            pltpu.SemaphoreType.DMA((PIECES,)),
            pltpu.SemaphoreType.DMA((rows,)),
        ],
        compiler_params=pltpu.CompilerParams(vmem_limit_bytes=16 * MIB),
        name="attention",
    )(*close(*plan), *near(*parts, cosine, sine, gain, wq, wkv, kv_near), *far(wo, kv))


def expert_input_kernel(n_tp, moved_slot, tokens, keep, other, gain, table, payload, residual_out):
    width = tokens.shape[1]
    tp = lax.axis_index("tp")
    residual = tokens[...].astype(f32) + keep[...] + other[...].astype(f32)
    part = width // n_tp
    mine = residual[:, :part]
    for t in range(1, n_tp):
        mine = jnp.where(tp == t, residual[:, t * part : (t + 1) * part], mine)
    residual_out[...] = mine
    expert_in = normed_rows(residual, gain[...].reshape(1, -1))
    lane = lax.broadcasted_iota(jnp.int32, table.shape, 1)
    slot = lax.broadcasted_iota(jnp.int32, table.shape, 0)
    n_experts = lax.axis_size("rep") * lax.axis_size("req")
    moved = (lane == 2 * n_experts) & (slot == moved_slot[0])
    marked = jnp.where(moved, 1.0, table[...].astype(f32)).astype(bf16)
    for q in range(payload.shape[0]):
        payload[q, :, :width] = expert_in
        payload[q, :, width:] = marked


def stacked_kernel(*refs):
    blocks, whole, tail = refs[:-2], refs[-2], refs[-1]
    rows = blocks[0].shape[0]
    for k, block in enumerate(blocks):
        whole[k * rows : (k + 1) * rows] = block[...]
        if k:
            tail[(k - 1) * rows : k * rows] = block[...]


def stacked(blocks):
    rows, width = blocks[0].shape
    return pl.pallas_call(
        stacked_kernel,
        out_shape=(
            pltpu.VMEM((len(blocks) * rows, width), bf16),
            pltpu.VMEM(((len(blocks) - 1) * rows, width), bf16),
        ),
        in_specs=[vmem()] * len(blocks),
        out_specs=(vmem(), vmem()),
        compiler_params=pltpu.CompilerParams(vmem_limit_bytes=8 * MIB),
        name="stacked",
    )(*near(*blocks))


def joined_kernel(first, second, out):
    rows = first.shape[0]
    out[:rows] = first[...]
    out[rows:] = second[...]


def joined(first, second):
    return pl.pallas_call(
        joined_kernel,
        out_shape=pltpu.VMEM((first.shape[0] + second.shape[0], first.shape[1]), bf16),
        in_specs=[vmem()] * 2,
        out_specs=vmem(),
        compiler_params=pltpu.CompilerParams(vmem_limit_bytes=8 * MIB),
        name="joined",
    )(*near(first, second))


def expert_input(n_tp, n_req, moved, tokens, keep, other, gain, table):
    rows, width = tokens.shape
    return pl.pallas_call(
        lambda *refs: expert_input_kernel(n_tp, *refs),
        out_shape=(
            pltpu.VMEM((n_req, rows, width + table.shape[1]), bf16),
            pltpu.VMEM((rows, width // n_tp), f32),
        ),
        in_specs=[smem()] + [vmem()] * 5,
        out_specs=(vmem(), vmem()),
        compiler_params=pltpu.CompilerParams(vmem_limit_bytes=8 * MIB),
        name="expert_input",
    )(moved, *near(tokens, keep, other), gain, *near(table))


def expert_rows(rows, gate_up, down):
    projected = jnp.dot(rows, gate_up, preferred_element_type=f32)
    hidden = projected.shape[1] // 2
    gate, up = projected[:, :hidden], projected[:, hidden:]
    active = (gate / (1.0 + jnp.exp(-gate)) * up).astype(bf16)
    return jnp.dot(active, down, preferred_element_type=f32)


def expert_cost(count, gate_up, down):
    return pl.CostEstimate(
        flops=2 * count * (gate_up.size + down.size),
        bytes_accessed=2 * (gate_up.size + down.size) + 10 * count * down.shape[1],
        transcendentals=count * down.shape[0],
    )


def traded(width, x_own, x_other, from_own, from_other, keep, send):
    n_req = lax.axis_size("req")
    n_experts = lax.axis_size("rep") * n_req
    expert = lax.axis_index("rep") * n_req + lax.axis_index("req")
    own_table = x_own[:, width:].astype(f32)
    other_table = x_other[:, width:].astype(f32)
    lane = lax.broadcasted_iota(jnp.int32, own_table.shape, 1)

    def picked(table, mask):
        return jnp.sum(jnp.where(mask, table, 0.0), axis=-1, keepdims=True)

    gated = (lane == expert) | (lane == expert + n_experts)
    own_gate, other_gate = picked(own_table, gated), picked(other_table, gated)
    moved = picked(own_table, lane == 2 * n_experts) > 0.5
    from_own = from_own(jnp.where(moved, other_gate, own_gate))
    from_other = from_other() * jnp.where(moved, own_gate, other_gate)
    keep[...] = jnp.where(moved, from_other, from_own)
    send[...] = jnp.where(moved, from_own, from_other).astype(bf16)


def home_expert_kernel(n_tp, place, n_more, x_own, x_other, residual, gate_up, down, *refs):
    more, (keep, send), rest = refs[:n_more], refs[n_more : n_more + 2], refs[n_more + 2 :]
    mine = rest[-1]
    width = down.shape[1]
    count = x_own.shape[0]
    rows_of = [x_own[:, :width], x_other[:, :width]] + [x[:, :width] for x in more]
    y = expert_rows(jnp.concatenate(rows_of, axis=0), gate_up[...], down[...])
    for i, out in enumerate(rest[:-1]):
        out[...] = y[(2 + i) * count : (3 + i) * count]
    rows, part = residual.shape
    tp = lax.axis_index("tp")
    here = pl.ds(place() * rows, rows)

    def from_own(gate):
        mine[...] = y[:count] * gate
        for t in range(n_tp):

            @pl.when(tp == t)
            def _():
                mine[here, t * part : (t + 1) * part] += residual[...]

        return mine[...]

    traded(width, x_own, x_other, from_own, lambda: y[count : 2 * count], keep, send)


def home_expert(n_tp, place, x_own, x_other, residual, gate_up, down, *more):
    shape = (x_own.shape[0], down.shape[1])
    return pl.pallas_call(
        lambda *refs: home_expert_kernel(n_tp, place, len(more), *refs),
        out_shape=(pltpu.VMEM(shape, f32), pltpu.VMEM(shape, bf16)) + (pltpu.VMEM(shape, f32),) * len(more),
        in_specs=[vmem()] * (5 + len(more)),
        out_specs=(vmem(),) * (2 + len(more)),
        scratch_shapes=[pltpu.VMEM(shape, f32)],
        compiler_params=pltpu.CompilerParams(vmem_limit_bytes=40 * MIB if shape[0] > 256 else 16 * MIB),
        cost_estimate=expert_cost(2 * shape[0], gate_up, down),
        name="home_expert",
    )(*near(x_own, x_other, residual), gate_up, down, *near(*more))


def other_expert_kernel(x_own, x_other, y_own, gate_up, down, keep, send):
    width = down.shape[1]

    def from_other():
        return expert_rows(x_other[:, :width], gate_up[...], down[...])

    traded(width, x_own, x_other, lambda gate: y_own[...] * gate, from_other, keep, send)


def other_expert(x_own, x_other, y_own, gate_up, down):
    return pl.pallas_call(
        other_expert_kernel,
        out_shape=(pltpu.VMEM(y_own.shape, f32), pltpu.VMEM(y_own.shape, bf16)),
        in_specs=[vmem()] * 5,
        out_specs=(vmem(), vmem()),
        compiler_params=pltpu.CompilerParams(vmem_limit_bytes=16 * MIB),
        cost_estimate=expert_cost(y_own.shape[0], gate_up, down),
        name="other_expert",
    )(*near(x_own, x_other, y_own), gate_up, down)


def pair_sum_kernel(n_tp, spots, *refs):
    out = refs[-1]
    _, _, rows, part = out.shape
    for i, spot in enumerate(spots):
        keep, recv = refs[2 * i], refs[2 * i + 1]
        total = (keep[...] + recv[...].astype(f32)).astype(bf16)
        for q in range(total.shape[0] // rows):
            for t in range(n_tp):
                out[spot(q), t] = total[q * rows : (q + 1) * rows, t * part : (t + 1) * part]


def pair_sum(n_tp, n_req, rows, spots, *sums):
    part = sums[0].shape[1] // n_tp
    return pl.pallas_call(
        lambda *refs: pair_sum_kernel(n_tp, spots, *refs),
        out_shape=pltpu.VMEM((n_req, n_tp, rows, part), bf16),
        in_specs=[vmem()] * len(sums),
        out_specs=vmem(),
        compiler_params=pltpu.CompilerParams(vmem_limit_bytes=16 * MIB),
        name="pair_sum",
    )(*near(*sums))


def halves_kernel(keep, recv, mine, cross):
    total = keep[...] + recv[...].astype(f32)
    part = mine.shape[1]
    low, high = total[:, :part], total[:, part:]
    first = lax.axis_index("tp") == 0
    mine[...] = jnp.where(first, low, high).astype(mine.dtype)
    cross[...] = jnp.where(first, high, low).astype(bf16)


def halves(keep, recv, kind):
    shape = (keep.shape[0], keep.shape[1] // 2)
    return pl.pallas_call(
        halves_kernel,
        out_shape=(pltpu.VMEM(shape, kind), pltpu.VMEM(shape, bf16)),
        in_specs=[vmem()] * 2,
        out_specs=(vmem(), vmem()),
        compiler_params=pltpu.CompilerParams(vmem_limit_bytes=8 * MIB),
        name="halves",
    )(*near(keep, recv))


def square_sum_kernel(mine, *refs):
    arrived, outs = refs[:3], refs[3:]
    total = mine[...]
    for piece in arrived:
        total = total + piece[...].astype(f32)
    rows = outs[0].shape[0]
    for k, out in enumerate(outs):
        out[...] = total[k * rows : (k + 1) * rows].astype(out.dtype)


def square_sum(rows, mine, *arrived):
    shape = (rows, mine.shape[1])
    count = mine.shape[0] // rows
    return pl.pallas_call(
        square_sum_kernel,
        out_shape=(pltpu.VMEM(shape, f32),) + (pltpu.VMEM(shape, bf16),) * (count - 1),
        in_specs=[vmem()] * 4,
        out_specs=(vmem(),) * count,
        compiler_params=pltpu.CompilerParams(vmem_limit_bytes=8 * MIB),
        name="square_sum",
    )(*near(mine, *arrived))


def line_sum_kernel(*refs):
    total = refs[0][...]
    for piece in refs[1:-1]:
        total = total + piece[...].astype(f32)
    refs[-1][...] = total.astype(bf16)


def line_sum(mine, *arrived):
    return pl.pallas_call(
        line_sum_kernel,
        out_shape=jax.ShapeDtypeStruct(mine.shape, bf16),
        in_specs=[vmem()] * (1 + len(arrived)),
        out_specs=vmem(),
        compiler_params=pltpu.CompilerParams(vmem_limit_bytes=8 * MIB),
        name="line_sum",
    )(*near(mine, *arrived))


def final_kernel(pieces, out):
    total = pieces[0].astype(f32)
    for i in range(1, pieces.shape[0]):
        total = total + pieces[i].astype(f32)
    out[...] = total.astype(bf16)


def final(pieces):
    return pl.pallas_call(
        final_kernel,
        out_shape=jax.ShapeDtypeStruct(pieces.shape[1:], bf16),
        in_specs=[vmem()],
        out_specs=vmem(),
        compiler_params=pltpu.CompilerParams(vmem_limit_bytes=8 * MIB),
        name="final",
    )(*near(pieces))


def shards(
    hidden,
    lengths,
    migrate,
    kv_cache,
    attn_gain,
    moe_gain,
    w_query,
    key_value_weight,
    output_weight,
    w_gateup,
    w_down,
    expert_ids,
    expert_gates,
):
    rows = hidden.shape[0]
    n_rep, n_req, n_tp = lax.axis_size("rep"), lax.axis_size("req"), lax.axis_size("tp")
    extra = -(-(2 * n_rep * n_req + 1) // LANES) * LANES

    if n_tp == 2:
        other_part = swapped(hidden, "tp")
    else:
        all_parts = lax.all_gather(hidden, "tp", axis=1, tiled=True)
    kv = kv_cache.reshape(rows, -1, LANES)
    own, gain, cosine, sine, table, kv_near, *plan = fetch(
        extra,
        lengths,
        expert_ids,
        expert_gates,
        attn_gain,
        hidden,
        w_query,
        key_value_weight,
        kv,
    )
    parts = [own, other_part] if n_tp == 2 else [all_parts]
    tokens, keep, send, _ = attention(
        plan, parts, cosine, sine, gain, w_query, key_value_weight, kv_near, output_weight, kv
    )
    gate_up = w_gateup[0].reshape(w_gateup.shape[1], -1)
    down = w_down[0]
    if n_tp == 2:
        other = swapped(send, "tp")
        gate_up, other = lax.optimization_barrier((gate_up, other))
    else:
        other = lax.psum(keep.astype(bf16), "tp").astype(f32) - keep
    by_permute = n_req == 8 and n_tp == 2
    payload, residual = expert_input(n_tp, 1 if by_permute else n_req, migrate, tokens, keep, other, moe_gain, table)
    if by_permute:
        payload = payload[0]
        steps = [[(q, q ^ 2 * k) for q in range(n_req)] for k in (1, 2, 3)]
        beside = [lax.ppermute(payload, "req", step) for step in steps]
        across = swapped(payload, "req")
        home, tail = stacked([payload] + beside)
        away = joined(across, swapped(tail, "req"))
        home_other = swapped(home, "rep")
        home_keep, home_send, away_own = home_expert(
            n_tp, lambda: 0, home, home_other, residual, gate_up, down, away
        )
        home_recv = swapped(home_send, "rep")
        away_other = swapped(away, "rep")
        away_keep, away_send = other_expert(away, away_other, away_own, gate_up, down)
        away_recv = swapped(away_send, "rep")
        home_mine, home_cross = halves(home_keep, home_recv, f32)
        from_x = swapped(home_cross, "tp")
        away_mine, away_cross = halves(away_keep, away_recv, bf16)
        from_y = swapped(away_mine, "req")
        corner = [(i, i ^ 3) for i in range(n_req * n_tp)]
        from_corner = lax.ppermute(away_cross, ("req", "tp"), corner)
        mine, *others = square_sum(rows, home_mine, from_x, from_y, from_corner)
        line = [lax.ppermute(other, "req", step) for other, step in zip(others, steps)]
        return line_sum(mine, *line)
    x_own = lax.all_to_all(payload, "req", split_axis=0, concat_axis=0, tiled=True)
    x_own = x_own.reshape(n_req * rows, -1)
    x_other = swapped(x_own, "rep")
    mix_keep, mix_send = home_expert(
        n_tp, lambda: lax.axis_index("req"), x_own, x_other, residual, gate_up, down
    )
    mix_recv = swapped(mix_send, "rep")
    pieces = pair_sum(n_tp, n_req, rows, (lambda q: q,), mix_keep, mix_recv)
    pieces = pieces.reshape(n_req * n_tp, rows, -1)
    pieces = lax.all_to_all(pieces, ("req", "tp"), split_axis=0, concat_axis=0, tiled=True)
    return final(pieces)


def solution(mesh):
    placed = (
        P(("rep", "req"), "tp"),
        P(None, "req"),
        P("req"),
        P(("rep", "req"), None, "tp", None),
        P(),
        P(),
        P(None, "tp"),
        P(None, "tp"),
        P("tp", None),
        P(("rep", "req"), None, None, "tp"),
        P(("rep", "req"), "tp", None),
        P(("rep", "req"), None),
        P(("rep", "req"), None),
    )
    return jax.shard_map(
        shards, mesh=mesh, in_specs=placed, out_specs=P(("rep", "req"), "tp"), check_vma=False
    )
```

```python
import jax
import jax.numpy as jnp
from jax import lax
from jax.experimental import pallas as pl
from jax.experimental.pallas import tpu as pltpu
from jax.sharding import PartitionSpec as P

HEAD = 64
EPS = 1e-06
ROPE_BASE = 10000.0
MASKED = -1e30
LANES = 128
QROWS = 16
SPAN = 128
UNROLL = 16
EARLY = 17
PIECES = 4
MIB = 1 << 20

bf16 = jnp.bfloat16
f32 = jnp.float32


def vmem():
    return pl.BlockSpec(memory_space=pltpu.VMEM)


def smem():
    return pl.BlockSpec(memory_space=pltpu.SMEM)


def hbm():
    return pl.BlockSpec(memory_space=pl.ANY)


def swapped(value, axis):
    return lax.ppermute(value, axis, [(i, i ^ 1) for i in range(lax.axis_size(axis))])


def normed_rows(rows, gain):
    mean_square = jnp.mean(rows * rows, axis=-1, keepdims=True)
    return (rows * lax.rsqrt(mean_square + EPS) * gain).astype(bf16)


def rest_copy(kv_hbm, kvbuf, sem, spans, wide, r):
    count = (spans[r] + SPAN - 1) // SPAN - 1
    rest = pl.ds(wide, pl.multiple_of(count * wide, wide))
    return count > 0, pltpu.make_async_copy(kv_hbm.at[r, rest], kvbuf.at[r, rest], sem.at[r])


def fetch_kernel(wide, per, *refs):
    (lens_hbm, ids_hbm, gates_hbm, gain_hbm, own_hbm, kv_hbm) = refs[:6]
    (own, gain, cos_out, sin_out, table_out, kvbuf, spans, items, count) = refs[6:15]
    lens, ids_t, gates_t, sems, ksem, rsem = refs[15:]
    rows = own.shape[0]
    rep = lax.axis_index("rep")

    pairs = (
        (lens_hbm, lens),
        (ids_hbm, ids_t),
        (gates_hbm, gates_t),
        (own_hbm, own),
        (gain_hbm, gain),
    )
    first = pl.ds(0, wide)
    copies = [pltpu.make_async_copy(src, dst, sems.at[i]) for i, (src, dst) in enumerate(pairs)]
    for copy in copies:
        copy.start()
    head_copies = [pltpu.make_async_copy(kv_hbm.at[r, first], kvbuf.at[r, first], ksem.at[r]) for r in range(rows)]
    for copy in head_copies:
        copy.start()

    lane = lax.broadcasted_iota(jnp.int32, (rows, LANES), 1)
    slot = lax.broadcasted_iota(jnp.int32, (rows, LANES), 0)
    half = HEAD // 2
    freq = jnp.zeros((1, LANES), f32)
    for i in range(half):
        freq = jnp.where(lane[:1] % half == i, ROPE_BASE ** (-2.0 * i / HEAD), freq)

    copies[0].wait()
    for r in range(rows):
        spans[r] = lens[rep, r]

        items[r] = r * per

    def plan_row(r, carry):
        n, early = carry
        some, copy = rest_copy(kv_hbm, kvbuf, rsem, spans, wide, r)
        soon = n < EARLY
        pl.when(some & soon)(copy.start)

        def plan_chunk(c, n):
            items[n] = r * per + c
            return n + 1

        later = lax.fori_loop(1, (spans[r] + SPAN - 1) // SPAN, plan_chunk, n)
        return later, jnp.where(soon, r + 1, early)

    total, early = lax.fori_loop(0, rows, plan_row, (rows, 0))
    for u in range(UNROLL):
        items[total + u] = rows * per
    count[0] = total
    count[1] = early

    copies[1].wait()
    copies[2].wait()
    span = jnp.zeros((rows, LANES), jnp.int32)
    for r in range(rows):
        span = jnp.where(slot == r, lens[rep, r], span)
    angle = span.astype(f32) * freq
    sine = jnp.sin(angle)
    cos_out[...] = jnp.cos(angle)
    sin_out[...] = jnp.where(lane % HEAD < half, -sine, sine)

    n_experts = lax.axis_size("rep") * lax.axis_size("req")
    extra = table_out.shape[1]
    lane = lax.broadcasted_iota(jnp.int32, (rows, extra), 1)
    ids, gates = jnp.transpose(ids_t[...]), jnp.transpose(gates_t[...])
    table = jnp.zeros((rows, extra), f32)
    for k in range(ids.shape[1]):
        chosen, weight = ids[:, k : k + 1], gates[:, k : k + 1]
        top = weight.astype(bf16).astype(f32)
        table = jnp.where(lane == chosen, top, table)
        table = jnp.where(lane == chosen + n_experts, weight - top, table)
    table_out[...] = table.astype(bf16)

    for copy in head_copies:
        copy.wait()

    def arrive(r, carry):
        some, copy = rest_copy(kv_hbm, kvbuf, rsem, spans, wide, r)
        pl.when(some)(copy.wait)
        return carry

    lax.fori_loop(0, early, arrive, 0)
    for copy in copies[3:]:
        copy.wait()


def far(*arrays):
    return [pltpu.with_memory_space_constraint(x, pltpu.HBM) for x in arrays]


def close(*arrays):
    return [pltpu.with_memory_space_constraint(x, pltpu.SMEM) for x in arrays]


def near(*arrays):
    return [pltpu.with_memory_space_constraint(x, pltpu.VMEM) for x in arrays]


def fetch(extra, lens, ids, gates, gain, own, wq, wkv, kv):
    rows = own.shape[0]
    wide = SPAN * (wkv.shape[1] // (2 * HEAD))
    per = kv.shape[1] // wide
    outs = [(own.shape, bf16), (gain.shape, f32)]
    outs += [((rows, LANES), f32), ((rows, LANES), f32), ((rows, extra), bf16), (kv.shape, bf16)]
    scalars = [(rows,), (rows * per + UNROLL,), (2,)]
    return pl.pallas_call(
        lambda *refs: fetch_kernel(wide, per, *refs),
        out_shape=tuple(pltpu.VMEM(shape, dtype) for shape, dtype in outs)
        + tuple(pltpu.SMEM(shape, jnp.int32) for shape in scalars),
        in_specs=[hbm()] * 6,
        out_specs=(vmem(),) * len(outs) + (smem(),) * len(scalars),
        scratch_shapes=[
            pltpu.SMEM(lens.shape, jnp.int32),
            pltpu.VMEM(ids.shape[::-1], jnp.int32),
            pltpu.VMEM(gates.shape[::-1], f32),
            pltpu.SemaphoreType.DMA((5,)),
            pltpu.SemaphoreType.DMA((rows,)),
            pltpu.SemaphoreType.DMA((rows,)),
        ],
        compiler_params=pltpu.CompilerParams(vmem_limit_bytes=8 * MIB),
        name="fetch",
    )(*far(lens, ids.T, gates.T, gain, own, kv))


def attention_kernel(n_parts, *refs):
    spans, items, count = refs[:3]
    refs = refs[3:]
    parts = refs[:n_parts]
    (cos_ref, sin_ref, gain_ref, wq, wkv, _, wo_hbm, kv_hbm) = refs[n_parts : 8 + n_parts]
    (tok_out, keep_out, send_out, kvbuf) = refs[8 + n_parts : 12 + n_parts]
    (wo, qf, qb, kvn, mixes, sums, peaks, macc, lacc, oacc, ctx, wsem, ksem) = refs[12 + n_parts :]
    rows = tok_out.shape[0]
    n_query = wq.shape[1] // HEAD
    n_kv = wkv.shape[1] // (2 * HEAD)
    group = n_query // n_kv
    wide = SPAN * n_kv
    per = kv_hbm.shape[1] // wide
    tp = lax.axis_index("tp")

    total, early = count[0], count[1]
    blocks = (total + UNROLL - 1) // UNROLL

    def begin(r, carry):
        some, copy = rest_copy(kv_hbm, kvbuf, ksem, spans, wide, r)
        pl.when(some)(copy.start)
        return carry

    lax.fori_loop(early, rows, begin, 0)
    part = wo.shape[0] // PIECES
    wo_copies = [
        pltpu.make_async_copy(wo_hbm.at[pl.ds(i * part, part)], wo.at[pl.ds(i * part, part)], wsem.at[i])
        for i in range(PIECES)
    ]
    for copy in wo_copies:
        copy.start()

    if n_parts == 2:
        tokens = jnp.concatenate(
            [
                jnp.where(tp == 0, parts[0][...], parts[1][...]),
                jnp.where(tp == 0, parts[1][...], parts[0][...]),
            ],
            axis=1,
        )
    else:
        tokens = parts[0][...]
    tok_out[...] = tokens
    normed = normed_rows(tokens.astype(f32), gain_ref[...].reshape(1, -1))

    lane = lax.broadcasted_iota(jnp.int32, (rows, LANES), 1)
    low_half = lane < HEAD
    first = lane % HEAD < HEAD // 2
    cosine, sine = cos_ref[...], sin_ref[...]

    def rotate(v):
        partner = jnp.where(first, pltpu.roll(v, LANES - HEAD // 2, 1), pltpu.roll(v, HEAD // 2, 1))
        return v * cosine + partner * sine

    qf[...] = jnp.zeros_like(qf)
    kvn[...] = jnp.zeros_like(kvn)
    macc[...] = jnp.full_like(macc, MASKED)
    lacc[...] = jnp.zeros_like(lacc)
    oacc[...] = jnp.zeros_like(oacc)
    queries = jnp.dot(normed, wq[...], preferred_element_type=f32)
    for k in range(n_query // 2):
        turned = rotate(queries[:, k * LANES : (k + 1) * LANES]).astype(bf16).astype(f32)
        turned = turned * HEAD**-0.5
        qf[pl.ds(2 * k, rows, stride=QROWS), :] = jnp.where(low_half, turned, 0.0)
        qf[pl.ds(2 * k + 1, rows, stride=QROWS), :] = jnp.where(low_half, pltpu.roll(turned, HEAD, 1), 0.0)
    keyval = jnp.dot(normed, wkv[...], preferred_element_type=f32)
    for h in range(n_kv):
        v = keyval[:, h * LANES : (h + 1) * LANES]
        new = jnp.where(low_half, rotate(v), v).astype(bf16).astype(f32)
        for g in range(group):
            kvn[pl.ds(h * group + g, rows, stride=QROWS), :] = new
    qb[...] = qf[...].astype(bf16).reshape(qb.shape)

    query_row = lax.broadcasted_iota(jnp.int32, (QROWS, wide), 0)
    row_head = sum((query_row >= h * group).astype(jnp.int32) for h in range(1, n_kv + 1))
    column = lax.broadcasted_iota(jnp.int32, (QROWS, wide), 1)
    reach = jnp.where(column % n_kv == row_head, column // n_kv, 1 << 30)

    def folded(op, value):
        out = value[:, :LANES]
        for j in range(1, wide // LANES):
            out = op(out, value[:, j * LANES : (j + 1) * LANES])
        return out

    def chunk(i):
        item = items[i]
        r = item // per
        c = item % per
        kr = jnp.minimum(r, rows - 1)
        return r, c, kvbuf[kr, pl.ds(pl.multiple_of(c * wide, wide), wide), :]

    def arrive(r, carry):
        some, copy = rest_copy(kv_hbm, kvbuf, ksem, spans, wide, r)
        pl.when(some)(copy.wait)
        return carry

    def merge(base, row_of):
        for u in range(UNROLL):
            r = row_of(u)
            before = macc[r]
            after = jnp.maximum(before, peaks[base + u])
            macc[r] = after
            fade, weight = jnp.exp(before - after), jnp.exp(peaks[base + u] - after)
            lacc[r] = fade * lacc[r] + weight * sums[base + u]
            oacc[r] = fade * oacc[r] + weight * mixes[base + u]

    def block(b, ready):
        last = jnp.minimum(items[b * UNROLL + UNROLL - 1] // per, rows - 1) + 1
        last = jnp.where(b * UNROLL + UNROLL <= rows, 0, last)
        lax.fori_loop(ready, last, arrive, 0)
        earlier = jnp.maximum(b - 1, 0) * UNROLL
        merge(b * UNROLL, lambda u: jnp.where(b == 0, rows, items[earlier + u] // per))
        got = [chunk(b * UNROLL + u) for u in range(UNROLL)]
        dots = [
            lax.dot_general(qb[r], kv, (((1,), (1,)), ((), ())), preferred_element_type=f32) for r, c, kv in got
        ]
        tops, probs = [], []
        for (r, c, kv), s in zip(got, dots):
            span = spans[jnp.minimum(r, rows - 1)]
            limit = jnp.where(r < rows, span - c * SPAN, 0)
            s = jnp.where(reach < limit, s, MASKED)
            top = jnp.max(folded(jnp.maximum, s), axis=-1, keepdims=True)
            tops.append(jnp.broadcast_to(top, (QROWS, LANES)))
            probs.append(jnp.exp(s - top))
        for u, p in enumerate(probs):
            i = (b + 1) * UNROLL + u
            mixes[i] = jnp.dot(p.astype(bf16), got[u][2], preferred_element_type=f32)
            sums[i] = folded(jnp.add, p)
            peaks[i] = tops[u]
        return jnp.maximum(ready, last)

    mixes[:UNROLL] = jnp.zeros((UNROLL, QROWS, LANES), f32)
    sums[:UNROLL] = jnp.zeros((UNROLL, QROWS, LANES), f32)
    peaks[:UNROLL] = jnp.full((UNROLL, QROWS, LANES), MASKED, f32)
    ready = lax.fori_loop(0, blocks, block, early)
    lax.fori_loop(ready, rows, arrive, 0)
    merge(blocks * UNROLL, lambda u: items[(blocks - 1) * UNROLL + u] // per)

    own = jnp.sum(qf[...] * kvn[...], axis=-1, keepdims=True)
    before = macc[...].reshape(qf.shape)
    peak = jnp.maximum(before, own)
    own_p, fade = jnp.exp(own - peak), jnp.exp(before - peak)

    total_p = jnp.sum(fade * lacc[...].reshape(qf.shape), axis=-1, keepdims=True) + own_p
    qf[...] = (fade * oacc[...].reshape(qf.shape) + own_p * kvn[...]) / total_p
    for k in range(n_query // 2):
        a = qf[pl.ds(2 * k, rows, stride=QROWS), :]
        b = qf[pl.ds(2 * k + 1, rows, stride=QROWS), :]
        ctx[:, k * LANES : (k + 1) * LANES] = jnp.where(low_half, pltpu.roll(a, HEAD, 1), b).astype(bf16)
    for copy in wo_copies:
        copy.wait()
    partial = jnp.dot(ctx[...], wo[...], preferred_element_type=f32)
    keep_out[...] = partial
    send_out[...] = partial.astype(bf16)


def attention(plan, parts, cosine, sine, gain, wq, wkv, kv_near, wo, kv):
    rows = parts[0].shape[0]
    width = wq.shape[0]
    n_kv = wkv.shape[1] // (2 * HEAD)
    per = kv.shape[1] // (SPAN * n_kv)
    slots = rows * per + 2 * UNROLL
    many = rows + 1
    return pl.pallas_call(
        lambda *refs: attention_kernel(len(parts), *refs),
        out_shape=(
            pltpu.VMEM((rows, width), bf16),
            pltpu.VMEM((rows, width), f32),
            pltpu.VMEM((rows, width), bf16),
            pltpu.VMEM(kv.shape, bf16),
        ),
        in_specs=[smem()] * 3 + [vmem()] * (len(parts) + 6) + [hbm()] * 2,
        out_specs=(vmem(), vmem(), vmem(), vmem()),
        input_output_aliases={8 + len(parts): 3},
        scratch_shapes=[
            pltpu.VMEM(wo.shape, bf16),
            pltpu.VMEM((many * QROWS, LANES), f32),
            pltpu.VMEM((many, QROWS, LANES), bf16),
            pltpu.VMEM((many * QROWS, LANES), f32),
            pltpu.VMEM((slots, QROWS, LANES), f32),
            pltpu.VMEM((slots, QROWS, LANES), f32),
            pltpu.VMEM((slots, QROWS, LANES), f32),
            pltpu.VMEM((many, QROWS, LANES), f32),
            pltpu.VMEM((many, QROWS, LANES), f32),
            pltpu.VMEM((many, QROWS, LANES), f32),
            pltpu.VMEM((rows, wq.shape[1]), bf16),
            pltpu.SemaphoreType.DMA((PIECES,)),
            pltpu.SemaphoreType.DMA((rows,)),
        ],
        compiler_params=pltpu.CompilerParams(vmem_limit_bytes=16 * MIB),
        name="attention",
    )(*close(*plan), *near(*parts, cosine, sine, gain, wq, wkv, kv_near), *far(wo, kv))


def expert_input_kernel(n_tp, moved_slot, tokens, keep, other, gain, table, payload, residual_out):
    width = tokens.shape[1]
    tp = lax.axis_index("tp")
    residual = tokens[...].astype(f32) + keep[...] + other[...].astype(f32)
    part = width // n_tp
    mine = residual[:, :part]
    for t in range(1, n_tp):
        mine = jnp.where(tp == t, residual[:, t * part : (t + 1) * part], mine)
    residual_out[...] = mine
    expert_in = normed_rows(residual, gain[...].reshape(1, -1))
    lane = lax.broadcasted_iota(jnp.int32, table.shape, 1)
    slot = lax.broadcasted_iota(jnp.int32, table.shape, 0)
    n_experts = lax.axis_size("rep") * lax.axis_size("req")
    moved = (lane == 2 * n_experts) & (slot == moved_slot[0])
    marked = jnp.where(moved, 1.0, table[...].astype(f32)).astype(bf16)
    for q in range(payload.shape[0]):
        payload[q, :, :width] = expert_in
        payload[q, :, width:] = marked


def stacked_kernel(*refs):
    blocks, whole, tail = refs[:-2], refs[-2], refs[-1]
    rows = blocks[0].shape[0]
    for k, block in enumerate(blocks):
        whole[k * rows : (k + 1) * rows] = block[...]
        if k:
            tail[(k - 1) * rows : k * rows] = block[...]


def stacked(blocks):
    rows, width = blocks[0].shape
    return pl.pallas_call(
        stacked_kernel,
        out_shape=(
            pltpu.VMEM((len(blocks) * rows, width), bf16),
            pltpu.VMEM(((len(blocks) - 1) * rows, width), bf16),
        ),
        in_specs=[vmem()] * len(blocks),
        out_specs=(vmem(), vmem()),
        compiler_params=pltpu.CompilerParams(vmem_limit_bytes=8 * MIB),
        name="stacked",
    )(*near(*blocks))


def joined_kernel(first, second, out):
    rows = first.shape[0]
    out[:rows] = first[...]
    out[rows:] = second[...]


def joined(first, second):
    return pl.pallas_call(
        joined_kernel,
        out_shape=pltpu.VMEM((first.shape[0] + second.shape[0], first.shape[1]), bf16),
        in_specs=[vmem()] * 2,
        out_specs=vmem(),
        compiler_params=pltpu.CompilerParams(vmem_limit_bytes=8 * MIB),
        name="joined",
    )(*near(first, second))


def expert_input(n_tp, n_req, moved, tokens, keep, other, gain, table):
    rows, width = tokens.shape
    return pl.pallas_call(
        lambda *refs: expert_input_kernel(n_tp, *refs),
        out_shape=(
            pltpu.VMEM((n_req, rows, width + table.shape[1]), bf16),
            pltpu.VMEM((rows, width // n_tp), f32),
        ),
        in_specs=[smem()] + [vmem()] * 5,
        out_specs=(vmem(), vmem()),
        compiler_params=pltpu.CompilerParams(vmem_limit_bytes=8 * MIB),
        name="expert_input",
    )(moved, *near(tokens, keep, other), gain, *near(table))


def expert_rows(rows, gate_up, down):
    projected = jnp.dot(rows, gate_up, preferred_element_type=f32)
    hidden = projected.shape[1] // 2
    gate, up = projected[:, :hidden], projected[:, hidden:]
    active = (gate / (1.0 + jnp.exp(-gate)) * up).astype(bf16)
    return jnp.dot(active, down, preferred_element_type=f32)


def expert_cost(count, gate_up, down):
    return pl.CostEstimate(
        flops=2 * count * (gate_up.size + down.size),
        bytes_accessed=2 * (gate_up.size + down.size) + 10 * count * down.shape[1],
        transcendentals=count * down.shape[0],
    )


def traded(width, x_own, x_other, from_own, from_other, keep, send):
    n_req = lax.axis_size("req")
    n_experts = lax.axis_size("rep") * n_req
    expert = lax.axis_index("rep") * n_req + lax.axis_index("req")
    own_table = x_own[:, width:].astype(f32)
    other_table = x_other[:, width:].astype(f32)
    lane = lax.broadcasted_iota(jnp.int32, own_table.shape, 1)

    def picked(table, mask):
        return jnp.sum(jnp.where(mask, table, 0.0), axis=-1, keepdims=True)

    gated = (lane == expert) | (lane == expert + n_experts)
    own_gate, other_gate = picked(own_table, gated), picked(other_table, gated)
    moved = picked(own_table, lane == 2 * n_experts) > 0.5
    from_own = from_own(jnp.where(moved, other_gate, own_gate))
    from_other = from_other() * jnp.where(moved, own_gate, other_gate)
    keep[...] = jnp.where(moved, from_other, from_own)
    send[...] = jnp.where(moved, from_own, from_other).astype(bf16)


def home_expert_kernel(n_tp, place, n_more, x_own, x_other, residual, gate_up, down, *refs):
    more, (keep, send), rest = refs[:n_more], refs[n_more : n_more + 2], refs[n_more + 2 :]
    mine = rest[-1]
    width = down.shape[1]
    count = x_own.shape[0]
    rows_of = [x_own[:, :width], x_other[:, :width]] + [x[:, :width] for x in more]
    y = expert_rows(jnp.concatenate(rows_of, axis=0), gate_up[...], down[...])
    for i, out in enumerate(rest[:-1]):
        out[...] = y[(2 + i) * count : (3 + i) * count]
    rows, part = residual.shape
    tp = lax.axis_index("tp")
    here = pl.ds(place() * rows, rows)

    def from_own(gate):
        mine[...] = y[:count] * gate
        for t in range(n_tp):

            @pl.when(tp == t)
            def _():
                mine[here, t * part : (t + 1) * part] += residual[...]

        return mine[...]

    traded(width, x_own, x_other, from_own, lambda: y[count : 2 * count], keep, send)


def home_expert(n_tp, place, x_own, x_other, residual, gate_up, down, *more):
    shape = (x_own.shape[0], down.shape[1])
    return pl.pallas_call(
        lambda *refs: home_expert_kernel(n_tp, place, len(more), *refs),
        out_shape=(pltpu.VMEM(shape, f32), pltpu.VMEM(shape, bf16)) + (pltpu.VMEM(shape, f32),) * len(more),
        in_specs=[vmem()] * (5 + len(more)),
        out_specs=(vmem(),) * (2 + len(more)),
        scratch_shapes=[pltpu.VMEM(shape, f32)],
        compiler_params=pltpu.CompilerParams(vmem_limit_bytes=40 * MIB if shape[0] > 256 else 16 * MIB),
        cost_estimate=expert_cost(2 * shape[0], gate_up, down),
        name="home_expert",
    )(*near(x_own, x_other, residual), gate_up, down, *near(*more))


def other_expert_kernel(x_own, x_other, y_own, gate_up, down, keep, send):
    width = down.shape[1]

    def from_other():
        return expert_rows(x_other[:, :width], gate_up[...], down[...])

    traded(width, x_own, x_other, lambda gate: y_own[...] * gate, from_other, keep, send)


def other_expert(x_own, x_other, y_own, gate_up, down):
    return pl.pallas_call(
        other_expert_kernel,
        out_shape=(pltpu.VMEM(y_own.shape, f32), pltpu.VMEM(y_own.shape, bf16)),
        in_specs=[vmem()] * 5,
        out_specs=(vmem(), vmem()),
        compiler_params=pltpu.CompilerParams(vmem_limit_bytes=16 * MIB),
        cost_estimate=expert_cost(y_own.shape[0], gate_up, down),
        name="other_expert",
    )(*near(x_own, x_other, y_own), gate_up, down)


def pair_sum_kernel(n_tp, spots, *refs):
    out = refs[-1]
    _, _, rows, part = out.shape
    for i, spot in enumerate(spots):
        keep, recv = refs[2 * i], refs[2 * i + 1]
        total = (keep[...] + recv[...].astype(f32)).astype(bf16)
        for q in range(total.shape[0] // rows):
            for t in range(n_tp):
                out[spot(q), t] = total[q * rows : (q + 1) * rows, t * part : (t + 1) * part]


def pair_sum(n_tp, n_req, rows, spots, *sums):
    part = sums[0].shape[1] // n_tp
    return pl.pallas_call(
        lambda *refs: pair_sum_kernel(n_tp, spots, *refs),
        out_shape=pltpu.VMEM((n_req, n_tp, rows, part), bf16),
        in_specs=[vmem()] * len(sums),
        out_specs=vmem(),
        compiler_params=pltpu.CompilerParams(vmem_limit_bytes=16 * MIB),
        name="pair_sum",
    )(*near(*sums))


def halves_kernel(keep, recv, mine, cross):
    total = keep[...] + recv[...].astype(f32)
    part = mine.shape[1]
    low, high = total[:, :part], total[:, part:]
    first = lax.axis_index("tp") == 0
    mine[...] = jnp.where(first, low, high).astype(mine.dtype)
    cross[...] = jnp.where(first, high, low).astype(bf16)


def halves(keep, recv, kind):
    shape = (keep.shape[0], keep.shape[1] // 2)
    return pl.pallas_call(
        halves_kernel,
        out_shape=(pltpu.VMEM(shape, kind), pltpu.VMEM(shape, bf16)),
        in_specs=[vmem()] * 2,
        out_specs=(vmem(), vmem()),
        compiler_params=pltpu.CompilerParams(vmem_limit_bytes=8 * MIB),
        name="halves",
    )(*near(keep, recv))


def square_sum_kernel(mine, *refs):
    arrived, outs = refs[:3], refs[3:]
    total = mine[...]
    for piece in arrived:
        total = total + piece[...].astype(f32)
    rows = outs[0].shape[0]
    for k, out in enumerate(outs):
        out[...] = total[k * rows : (k + 1) * rows].astype(out.dtype)


def square_sum(rows, mine, *arrived):
    shape = (rows, mine.shape[1])
    count = mine.shape[0] // rows
    return pl.pallas_call(
        square_sum_kernel,
        out_shape=(pltpu.VMEM(shape, f32),) + (pltpu.VMEM(shape, bf16),) * (count - 1),
        in_specs=[vmem()] * 4,
        out_specs=(vmem(),) * count,
        compiler_params=pltpu.CompilerParams(vmem_limit_bytes=8 * MIB),
        name="square_sum",
    )(*near(mine, *arrived))


def line_sum_kernel(*refs):
    total = refs[0][...]
    for piece in refs[1:-1]:
        total = total + piece[...].astype(f32)
    refs[-1][...] = total.astype(bf16)


def line_sum(mine, *arrived):
    return pl.pallas_call(
        line_sum_kernel,
        out_shape=jax.ShapeDtypeStruct(mine.shape, bf16),
        in_specs=[vmem()] * (1 + len(arrived)),
        out_specs=vmem(),
        compiler_params=pltpu.CompilerParams(vmem_limit_bytes=8 * MIB),
        name="line_sum",
    )(*near(mine, *arrived))


def final_kernel(pieces, out):
    total = pieces[0].astype(f32)
    for i in range(1, pieces.shape[0]):
        total = total + pieces[i].astype(f32)
    out[...] = total.astype(bf16)


def final(pieces):
    return pl.pallas_call(
        final_kernel,
        out_shape=jax.ShapeDtypeStruct(pieces.shape[1:], bf16),
        in_specs=[vmem()],
        out_specs=vmem(),
        compiler_params=pltpu.CompilerParams(vmem_limit_bytes=8 * MIB),
        name="final",
    )(*near(pieces))


def shards(
    hidden,
    lengths,
    migrate,
    kv_cache,
    attn_gain,
    moe_gain,
    w_query,
    key_value_weight,
    output_weight,
    w_gateup,
    w_down,
    expert_ids,
    expert_gates,
):
    rows = hidden.shape[0]
    n_rep, n_req, n_tp = lax.axis_size("rep"), lax.axis_size("req"), lax.axis_size("tp")
    extra = -(-(2 * n_rep * n_req + 1) // LANES) * LANES

    if n_tp == 2:
        other_part = swapped(hidden, "tp")
    else:
        all_parts = lax.all_gather(hidden, "tp", axis=1, tiled=True)
    kv = kv_cache.reshape(rows, -1, LANES)
    own, gain, cosine, sine, table, kv_near, *plan = fetch(
        extra,
        lengths,
        expert_ids,
        expert_gates,
        attn_gain,
        hidden,
        w_query,
        key_value_weight,
        kv,
    )
    parts = [own, other_part] if n_tp == 2 else [all_parts]
    tokens, keep, send, _ = attention(
        plan, parts, cosine, sine, gain, w_query, key_value_weight, kv_near, output_weight, kv
    )
    gate_up = w_gateup[0].reshape(w_gateup.shape[1], -1)
    down = w_down[0]
    if n_tp == 2:
        other = swapped(send, "tp")
        gate_up, other = lax.optimization_barrier((gate_up, other))
    else:
        other = lax.psum(keep.astype(bf16), "tp").astype(f32) - keep
    by_permute = n_req == 8 and n_tp == 2
    payload, residual = expert_input(n_tp, 1 if by_permute else n_req, migrate, tokens, keep, other, moe_gain, table)
    if by_permute:
        payload = payload[0]
        steps = [[(q, q ^ 2 * k) for q in range(n_req)] for k in (3, 2, 1)]
        beside = [lax.ppermute(payload, "req", step) for step in steps]
        across = swapped(payload, "req")
        home, tail = stacked([payload] + beside)
        away = joined(across, swapped(tail, "req"))
        home_other = swapped(home, "rep")
        home_keep, home_send, away_own = home_expert(
            n_tp, lambda: 0, home, home_other, residual, gate_up, down, away
        )
        home_recv = swapped(home_send, "rep")
        away_other = swapped(away, "rep")
        away_keep, away_send = other_expert(away, away_other, away_own, gate_up, down)
        away_recv = swapped(away_send, "rep")
        home_mine, home_cross = halves(home_keep, home_recv, f32)
        from_x = swapped(home_cross, "tp")
        away_mine, away_cross = halves(away_keep, away_recv, bf16)
        from_y = swapped(away_mine, "req")
        corner = [(i, i ^ 3) for i in range(n_req * n_tp)]
        from_corner = lax.ppermute(away_cross, ("req", "tp"), corner)
        mine, *others = square_sum(rows, home_mine, from_x, from_y, from_corner)
        line = [lax.ppermute(other, "req", step) for other, step in zip(others, steps)]
        return line_sum(mine, *line)
    x_own = lax.all_to_all(payload, "req", split_axis=0, concat_axis=0, tiled=True)
    x_own = x_own.reshape(n_req * rows, -1)
    x_other = swapped(x_own, "rep")
    mix_keep, mix_send = home_expert(
        n_tp, lambda: lax.axis_index("req"), x_own, x_other, residual, gate_up, down
    )
    mix_recv = swapped(mix_send, "rep")
    pieces = pair_sum(n_tp, n_req, rows, (lambda q: q,), mix_keep, mix_recv)
    pieces = pieces.reshape(n_req * n_tp, rows, -1)
    pieces = lax.all_to_all(pieces, ("req", "tp"), split_axis=0, concat_axis=0, tiled=True)
    return final(pieces)


def solution(mesh):
    placed = (
        P(("rep", "req"), "tp"),
        P(None, "req"),
        P("req"),
        P(("rep", "req"), None, "tp", None),
        P(),
        P(),
        P(None, "tp"),
        P(None, "tp"),
        P("tp", None),
        P(("rep", "req"), None, None, "tp"),
        P(("rep", "req"), "tp", None),
        P(("rep", "req"), None),
        P(("rep", "req"), None),
    )
    return jax.shard_map(
        shards, mesh=mesh, in_specs=placed, out_specs=P(("rep", "req"), "tp"), check_vma=False
    )
```

```python
import jax
import jax.numpy as jnp
from jax import lax
from jax.experimental import pallas as pl
from jax.experimental.pallas import tpu as pltpu
from jax.sharding import PartitionSpec as P

HEAD = 64
EPS = 1e-06
ROPE_BASE = 10000.0
MASKED = -1e30
LANES = 128
QROWS = 16
SPAN = 128
UNROLL = 16
EARLY = 17
PIECES = 4
MIB = 1 << 20

bf16 = jnp.bfloat16
f32 = jnp.float32


def vmem():
    return pl.BlockSpec(memory_space=pltpu.VMEM)


def smem():
    return pl.BlockSpec(memory_space=pltpu.SMEM)


def hbm():
    return pl.BlockSpec(memory_space=pl.ANY)


def swapped(value, axis):
    return lax.ppermute(value, axis, [(i, i ^ 1) for i in range(lax.axis_size(axis))])


def normed_rows(rows, gain):
    mean_square = jnp.mean(rows * rows, axis=-1, keepdims=True)
    return (rows * lax.rsqrt(mean_square + EPS) * gain).astype(bf16)


def rest_copy(kv_hbm, kvbuf, sem, spans, wide, r):
    count = (spans[r] + SPAN - 1) // SPAN - 1
    rest = pl.ds(wide, pl.multiple_of(count * wide, wide))
    return count > 0, pltpu.make_async_copy(kv_hbm.at[r, rest], kvbuf.at[r, rest], sem.at[r])


def fetch_kernel(wide, per, *refs):
    (lens_hbm, ids_hbm, gates_hbm, gain_hbm, own_hbm, kv_hbm) = refs[:6]
    (own, gain, cos_out, sin_out, table_out, kvbuf, spans, items, count) = refs[6:15]
    lens, ids_t, gates_t, sems, ksem, rsem = refs[15:]
    rows = own.shape[0]
    rep = lax.axis_index("rep")

    pairs = (
        (lens_hbm, lens),
        (ids_hbm, ids_t),
        (gates_hbm, gates_t),
        (own_hbm, own),
        (gain_hbm, gain),
    )
    first = pl.ds(0, wide)
    copies = [pltpu.make_async_copy(src, dst, sems.at[i]) for i, (src, dst) in enumerate(pairs)]
    for copy in copies:
        copy.start()
    head_copies = [pltpu.make_async_copy(kv_hbm.at[r, first], kvbuf.at[r, first], ksem.at[r]) for r in range(rows)]
    for copy in head_copies:
        copy.start()

    lane = lax.broadcasted_iota(jnp.int32, (rows, LANES), 1)
    slot = lax.broadcasted_iota(jnp.int32, (rows, LANES), 0)
    half = HEAD // 2
    freq = jnp.zeros((1, LANES), f32)
    for i in range(half):
        freq = jnp.where(lane[:1] % half == i, ROPE_BASE ** (-2.0 * i / HEAD), freq)

    copies[0].wait()
    for r in range(rows):
        spans[r] = lens[rep, r]

        items[r] = r * per

    def plan_row(r, carry):
        n, early = carry
        some, copy = rest_copy(kv_hbm, kvbuf, rsem, spans, wide, r)
        soon = n < EARLY
        pl.when(some & soon)(copy.start)

        def plan_chunk(c, n):
            items[n] = r * per + c
            return n + 1

        later = lax.fori_loop(1, (spans[r] + SPAN - 1) // SPAN, plan_chunk, n)
        return later, jnp.where(soon, r + 1, early)

    total, early = lax.fori_loop(0, rows, plan_row, (rows, 0))
    for u in range(UNROLL):
        items[total + u] = rows * per
    count[0] = total
    count[1] = early

    copies[1].wait()
    copies[2].wait()
    span = jnp.zeros((rows, LANES), jnp.int32)
    for r in range(rows):
        span = jnp.where(slot == r, lens[rep, r], span)
    angle = span.astype(f32) * freq
    sine = jnp.sin(angle)
    cos_out[...] = jnp.cos(angle)
    sin_out[...] = jnp.where(lane % HEAD < half, -sine, sine)

    n_experts = lax.axis_size("rep") * lax.axis_size("req")
    extra = table_out.shape[1]
    lane = lax.broadcasted_iota(jnp.int32, (rows, extra), 1)
    ids, gates = jnp.transpose(ids_t[...]), jnp.transpose(gates_t[...])
    table = jnp.zeros((rows, extra), f32)
    for k in range(ids.shape[1]):
        chosen, weight = ids[:, k : k + 1], gates[:, k : k + 1]
        top = weight.astype(bf16).astype(f32)
        table = jnp.where(lane == chosen, top, table)
        table = jnp.where(lane == chosen + n_experts, weight - top, table)
    table_out[...] = table.astype(bf16)

    for copy in head_copies:
        copy.wait()

    def arrive(r, carry):
        some, copy = rest_copy(kv_hbm, kvbuf, rsem, spans, wide, r)
        pl.when(some)(copy.wait)
        return carry

    lax.fori_loop(0, early, arrive, 0)
    for copy in copies[3:]:
        copy.wait()


def far(*arrays):
    return [pltpu.with_memory_space_constraint(x, pltpu.HBM) for x in arrays]


def close(*arrays):
    return [pltpu.with_memory_space_constraint(x, pltpu.SMEM) for x in arrays]


def near(*arrays):
    return [pltpu.with_memory_space_constraint(x, pltpu.VMEM) for x in arrays]


def fetch(extra, lens, ids, gates, gain, own, wq, wkv, kv):
    rows = own.shape[0]
    wide = SPAN * (wkv.shape[1] // (2 * HEAD))
    per = kv.shape[1] // wide
    outs = [(own.shape, bf16), (gain.shape, f32)]
    outs += [((rows, LANES), f32), ((rows, LANES), f32), ((rows, extra), bf16), (kv.shape, bf16)]
    scalars = [(rows,), (rows * per + UNROLL,), (2,)]
    return pl.pallas_call(
        lambda *refs: fetch_kernel(wide, per, *refs),
        out_shape=tuple(pltpu.VMEM(shape, dtype) for shape, dtype in outs)
        + tuple(pltpu.SMEM(shape, jnp.int32) for shape in scalars),
        in_specs=[hbm()] * 6,
        out_specs=(vmem(),) * len(outs) + (smem(),) * len(scalars),
        scratch_shapes=[
            pltpu.SMEM(lens.shape, jnp.int32),
            pltpu.VMEM(ids.shape[::-1], jnp.int32),
            pltpu.VMEM(gates.shape[::-1], f32),
            pltpu.SemaphoreType.DMA((5,)),
            pltpu.SemaphoreType.DMA((rows,)),
            pltpu.SemaphoreType.DMA((rows,)),
        ],
        compiler_params=pltpu.CompilerParams(vmem_limit_bytes=8 * MIB),
        name="fetch",
    )(*far(lens, ids.T, gates.T, gain, own, kv))


def attention_kernel(n_parts, *refs):
    spans, items, count = refs[:3]
    refs = refs[3:]
    parts = refs[:n_parts]
    (cos_ref, sin_ref, gain_ref, wq, wkv, _, wo_hbm, kv_hbm) = refs[n_parts : 8 + n_parts]
    (tok_out, keep_out, send_out, kvbuf) = refs[8 + n_parts : 12 + n_parts]
    (wo, qf, qb, kvn, mixes, sums, peaks, macc, lacc, oacc, ctx, wsem, ksem) = refs[12 + n_parts :]
    rows = tok_out.shape[0]
    n_query = wq.shape[1] // HEAD
    n_kv = wkv.shape[1] // (2 * HEAD)
    group = n_query // n_kv
    wide = SPAN * n_kv
    per = kv_hbm.shape[1] // wide
    tp = lax.axis_index("tp")

    total, early = count[0], count[1]
    blocks = (total + UNROLL - 1) // UNROLL

    def begin(r, carry):
        some, copy = rest_copy(kv_hbm, kvbuf, ksem, spans, wide, r)
        pl.when(some)(copy.start)
        return carry

    lax.fori_loop(early, rows, begin, 0)
    part = wo.shape[0] // PIECES
    wo_copies = [
        pltpu.make_async_copy(wo_hbm.at[pl.ds(i * part, part)], wo.at[pl.ds(i * part, part)], wsem.at[i])
        for i in range(PIECES)
    ]
    for copy in wo_copies:
        copy.start()

    if n_parts == 2:
        tokens = jnp.concatenate(
            [
                jnp.where(tp == 0, parts[0][...], parts[1][...]),
                jnp.where(tp == 0, parts[1][...], parts[0][...]),
            ],
            axis=1,
        )
    else:
        tokens = parts[0][...]
    tok_out[...] = tokens
    normed = normed_rows(tokens.astype(f32), gain_ref[...].reshape(1, -1))

    lane = lax.broadcasted_iota(jnp.int32, (rows, LANES), 1)
    low_half = lane < HEAD
    first = lane % HEAD < HEAD // 2
    cosine, sine = cos_ref[...], sin_ref[...]

    def rotate(v):
        partner = jnp.where(first, pltpu.roll(v, LANES - HEAD // 2, 1), pltpu.roll(v, HEAD // 2, 1))
        return v * cosine + partner * sine

    qf[...] = jnp.zeros_like(qf)
    kvn[...] = jnp.zeros_like(kvn)
    macc[...] = jnp.full_like(macc, MASKED)
    lacc[...] = jnp.zeros_like(lacc)
    oacc[...] = jnp.zeros_like(oacc)
    queries = jnp.dot(normed, wq[...], preferred_element_type=f32)
    for k in range(n_query // 2):
        turned = rotate(queries[:, k * LANES : (k + 1) * LANES]).astype(bf16).astype(f32)
        turned = turned * HEAD**-0.5
        qf[pl.ds(2 * k, rows, stride=QROWS), :] = jnp.where(low_half, turned, 0.0)
        qf[pl.ds(2 * k + 1, rows, stride=QROWS), :] = jnp.where(low_half, pltpu.roll(turned, HEAD, 1), 0.0)
    keyval = jnp.dot(normed, wkv[...], preferred_element_type=f32)
    for h in range(n_kv):
        v = keyval[:, h * LANES : (h + 1) * LANES]
        new = jnp.where(low_half, rotate(v), v).astype(bf16).astype(f32)
        for g in range(group):
            kvn[pl.ds(h * group + g, rows, stride=QROWS), :] = new
    qb[...] = qf[...].astype(bf16).reshape(qb.shape)

    query_row = lax.broadcasted_iota(jnp.int32, (QROWS, wide), 0)
    row_head = sum((query_row >= h * group).astype(jnp.int32) for h in range(1, n_kv + 1))
    column = lax.broadcasted_iota(jnp.int32, (QROWS, wide), 1)
    reach = jnp.where(column % n_kv == row_head, column // n_kv, 1 << 30)

    def folded(op, value):
        out = value[:, :LANES]
        for j in range(1, wide // LANES):
            out = op(out, value[:, j * LANES : (j + 1) * LANES])
        return out

    def chunk(i):
        item = items[i]
        r = item // per
        c = item % per
        kr = jnp.minimum(r, rows - 1)
        return r, c, kvbuf[kr, pl.ds(pl.multiple_of(c * wide, wide), wide), :]

    def arrive(r, carry):
        some, copy = rest_copy(kv_hbm, kvbuf, ksem, spans, wide, r)
        pl.when(some)(copy.wait)
        return carry

    def merge(base, row_of):
        for u in range(UNROLL):
            r = row_of(u)
            before = macc[r]
            after = jnp.maximum(before, peaks[base + u])
            macc[r] = after
            fade, weight = jnp.exp(before - after), jnp.exp(peaks[base + u] - after)
            lacc[r] = fade * lacc[r] + weight * sums[base + u]
            oacc[r] = fade * oacc[r] + weight * mixes[base + u]

    def block(b, ready):
        last = jnp.minimum(items[b * UNROLL + UNROLL - 1] // per, rows - 1) + 1
        last = jnp.where(b * UNROLL + UNROLL <= rows, 0, last)
        lax.fori_loop(ready, last, arrive, 0)
        got = [chunk(b * UNROLL + u) for u in range(UNROLL)]
        dots = [
            lax.dot_general(qb[r], kv, (((1,), (1,)), ((), ())), preferred_element_type=f32) for r, c, kv in got
        ]
        tops, probs = [], []
        for (r, c, kv), s in zip(got, dots):
            span = spans[jnp.minimum(r, rows - 1)]
            limit = jnp.where(r < rows, span - c * SPAN, 0)
            s = jnp.where(reach < limit, s, MASKED)
            top = jnp.max(folded(jnp.maximum, s), axis=-1, keepdims=True)
            tops.append(jnp.broadcast_to(top, (QROWS, LANES)))
            probs.append(jnp.exp(s - top))
        earlier = jnp.maximum(b - 1, 0) * UNROLL
        merge(b * UNROLL, lambda u: jnp.where(b == 0, rows, items[earlier + u] // per))
        for u, p in enumerate(probs):
            i = (b + 1) * UNROLL + u
            mixes[i] = jnp.dot(p.astype(bf16), got[u][2], preferred_element_type=f32)
            sums[i] = folded(jnp.add, p)
            peaks[i] = tops[u]
        return jnp.maximum(ready, last)

    mixes[:UNROLL] = jnp.zeros((UNROLL, QROWS, LANES), f32)
    sums[:UNROLL] = jnp.zeros((UNROLL, QROWS, LANES), f32)
    peaks[:UNROLL] = jnp.full((UNROLL, QROWS, LANES), MASKED, f32)
    ready = lax.fori_loop(0, blocks, block, early)
    lax.fori_loop(ready, rows, arrive, 0)
    merge(blocks * UNROLL, lambda u: items[(blocks - 1) * UNROLL + u] // per)

    own = jnp.sum(qf[...] * kvn[...], axis=-1, keepdims=True)
    before = macc[...].reshape(qf.shape)
    peak = jnp.maximum(before, own)
    own_p, fade = jnp.exp(own - peak), jnp.exp(before - peak)

    total_p = jnp.sum(fade * lacc[...].reshape(qf.shape), axis=-1, keepdims=True) + own_p
    qf[...] = (fade * oacc[...].reshape(qf.shape) + own_p * kvn[...]) / total_p
    for k in range(n_query // 2):
        a = qf[pl.ds(2 * k, rows, stride=QROWS), :]
        b = qf[pl.ds(2 * k + 1, rows, stride=QROWS), :]
        ctx[:, k * LANES : (k + 1) * LANES] = jnp.where(low_half, pltpu.roll(a, HEAD, 1), b).astype(bf16)
    for copy in wo_copies:
        copy.wait()
    partial = jnp.dot(ctx[...], wo[...], preferred_element_type=f32)
    keep_out[...] = partial
    send_out[...] = partial.astype(bf16)


def attention(plan, parts, cosine, sine, gain, wq, wkv, kv_near, wo, kv):
    rows = parts[0].shape[0]
    width = wq.shape[0]
    n_kv = wkv.shape[1] // (2 * HEAD)
    per = kv.shape[1] // (SPAN * n_kv)
    slots = rows * per + 2 * UNROLL
    many = rows + 1
    return pl.pallas_call(
        lambda *refs: attention_kernel(len(parts), *refs),
        out_shape=(
            pltpu.VMEM((rows, width), bf16),
            pltpu.VMEM((rows, width), f32),
            pltpu.VMEM((rows, width), bf16),
            pltpu.VMEM(kv.shape, bf16),
        ),
        in_specs=[smem()] * 3 + [vmem()] * (len(parts) + 6) + [hbm()] * 2,
        out_specs=(vmem(), vmem(), vmem(), vmem()),
        input_output_aliases={8 + len(parts): 3},
        scratch_shapes=[
            pltpu.VMEM(wo.shape, bf16),
            pltpu.VMEM((many * QROWS, LANES), f32),
            pltpu.VMEM((many, QROWS, LANES), bf16),
            pltpu.VMEM((many * QROWS, LANES), f32),
            pltpu.VMEM((slots, QROWS, LANES), f32),
            pltpu.VMEM((slots, QROWS, LANES), f32),
            pltpu.VMEM((slots, QROWS, LANES), f32),
            pltpu.VMEM((many, QROWS, LANES), f32),
            pltpu.VMEM((many, QROWS, LANES), f32),
            pltpu.VMEM((many, QROWS, LANES), f32),
            pltpu.VMEM((rows, wq.shape[1]), bf16),
            pltpu.SemaphoreType.DMA((PIECES,)),
            pltpu.SemaphoreType.DMA((rows,)),
        ],
        compiler_params=pltpu.CompilerParams(vmem_limit_bytes=16 * MIB),
        name="attention",
    )(*close(*plan), *near(*parts, cosine, sine, gain, wq, wkv, kv_near), *far(wo, kv))


def expert_input_kernel(n_tp, moved_slot, tokens, keep, other, gain, table, payload, residual_out):
    width = tokens.shape[1]
    tp = lax.axis_index("tp")
    residual = tokens[...].astype(f32) + keep[...] + other[...].astype(f32)
    part = width // n_tp
    mine = residual[:, :part]
    for t in range(1, n_tp):
        mine = jnp.where(tp == t, residual[:, t * part : (t + 1) * part], mine)
    residual_out[...] = mine
    expert_in = normed_rows(residual, gain[...].reshape(1, -1))
    lane = lax.broadcasted_iota(jnp.int32, table.shape, 1)
    slot = lax.broadcasted_iota(jnp.int32, table.shape, 0)
    n_experts = lax.axis_size("rep") * lax.axis_size("req")
    moved = (lane == 2 * n_experts) & (slot == moved_slot[0])
    marked = jnp.where(moved, 1.0, table[...].astype(f32)).astype(bf16)
    for q in range(payload.shape[0]):
        payload[q, :, :width] = expert_in
        payload[q, :, width:] = marked


def stacked_kernel(*refs):
    blocks, whole, tail = refs[:-2], refs[-2], refs[-1]
    rows = blocks[0].shape[0]
    for k, block in enumerate(blocks):
        whole[k * rows : (k + 1) * rows] = block[...]
        if k:
            tail[(k - 1) * rows : k * rows] = block[...]


def stacked(blocks):
    rows, width = blocks[0].shape
    return pl.pallas_call(
        stacked_kernel,
        out_shape=(
            pltpu.VMEM((len(blocks) * rows, width), bf16),
            pltpu.VMEM(((len(blocks) - 1) * rows, width), bf16),
        ),
        in_specs=[vmem()] * len(blocks),
        out_specs=(vmem(), vmem()),
        compiler_params=pltpu.CompilerParams(vmem_limit_bytes=8 * MIB),
        name="stacked",
    )(*near(*blocks))


def joined_kernel(first, second, out):
    rows = first.shape[0]
    out[:rows] = first[...]
    out[rows:] = second[...]


def joined(first, second):
    return pl.pallas_call(
        joined_kernel,
        out_shape=pltpu.VMEM((first.shape[0] + second.shape[0], first.shape[1]), bf16),
        in_specs=[vmem()] * 2,
        out_specs=vmem(),
        compiler_params=pltpu.CompilerParams(vmem_limit_bytes=8 * MIB),
        name="joined",
    )(*near(first, second))


def expert_input(n_tp, n_req, moved, tokens, keep, other, gain, table):
    rows, width = tokens.shape
    return pl.pallas_call(
        lambda *refs: expert_input_kernel(n_tp, *refs),
        out_shape=(
            pltpu.VMEM((n_req, rows, width + table.shape[1]), bf16),
            pltpu.VMEM((rows, width // n_tp), f32),
        ),
        in_specs=[smem()] + [vmem()] * 5,
        out_specs=(vmem(), vmem()),
        compiler_params=pltpu.CompilerParams(vmem_limit_bytes=8 * MIB),
        name="expert_input",
    )(moved, *near(tokens, keep, other), gain, *near(table))


def expert_rows(rows, gate_up, down):
    projected = jnp.dot(rows, gate_up, preferred_element_type=f32)
    hidden = projected.shape[1] // 2
    gate, up = projected[:, :hidden], projected[:, hidden:]
    active = (gate / (1.0 + jnp.exp(-gate)) * up).astype(bf16)
    return jnp.dot(active, down, preferred_element_type=f32)


def expert_cost(count, gate_up, down):
    return pl.CostEstimate(
        flops=2 * count * (gate_up.size + down.size),
        bytes_accessed=2 * (gate_up.size + down.size) + 10 * count * down.shape[1],
        transcendentals=count * down.shape[0],
    )


def traded(width, x_own, x_other, from_own, from_other, keep, send):
    n_req = lax.axis_size("req")
    n_experts = lax.axis_size("rep") * n_req
    expert = lax.axis_index("rep") * n_req + lax.axis_index("req")
    own_table = x_own[:, width:].astype(f32)
    other_table = x_other[:, width:].astype(f32)
    lane = lax.broadcasted_iota(jnp.int32, own_table.shape, 1)

    def picked(table, mask):
        return jnp.sum(jnp.where(mask, table, 0.0), axis=-1, keepdims=True)

    gated = (lane == expert) | (lane == expert + n_experts)
    own_gate, other_gate = picked(own_table, gated), picked(other_table, gated)
    moved = picked(own_table, lane == 2 * n_experts) > 0.5
    from_own = from_own(jnp.where(moved, other_gate, own_gate))
    from_other = from_other() * jnp.where(moved, own_gate, other_gate)
    keep[...] = jnp.where(moved, from_other, from_own)
    send[...] = jnp.where(moved, from_own, from_other).astype(bf16)


def home_expert_kernel(n_tp, place, n_more, x_own, x_other, residual, gate_up, down, *refs):
    more, (keep, send), rest = refs[:n_more], refs[n_more : n_more + 2], refs[n_more + 2 :]
    mine = rest[-1]
    width = down.shape[1]
    count = x_own.shape[0]
    rows_of = [x_own[:, :width], x_other[:, :width]] + [x[:, :width] for x in more]
    y = expert_rows(jnp.concatenate(rows_of, axis=0), gate_up[...], down[...])
    for i, out in enumerate(rest[:-1]):
        out[...] = y[(2 + i) * count : (3 + i) * count]
    rows, part = residual.shape
    tp = lax.axis_index("tp")
    here = pl.ds(place() * rows, rows)

    def from_own(gate):
        mine[...] = y[:count] * gate
        for t in range(n_tp):

            @pl.when(tp == t)
            def _():
                mine[here, t * part : (t + 1) * part] += residual[...]

        return mine[...]

    traded(width, x_own, x_other, from_own, lambda: y[count : 2 * count], keep, send)


def home_expert(n_tp, place, x_own, x_other, residual, gate_up, down, *more):
    shape = (x_own.shape[0], down.shape[1])
    return pl.pallas_call(
        lambda *refs: home_expert_kernel(n_tp, place, len(more), *refs),
        out_shape=(pltpu.VMEM(shape, f32), pltpu.VMEM(shape, bf16)) + (pltpu.VMEM(shape, f32),) * len(more),
        in_specs=[vmem()] * (5 + len(more)),
        out_specs=(vmem(),) * (2 + len(more)),
        scratch_shapes=[pltpu.VMEM(shape, f32)],
        compiler_params=pltpu.CompilerParams(vmem_limit_bytes=40 * MIB if shape[0] > 256 else 16 * MIB),
        cost_estimate=expert_cost(2 * shape[0], gate_up, down),
        name="home_expert",
    )(*near(x_own, x_other, residual), gate_up, down, *near(*more))


def other_expert_kernel(x_own, x_other, y_own, gate_up, down, keep, send):
    width = down.shape[1]

    def from_other():
        return expert_rows(x_other[:, :width], gate_up[...], down[...])

    traded(width, x_own, x_other, lambda gate: y_own[...] * gate, from_other, keep, send)


def other_expert(x_own, x_other, y_own, gate_up, down):
    return pl.pallas_call(
        other_expert_kernel,
        out_shape=(pltpu.VMEM(y_own.shape, f32), pltpu.VMEM(y_own.shape, bf16)),
        in_specs=[vmem()] * 5,
        out_specs=(vmem(), vmem()),
        compiler_params=pltpu.CompilerParams(vmem_limit_bytes=16 * MIB),
        cost_estimate=expert_cost(y_own.shape[0], gate_up, down),
        name="other_expert",
    )(*near(x_own, x_other, y_own), gate_up, down)


def pair_sum_kernel(n_tp, spots, *refs):
    out = refs[-1]
    _, _, rows, part = out.shape
    for i, spot in enumerate(spots):
        keep, recv = refs[2 * i], refs[2 * i + 1]
        total = (keep[...] + recv[...].astype(f32)).astype(bf16)
        for q in range(total.shape[0] // rows):
            for t in range(n_tp):
                out[spot(q), t] = total[q * rows : (q + 1) * rows, t * part : (t + 1) * part]


def pair_sum(n_tp, n_req, rows, spots, *sums):
    part = sums[0].shape[1] // n_tp
    return pl.pallas_call(
        lambda *refs: pair_sum_kernel(n_tp, spots, *refs),
        out_shape=pltpu.VMEM((n_req, n_tp, rows, part), bf16),
        in_specs=[vmem()] * len(sums),
        out_specs=vmem(),
        compiler_params=pltpu.CompilerParams(vmem_limit_bytes=16 * MIB),
        name="pair_sum",
    )(*near(*sums))


def halves_kernel(keep, recv, mine, cross):
    total = keep[...] + recv[...].astype(f32)
    part = mine.shape[1]
    low, high = total[:, :part], total[:, part:]
    first = lax.axis_index("tp") == 0
    mine[...] = jnp.where(first, low, high).astype(mine.dtype)
    cross[...] = jnp.where(first, high, low).astype(bf16)


def halves(keep, recv, kind):
    shape = (keep.shape[0], keep.shape[1] // 2)
    return pl.pallas_call(
        halves_kernel,
        out_shape=(pltpu.VMEM(shape, kind), pltpu.VMEM(shape, bf16)),
        in_specs=[vmem()] * 2,
        out_specs=(vmem(), vmem()),
        compiler_params=pltpu.CompilerParams(vmem_limit_bytes=8 * MIB),
        name="halves",
    )(*near(keep, recv))


def square_sum_kernel(mine, *refs):
    arrived, outs = refs[:3], refs[3:]
    total = mine[...]
    for piece in arrived:
        total = total + piece[...].astype(f32)
    rows = outs[0].shape[0]
    for k, out in enumerate(outs):
        out[...] = total[k * rows : (k + 1) * rows].astype(out.dtype)


def square_sum(rows, mine, *arrived):
    shape = (rows, mine.shape[1])
    count = mine.shape[0] // rows
    return pl.pallas_call(
        square_sum_kernel,
        out_shape=(pltpu.VMEM(shape, f32),) + (pltpu.VMEM(shape, bf16),) * (count - 1),
        in_specs=[vmem()] * 4,
        out_specs=(vmem(),) * count,
        compiler_params=pltpu.CompilerParams(vmem_limit_bytes=8 * MIB),
        name="square_sum",
    )(*near(mine, *arrived))


def line_sum_kernel(*refs):
    total = refs[0][...]
    for piece in refs[1:-1]:
        total = total + piece[...].astype(f32)
    refs[-1][...] = total.astype(bf16)


def line_sum(mine, *arrived):
    return pl.pallas_call(
        line_sum_kernel,
        out_shape=jax.ShapeDtypeStruct(mine.shape, bf16),
        in_specs=[vmem()] * (1 + len(arrived)),
        out_specs=vmem(),
        compiler_params=pltpu.CompilerParams(vmem_limit_bytes=8 * MIB),
        name="line_sum",
    )(*near(mine, *arrived))


def final_kernel(pieces, out):
    total = pieces[0].astype(f32)
    for i in range(1, pieces.shape[0]):
        total = total + pieces[i].astype(f32)
    out[...] = total.astype(bf16)


def final(pieces):
    return pl.pallas_call(
        final_kernel,
        out_shape=jax.ShapeDtypeStruct(pieces.shape[1:], bf16),
        in_specs=[vmem()],
        out_specs=vmem(),
        compiler_params=pltpu.CompilerParams(vmem_limit_bytes=8 * MIB),
        name="final",
    )(*near(pieces))


def shards(
    hidden,
    lengths,
    migrate,
    kv_cache,
    attn_gain,
    moe_gain,
    w_query,
    key_value_weight,
    output_weight,
    w_gateup,
    w_down,
    expert_ids,
    expert_gates,
):
    rows = hidden.shape[0]
    n_rep, n_req, n_tp = lax.axis_size("rep"), lax.axis_size("req"), lax.axis_size("tp")
    extra = -(-(2 * n_rep * n_req + 1) // LANES) * LANES

    if n_tp == 2:
        other_part = swapped(hidden, "tp")
    else:
        all_parts = lax.all_gather(hidden, "tp", axis=1, tiled=True)
    kv = kv_cache.reshape(rows, -1, LANES)
    own, gain, cosine, sine, table, kv_near, *plan = fetch(
        extra,
        lengths,
        expert_ids,
        expert_gates,
        attn_gain,
        hidden,
        w_query,
        key_value_weight,
        kv,
    )
    parts = [own, other_part] if n_tp == 2 else [all_parts]
    tokens, keep, send, _ = attention(
        plan, parts, cosine, sine, gain, w_query, key_value_weight, kv_near, output_weight, kv
    )
    gate_up = w_gateup[0].reshape(w_gateup.shape[1], -1)
    down = w_down[0]
    if n_tp == 2:
        other = swapped(send, "tp")
        gate_up, other = lax.optimization_barrier((gate_up, other))
    else:
        other = lax.psum(keep.astype(bf16), "tp").astype(f32) - keep
    by_permute = n_req == 8 and n_tp == 2
    payload, residual = expert_input(n_tp, 1 if by_permute else n_req, migrate, tokens, keep, other, moe_gain, table)
    if by_permute:
        payload = payload[0]
        steps = [[(q, q ^ 2 * k) for q in range(n_req)] for k in (3, 2, 1)]
        beside = [lax.ppermute(payload, "req", step) for step in steps]
        across = swapped(payload, "req")
        home, tail = stacked([payload] + beside)
        away = joined(across, swapped(tail, "req"))
        home_other = swapped(home, "rep")
        home_keep, home_send, away_own = home_expert(
            n_tp, lambda: 0, home, home_other, residual, gate_up, down, away
        )
        home_recv = swapped(home_send, "rep")
        away_other = swapped(away, "rep")
        away_keep, away_send = other_expert(away, away_other, away_own, gate_up, down)
        away_recv = swapped(away_send, "rep")
        home_mine, home_cross = halves(home_keep, home_recv, f32)
        from_x = swapped(home_cross, "tp")
        away_mine, away_cross = halves(away_keep, away_recv, bf16)
        from_y = swapped(away_mine, "req")
        corner = [(i, i ^ 3) for i in range(n_req * n_tp)]
        from_corner = lax.ppermute(away_cross, ("req", "tp"), corner)
        mine, *others = square_sum(rows, home_mine, from_x, from_y, from_corner)
        line = [lax.ppermute(other, "req", step) for other, step in zip(others, steps)]
        return line_sum(mine, *line)
    x_own = lax.all_to_all(payload, "req", split_axis=0, concat_axis=0, tiled=True)
    x_own = x_own.reshape(n_req * rows, -1)
    x_other = swapped(x_own, "rep")
    mix_keep, mix_send = home_expert(
        n_tp, lambda: lax.axis_index("req"), x_own, x_other, residual, gate_up, down
    )
    mix_recv = swapped(mix_send, "rep")
    pieces = pair_sum(n_tp, n_req, rows, (lambda q: q,), mix_keep, mix_recv)
    pieces = pieces.reshape(n_req * n_tp, rows, -1)
    pieces = lax.all_to_all(pieces, ("req", "tp"), split_axis=0, concat_axis=0, tiled=True)
    return final(pieces)


def solution(mesh):
    placed = (
        P(("rep", "req"), "tp"),
        P(None, "req"),
        P("req"),
        P(("rep", "req"), None, "tp", None),
        P(),
        P(),
        P(None, "tp"),
        P(None, "tp"),
        P("tp", None),
        P(("rep", "req"), None, None, "tp"),
        P(("rep", "req"), "tp", None),
        P(("rep", "req"), None),
        P(("rep", "req"), None),
    )
    return jax.shard_map(
        shards, mesh=mesh, in_specs=placed, out_specs=P(("rep", "req"), "tp"), check_vma=False
    )
```
